32 devices in a mesh: cell: 4 (over x, core), spot: 2 (over y), gene: 4 (over z).
Axes of the slice: x: 2, y: 2, z: 4, core: 2. Of those that a mesh axis runs over, the one named last changes fastest.
Arguments:
- logits: bfloat16 [45056, 1024], P(('cell', 'gene'), 'spot'), may hold values from -8 to 8
- expression: bfloat16 [45056, 2048], P(('cell', 'spot'), 'gene'), may hold values from 5e-05 to 12, as said below
- spatial: bfloat16 [1024, 2048], P('spot', 'gene'), may hold values from 5e-05 to 12, as said below
- slide_ids: int32 [1024], P('spot'), may hold values from 0 to 2, never falling along the last dimension, each value on 1 to 512 neighbouring positions
- spot_mask: int32 [1024], P('spot'), may hold values 0 or 1
- densities: float32 [45056], P(('cell', 'gene')), may hold values from 0.2 to 5
Outputs:
- loss_terms: float32 [5], replicated
- grad_logits: float32 [45056, 1024], P(('cell', 'gene'), 'spot')
The draws below stay inside these ranges and needn't reach their ends.
Inputs may be any that keep to these rules, and one draw needn't show every extreme that they name: `slide_ids`: spots are ordered by slide: the ids never fall, every slide has at least one spot, and the largest slide has exactly 512 spots. Positive expression levels. `spatial`: positive expression levels.
All inputs are finite; a program needn't handle non-finite values. No bound on the sum of `spot_mask` on one device may be relied on, other than what follows from the above.
Results may differ from the reference program's by a relative error of at most 0.0003.
Values may be sent and summed in bfloat16 or wider, within the bound.
No kernel may reach another device: no remote copies, remote signals or barrier semaphores. Data moves between devices by JAX's collectives and lax.ppermute only.
A program may use at most 128 MiB of HBM per device.

```python
import math
import jax
import jax.numpy as jnp
import numpy as np
from jax import lax

GENES = 2048
SLIDES = 3
CELLS = 45056
SPOTS = 1024


def gene_scales(key, low_end, high_end):
    key = jax.random.fold_in(key, 11)
    spread = jax.random.uniform(key, (GENES,), jnp.float32)
    return jnp.exp(math.log(low_end) + spread * (math.log(high_end) - math.log(low_end)))


def level_factors(key, row_count, low_end, high_end):
    spread = jax.random.uniform(key, (row_count, GENES), jnp.float32)
    return jnp.exp(math.log(low_end) + spread * (math.log(high_end) - math.log(low_end)))


def draw_expression(key, part):
    scales = gene_scales(key, 0.002, 2.0)
    key = jax.random.fold_in(key, 1)
    factors = level_factors(key, CELLS, 0.05, 4.0)
    return (scales[None, :] * factors).astype(jnp.bfloat16)


def draw_spatial(key, part):
    scales = gene_scales(key, 0.002, 2.0)
    key = jax.random.fold_in(key, 2)
    factors = level_factors(key, SPOTS, 0.05, 4.0)
    return (scales[None, :] * factors).astype(jnp.bfloat16)


def plant(entries, own_key, least, high):
    longest = entries.shape.index(max(entries.shape))
    spots = []
    for shift in (0, 1):
        where = [jax.random.randint(jax.random.fold_in(own_key, axis), (), 0, length) for axis, length in enumerate(entries.shape)]
        where[longest] = (where[longest] + shift) % entries.shape[longest]
        spots.append(tuple(where))
    return entries.at[spots[0]].set(least).at[spots[1]].set(high)


def shard_levels(key, extent, pieces, least, top_value):
    level = 1.0
    for dim, shards_of in pieces:
        steps = jax.random.uniform(jax.random.fold_in(jax.random.fold_in(key, 6), dim), (shards_of,), jnp.float32, least / len(pieces), top_value / len(pieces))
        level = level * jnp.repeat(jnp.exp(steps), extent[dim] // shards_of).reshape((-1,) + (1,) * (len(extent) - 1 - dim))
    return level


def length_profile(amount, total, bound, slope):
    loads = [(1 << 20) // math.isqrt(standing ** slope) + 1 for standing in range(2, amount + 1)]
    rest, given = total - bound - (amount - 1), [1] * (amount - 1)
    while rest > 0:
        movable = [i for i in range(amount - 1) if given[i] < bound]
        pool, remaining = sum([loads[i] for i in movable]), rest
        for i in movable:
            extra = min(bound - given[i], max(1, remaining * loads[i] // pool), rest)
            given[i] = given[i] + extra
            rest = rest - extra
    return np.array([bound] + given)


def uneven_parts(key, count, total, most, skew):
    if count == 2:
        one = jax.random.randint(key, (), max(1, total - most), min(most, total - 1) + 1)
        return jnp.stack([one, total - one])
    lengths = jnp.asarray(length_profile(count, total, most, skew), jnp.int32)
    pairs = (count - 1) // 2
    donor, receiver = lengths[1:1 + 2 * pairs:2], lengths[2:2 + 2 * pairs:2]
    room = jnp.minimum(donor - 1, most - receiver)
    passed = jax.random.randint(jax.random.fold_in(key, 1), (pairs,), 0, 1 << 20) % (room + 1)
    lengths = lengths.at[1:1 + 2 * pairs:2].set(donor - passed).at[2:2 + 2 * pairs:2].set(receiver + passed)
    return lengths[jax.random.permutation(jax.random.fold_in(key, 2), count)]


def normal_values(own_key, dims, width, bound, split=(), kind=jnp.bfloat16):
    array = width * jax.random.normal(own_key, dims, jnp.float32)
    if split:
        array = array * shard_levels(own_key, dims, split, -0.22, 0.18)
    return jnp.clip(array, -bound, bound).astype(kind)


def setup_inputs(seed: int = 0) -> dict:
    keys = jax.random.split(jax.random.key(seed), 7)
    return {
        "logits": normal_values(keys[0], (CELLS, SPOTS), 1.5, 8.0, ((0, 16), (1, 2))),
        "expression": draw_expression(jax.random.fold_in(keys[6], 71), 0),
        "spatial": draw_spatial(jax.random.fold_in(keys[6], 71), 0),
        "slide_ids": jnp.searchsorted(jnp.cumsum(uneven_parts(keys[3], SLIDES, SPOTS, SPOTS // 2, 1)), jnp.arange(SPOTS), side="right").astype(jnp.int32),
        "spot_mask": plant((jax.random.randint(keys[4], (SPOTS,), 0, 4) < 3).astype(jnp.int32), jax.random.fold_in(keys[4], 1), 0, 1),
        "densities": jnp.clip(jnp.exp(math.log(5.0) - 3.218876 * jax.random.uniform(keys[5], (CELLS,), jnp.float32) ** shard_levels(keys[5], (CELLS,), ((0, 16),), -0.2, 0.2)), 0.2, 5.0),
    }


@jax.custom_vjp
def low(v):
    return lax.optimization_barrier(v.astype(jnp.bfloat16)).astype(jnp.float32)

@jax.custom_vjp
def low_back(v):
    return v

def low_keep(v):
    return (low(v), None)

def low_pass(kept, grad):
    return (grad,)

def back_keep(v):
    return (v, None)

def back_low(kept, grad):
    return (low(grad),)
low.defvjp(low_keep, low_pass)
low_back.defvjp(back_keep, back_low)

def reference(logits, expression, spatial, slide_ids, spot_mask, densities):
    highest = lax.Precision.HIGHEST
    logit_vals = logits.astype(jnp.float32)
    expr_vals = expression.astype(jnp.float32)
    target = spatial.astype(jnp.float32)
    valid_spots = spot_mask.astype(jnp.float32)
    member = jnp.where((slide_ids[None, :] == jnp.arange(SLIDES, dtype=jnp.int32)[:, None]) & (spot_mask[None, :] == 1), 1.0, 0.0).astype(jnp.float32)
    valid_total = jnp.maximum(jnp.sum(valid_spots), 1.0)
    target_share = densities / jnp.sum(densities)
    spot_count = logit_vals.shape[1]
    gene_count = target.shape[1]

    def forward(logit_vals):
        col_max = lax.optimization_barrier(jnp.max(logit_vals, axis=0))
        expo_vals = jnp.exp(logit_vals - col_max)
        col_total = lax.optimization_barrier(jnp.sum(expo_vals, axis=0))
        prob_vals = expo_vals / col_total
        predicted = low_back(jnp.dot(low(prob_vals).T, expr_vals, precision=highest))
        numerator = jnp.dot(member, predicted * target, precision=highest)
        pred_sq = jnp.dot(member, predicted * predicted, precision=highest)
        target_sq = jnp.dot(member, target * target, precision=highest)
        cos_gene = numerator / jnp.sqrt(jnp.maximum(pred_sq, 1.0) * jnp.maximum(target_sq, 1.0))
        spot_num = lax.optimization_barrier(jnp.sum(predicted * target, axis=1))
        spot_pred = lax.optimization_barrier(jnp.sum(predicted * predicted, axis=1)) + 1e-06
        spot_target = lax.optimization_barrier(jnp.sum(target * target, axis=1)) + 1e-06
        cos_spot = spot_num / jnp.sqrt(spot_pred * spot_target)
        cell_mass = lax.optimization_barrier(jnp.sum(prob_vals, axis=1)) / spot_count
        divergence = jnp.sum(target_share * (jnp.log(target_share) - jnp.log(cell_mass)))
        log_prob = logit_vals - col_max - jnp.log(col_total)
        entropy = -jnp.sum(prob_vals * log_prob) / spot_count
        gene_term = jnp.sum(cos_gene) / (SLIDES * gene_count)
        spot_term = jnp.sum(valid_spots * cos_spot) / valid_total
        total = -gene_term - spot_term + divergence
        return (total, jnp.stack([total, gene_term, spot_term, divergence, entropy]))
    total, backward, loss_terms = jax.vjp(forward, logit_vals, has_aux=True)
    grad_logits, = backward(jnp.ones((), jnp.float32))
    return (loss_terms, grad_logits)
```

```python
import functools
import jax
import jax.numpy as jnp
from jax import lax
from jax.experimental import pallas as pl
from jax.experimental.pallas import tpu as pltpu
from jax.sharding import PartitionSpec as P

SLIDES = 3
LANES = 128
ANY = pl.BlockSpec(memory_space=pl.ANY)
BF = jnp.bfloat16
F32 = jnp.float32
VMEM_BYTES = 56 * 1024 * 1024
WIDTHS = (256, 128, 128)
ORDER = (
    "Y0 Y1 t0 e0",
    "Z0 L0 e1 Y2",
    "Z1 L1 t1 S0",
    "Z2 L2 e2 t2",
    "S1 e3 F0 m0",
    "P0 S2 Q0 F1",
    "P1 R0 Q1 G0",
    "R1 H0 F2 P2",
    "Q2 T0 R2 G1",
    "H1 T1 G2 H2",
    "T2",
)


def sds(shape, dtype):
    return jax.ShapeDtypeStruct(shape, dtype)


def whole(shape):
    zeros = (0,) * len(shape)
    return pl.BlockSpec(shape, lambda *_: zeros)


def xor_pairs(size, step):
    return [(n, n ^ step) for n in range(size)]


class Chain:
    def __init__(self, flags):
        self.flags = flags
        self.token = jnp.zeros((8, LANES), F32)

    def run(self, name, body, ins=(), outs=(), through=(), grid=(1,), scratch=()):
        n_in, n_out, n_thr = len(ins), len(outs), len(through) + 1

        def kernel(flags, *refs):
            in_refs = refs[:n_in]
            out_refs = refs[n_in + n_thr : n_in + n_thr + n_out]
            scratch_refs = refs[n_in + 2 * n_thr + n_out :]
            if body is not None:
                body(flags, in_refs, out_refs, *scratch_refs)

        carried = (*through, self.token)
        results = pl.pallas_call(
            kernel,
            out_shape=[s for s, _ in outs] + [sds(a.shape, a.dtype) for a in carried],
            grid_spec=pltpu.PrefetchScalarGridSpec(
                num_scalar_prefetch=1,
                grid=grid,
                in_specs=[s for _, s in ins] + [ANY] * n_thr,
                out_specs=[s for _, s in outs] + [ANY] * n_thr,
                scratch_shapes=list(scratch),
            ),
            input_output_aliases={1 + n_in + j: n_out + j for j in range(n_thr)},
            compiler_params=pltpu.CompilerParams(vmem_limit_bytes=VMEM_BYTES),
            name=name,
        )(self.flags, *[a for a, _ in ins], *carried)
        self.token = results[-1]
        return results[:-1]


def copy_all(copies, sems):
    made = [(c, pltpu.make_async_copy(s, d, sems.at[n])) for n, (c, s, d) in enumerate(copies)]
    for act in ("start", "wait"):
        for cond, copy in made:
            if cond is None:
                getattr(copy, act)()
            else:
                pl.when(cond)(getattr(copy, act))


def column(row):
    return jnp.transpose(jnp.broadcast_to(row, (LANES, row.shape[1])))


def per_device(sizes, logits, expression, spatial, slide_ids, spot_mask, densities):
    spot_size = sizes["spot"]
    rows, spots = logits.shape
    genes = spatial.shape[1]
    spots_all = spots * spot_size
    genes_all = genes * sizes["gene"]
    slots = sizes["gene"]
    quarter = spots // sizes["cell"]
    half = rows // 2
    cell, spot, gene = (lax.axis_index(a) for a in ("cell", "spot", "gene"))
    home = (gene // 2 == spot).astype(jnp.int32)
    side = (gene % 2).astype(jnp.int32)
    chain = Chain(jnp.stack([home, side, cell.astype(jnp.int32)]))
    run = chain.run
    offsets = [sum(WIDTHS[:n]) for n in range(len(WIDTHS))]
    chunks = range(len(WIDTHS))

    def over_core(v):
        return lax.ppermute(v, "cell", xor_pairs(4, 1))

    def over_x(v):
        return lax.ppermute(v, "cell", xor_pairs(4, 2))

    def over_gene(v, step):
        return lax.ppermute(v, "gene", xor_pairs(4, step))

    def over_spot(v, step=1):
        return lax.ppermute(v, "spot", xor_pairs(spot_size, step))

    def sum_spot(v):
        step = 1
        while step < spot_size:
            v = v + over_spot(v, step)
            step *= 2
        return v

    mask_f = spot_mask.astype(F32)
    order = cell ^ jnp.arange(sizes["cell"])

    def ordered(v):
        return v.reshape(sizes["cell"], quarter)[order].reshape(spots)

    lanes = jnp.arange(LANES)[None, :]
    ids_o, mask_o = ordered(slide_ids)[:, None], ordered(spot_mask)[:, None]
    member = jnp.where((lanes < SLIDES) & (lanes == ids_o) & (mask_o == 1), 1.0, 0.0)
    member = jnp.where(lanes == SLIDES, mask_o.astype(F32), member).astype(F32)
    dens_row = densities.reshape(1, rows)

    expr = expression.reshape(2, half * 2, genes) if spot_size == 2 else None
    st = {}

    def start_swap(c):
        w, o = WIDTHS[c], offsets[c] // WIDTHS[c]
        blk = (1, half, w)

        def body(fl, i, out):
            out[0][...] = i[0][...]
            out[1][...] = i[1][...]

        spec_a = pl.BlockSpec(
            blk, lambda g, f: (jnp.where(f[0] == 1, f[1], g), jnp.where(f[0] == 1, g, 0), o)
        )
        spec_b = pl.BlockSpec(blk, lambda g, f: (1 - f[1], g, o))
        out_spec = pl.BlockSpec(blk, lambda g, f: (g, 0, 0))
        ya, yb = run(
            f"swap{c}", body, [(expr, spec_a), (expr, spec_b)], [(sds((2, half, w), BF), out_spec)] * 2, grid=(2,)
        )
        st["y", c] = lax.ppermute(ya, "spot", xor_pairs(2, 1))
        st["n", c] = lax.ppermute(yb, ("spot", "gene"), [(0, 1), (1, 0), (6, 7), (7, 6)])

    def start_far(c):
        w, o = WIDTHS[c], offsets[c] // WIDTHS[c]
        blk = (1, half, w)

        def body(fl, i, out):
            @pl.when(fl[0] == 1)
            def _():
                out[0][...] = i[0][0]
                out[1][...] = i[1][0]

            @pl.when(fl[0] == 0)
            def _():
                out[0][...] = i[2][0]
                out[1][...] = i[3][0]

        specs = [
            pl.BlockSpec(blk, lambda g, f: (f[1], 0, 0)),
            pl.BlockSpec(blk, lambda g, f: (1 - f[1], 0, 0)),
            pl.BlockSpec(blk, lambda g, f: (f[1], 1, o)),
            pl.BlockSpec(blk, lambda g, f: (1 - f[1], 1, o)),
        ]
        y = st["y", c]
        a, b = run(
            f"far{c}", body, list(zip([y, y, expr, expr], specs)), [(sds((half, w), BF), whole((half, w)))] * 2
        )
        st["f2", c], st["f3", c] = over_gene(a, 2), over_gene(b, 3)

    def start_near(c):
        (st["n", c],) = run(f"near{c}", None, through=[st["n", c]])
        st["l", c] = lax.ppermute(st["n", c], ("spot", "gene"), [(0, 4), (1, 5), (6, 2), (7, 3)])

    def start_back(c):
        st["f2", c], st["f3", c] = run(f"back{c}", None, through=[st["f2", c], st["f3", c]])
        st["s2", c], st["s3", c] = over_spot(st["f2", c]), over_spot(st["f3", c])

    def totals(n):
        if n == 0:

            def body(fl, i, out):
                out[0][...] = jnp.zeros((8, spots), F32)
                out[0][0:1, :] = jnp.sum(jnp.exp(i[0][...].astype(F32)), axis=0, keepdims=True)
                out[0][1:2, :] = jnp.broadcast_to(jnp.sum(i[1][...]), (1, spots))

            (v,) = run(
                "totals", body, [(logits, whole(logits.shape)), (dens_row, whole(dens_row.shape))],
                [(sds((8, spots), F32), whole((8, spots)))],
            )
            st["tot"] = (v, over_core(v))
        elif n in (1, 2):

            def body(fl, i, out):
                out[0][...] = i[0][...] + i[1][...]

            sp = whole((8, spots))
            (v,) = run(f"totals{n}", body, [(a, sp) for a in st["tot"]], [(sds((8, spots), F32), sp)])
            st["tot"] = (v, over_x(v)) if n == 1 else (v, *[over_gene(v, s) for s in (1, 2, 3)])
        else:
            blk = LANES

            def body(fl, i, out):
                tot = (i[1][...] + i[2][...]) + (i[3][...] + i[4][...])
                out[3][...] = tot
                inv = 1.0 / tot[0:1, :]
                log_tot = jnp.log(tot[0:1, :])
                vals = i[0][...].astype(F32)
                prob = jnp.exp(vals) * inv
                ent = -jnp.sum(prob * (vals - log_tot))
                prob_t = jnp.transpose(prob)
                out[1][...] = jnp.broadcast_to(jnp.sum(prob_t, axis=0, keepdims=True), (8, blk))
                for q in range(sizes["cell"]):
                    at = pl.multiple_of((fl[2] ^ q) * quarter, quarter)
                    out[0][pl.ds(at, quarter), :] = prob_t[q * quarter : (q + 1) * quarter].astype(BF)

                @pl.when(pl.program_id(0) == 0)
                def _():
                    out[2][...] = jnp.zeros((8, LANES), F32)

                out[2][...] += ent

            sp = whole((8, spots))
            pt, mass, ent, tot = run(
                "prob", body,
                [(logits, pl.BlockSpec((blk, spots), lambda g, f: (g, 0)))] + [(a, sp) for a in st["tot"]],
                [
                    (sds((spots, rows), BF), pl.BlockSpec((spots, blk), lambda g, f: (0, g))),
                    (sds((8, rows), F32), pl.BlockSpec((8, blk), lambda g, f: (0, g))),
                    (sds((8, LANES), F32), whole((8, LANES))),
                    (sds((8, spots), F32), sp),
                ],
                grid=(rows // blk,),
            )
            st["pt"], st["ent"], st["tot"] = pt, ent, tot
            st["mass"] = [mass, over_spot(mass)] if spot_size == 2 else [sum_spot(mass)]

    def shares(_):
        masses = st["mass"]

        def body(fl, i, out):
            mass = i[2][0:1, :]
            for extra in i[3:]:
                mass = mass + extra[0:1, :]
            share = i[0][...] / i[1][1:2, 0:1]
            out[0][...] = jnp.broadcast_to(share / mass, (8, rows))
            kl = jnp.sum(share * (jnp.log(share) - jnp.log(mass / spots_all)))
            out[1][...] = jnp.broadcast_to(kl, (8, LANES))

        st["sm"], st["kl"] = run(
            "shares", body,
            [(dens_row, whole(dens_row.shape)), (st["tot"], whole((8, spots)))]
            + [(m, whole((8, rows))) for m in masses],
            [(sds((8, rows), F32), whole((8, rows))), (sds((8, LANES), F32), whole((8, LANES)))],
        )

    def target(n):
        blk = (quarter, genes)
        if n == 0:

            def body(fl, i, out):
                out[0][...] = i[0][...]

            (v,) = run(
                "target", body, [(spatial, pl.BlockSpec(blk, lambda g, f: (f[2], 0)))], [(sds(blk, BF), whole(blk))]
            )
            st["t"] = [v] + [over_gene(v, s) for s in (1, 2, 3)]
        elif n == 1:
            shape = (slots, *blk)

            def body(fl, i, out):
                for s in range(slots):
                    out[0][s] = i[s][...]

            (v,) = run("target1", body, [(a, whole(blk)) for a in st["t"]], [(sds(shape, BF), whole(shape))])
            st["t"] = [v, over_core(v), over_x(v)]
        else:
            (v,) = run("target2", None, through=[st["t"][2]])
            st["t"] = [st["t"][0], st["t"][1], v, over_core(v)]

    def forward(c):
        w = WIDTHS[c]
        wide = slots * w
        shape = (2, quarter, wide)
        outs = [
            (sds((rows, wide), BF), whole((rows, wide))),
            (sds(shape, F32), whole(shape)),
            (sds(shape, F32), whole(shape)),
        ]

        def product(pt, ef, keep, send):
            tile = 256

            @pl.loop(0, wide // tile)
            def _(n):
                at = pl.ds(pl.multiple_of(n * tile, tile), tile)
                acc = jnp.dot(pt[...], ef[:, at], preferred_element_type=F32)
                for q, ref in enumerate((keep, send, keep, send)):
                    ref[q // 2, :, at] = acc[q * quarter : (q + 1) * quarter]

        if spot_size == 2:
            col = pl.ds(offsets[c], w)

            def body(fl, i, out, sems):
                pt, e, y, n, l, f2, f3, s2, s3 = i
                ef = out[0]
                at_home, away = fl[0] == 1, fl[0] == 0
                top, low = pl.ds(0, half), pl.ds(half, half)
                copies = [
                    (at_home, e.at[fl[1], :, col], ef.at[:, pl.ds(0, w)]),
                    (away, y.at[0], ef.at[top, pl.ds(0, w)]),
                    (away, y.at[1], ef.at[low, pl.ds(0, w)]),
                ]
                for part, at in ((0, top), (1, low)):
                    copies += [
                        (at_home, n.at[part], ef.at[at, pl.ds(w, w)]),
                        (away, l.at[part], ef.at[at, pl.ds(w, w)]),
                    ]
                for s, direct, swapped in ((2, f2, s2), (3, f3, s3)):
                    cols = pl.ds(s * w, w)
                    copies += [
                        (at_home, direct, ef.at[low, cols]),
                        (at_home, swapped, ef.at[top, cols]),
                        (away, direct, ef.at[top, cols]),
                        (away, swapped, ef.at[low, cols]),
                    ]
                copy_all(copies, sems)
                product(pt, ef, out[1], out[2])

            names = ("y", "n", "l", "f2", "f3", "s2", "s3")
            ins = [(st["pt"], whole((spots, rows))), (expr, ANY)] + [(st[k, c], ANY) for k in names]
            scratch = [pltpu.SemaphoreType.DMA((16,))]
        else:

            def body(fl, i, out):
                for s in range(slots):
                    out[0][:, s * w : (s + 1) * w] = i[1 + s][...]
                product(i[0], *out)

            o = offsets[c] // w
            ins = [(st["pt"], whole((spots, rows)))] + [
                (a, pl.BlockSpec((rows, w), lambda *_: (0, o))) for a in st["pieces"]
            ]
            scratch = []
        st["e", c], keep, send = run(f"forward{c}", body, ins, outs, scratch=scratch)
        st["r", c] = (keep, over_core(send))

    def reduce_core(c):
        wide = slots * WIDTHS[c]
        shape, one = (2, quarter, wide), (quarter, wide)

        def body(fl, i, out):
            out[0][...] = i[0][0] + i[1][0]
            out[1][...] = i[0][1] + i[1][1]

        a, b = run(
            f"core{c}", body, [(v, whole(shape)) for v in st["r", c]], [(sds(one, F32), whole(one))] * 2
        )
        st["r", c] = (a, over_x(b))

    def reduce_x(c):
        w = WIDTHS[c]
        one, part = (quarter, slots * w), (quarter, w)

        def body(fl, i, out):
            for s in range(slots):
                at = slice(s * w, (s + 1) * w)
                out[s][...] = i[0][:, at] + i[1][:, at]

        parts = run(
            f"x{c}", body, [(v, whole(one)) for v in st["r", c]], [(sds(part, F32), whole(part))] * slots
        )
        st["r", c] = [parts[0]] + [over_gene(parts[s], s) for s in (1, 2, 3)]

    def reduce_gene(c):
        part = (quarter, WIDTHS[c])

        def body(fl, i, out):
            out[0][...] = (i[0][...] + i[1][...]) + (i[2][...] + i[3][...])

        (v,) = run(
            f"gene{c}", body, [(a, whole(part)) for a in st["r", c]], [(sds(part, F32), whole(part))]
        )
        st["r", c] = [v] + [over_gene(v, s) for s in (1, 2, 3)]

    def gather_x(c):
        w = WIDTHS[c]
        one, part = (quarter, slots * w), (quarter, w)

        def body(fl, i, out):
            for s in range(slots):
                out[0][:, s * w : (s + 1) * w] = i[s][...]

        (v,) = run(
            f"gather{c}", body, [(a, whole(part)) for a in st["r", c]], [(sds(one, F32), whole(one))]
        )
        st["p", c] = [v, over_core(v), over_x(v)]

    def gather_core(c):
        (v,) = run(f"gathercore{c}", None, through=[st["p", c][2]])
        st["p", c] = [st["p", c][0], st["p", c][1], v, over_core(v)]

    def stats(c):
        w = WIDTHS[c]
        wide, o = slots * w, offsets[c] // w
        n_blk = len(st["t"])
        first = c == 0

        def body(fl, i, out):
            preds, targets, memb = i[:n_blk], i[n_blk : 2 * n_blk], i[2 * n_blk]
            lane = lax.broadcasted_iota(jnp.int32, (quarter, LANES), 1)
            valid = jnp.sum(memb[:, SLIDES : SLIDES + 1])
            out[0][9:16, :] = jnp.broadcast_to(valid, (7, wide))
            for s in range(slots):
                at = slice(s * w, (s + 1) * w)
                rows_k = [jnp.zeros((1, w), F32) for _ in range(9)]
                for b in range(n_blk):
                    pr, ta = preds[b][:, at], targets[b][s].astype(F32)
                    prods = (pr * ta, pr * pr, ta * ta)
                    mb = slice(b * quarter, (b + 1) * quarter)
                    spot_vals = [jnp.sum(v, axis=1, keepdims=True) for v in prods]
                    new = jnp.where(lane == 0, spot_vals[0], 0.0)
                    new = jnp.where(lane == 1, spot_vals[1], new)
                    new = jnp.where(lane == 2, spot_vals[2], new)
                    if s > 0:
                        new = new + out[1][mb, :]
                    elif not first:
                        new = new + i[2 * n_blk + 1][mb, :]
                    out[1][mb, :] = new
                    for k in range(SLIDES):
                        col = memb[mb, k : k + 1]
                        for j, v in enumerate(prods):
                            rows_k[3 * j + k] += jnp.sum(col * v, axis=0, keepdims=True)
                for n, v in enumerate(rows_k):
                    out[0][n : n + 1, at] = v

        ins = [(a, whole((quarter, wide))) for a in st["p", c]]
        ins += [(a, pl.BlockSpec((slots, quarter, w), lambda *_: (0, 0, o))) for a in st["t"]]
        ins += [(member, whole((spots, LANES)))]
        if not first:
            ins += [(st["sp"], whole((spots, LANES)))]
        gs, st["sp"] = run(
            f"stats{c}", body, ins,
            [(sds((16, wide), F32), whole((16, wide))), (sds((spots, LANES), F32), whole((spots, LANES)))],
        )
        st["gs", c] = [gs, over_spot(gs)] if spot_size == 2 else [sum_spot(gs)]

    steps = {
        "Y": start_swap, "Z": start_far, "L": start_near, "S": start_back, "e": totals, "m": shares, "t": target,
        "F": forward, "P": reduce_core, "Q": reduce_x, "R": reduce_gene, "G": gather_x, "H": gather_core, "T": stats,
    }
    if spot_size != 2:
        full = lax.all_gather(expression, "spot", axis=0, tiled=True).reshape(slots, rows, genes)
        pieces = [lax.dynamic_index_in_dim(full, gene ^ s, 0, False) for s in range(slots)]
        st["pieces"] = [pieces[0]] + [over_gene(pieces[s], s) for s in (1, 2, 3)]
    for word in " ".join(ORDER).split():
        if spot_size == 2 or word[0] not in "YZLS":
            steps[word[0]](int(word[1]))

    row_blk = rows // 2
    n_blk = sizes["cell"]
    n_ch = len(WIDTHS)
    n_gs = len(st["gs", 0])

    def backward_body(fl, i, out, *grads):
        i = list(i)
        lg, tot, sm, memb, sp = i[:5]
        efs = i[5 : 5 + n_ch]
        gss = i[5 + n_ch : 5 + n_ch + n_ch * n_gs]
        preds = i[5 + n_ch + n_ch * n_gs : 5 + n_ch + n_ch * n_gs + n_ch * n_blk]
        targets = i[5 + n_ch + n_ch * n_gs + n_ch * n_blk :]

        @pl.when(pl.program_id(0) == 0)
        def _():
            scale = -1.0 / (SLIDES * genes_all)
            gene_sum = jnp.zeros((), F32)
            gene_rows = []
            for c in range(n_ch):
                g_all = gss[c * n_gs][...]
                for extra in gss[c * n_gs + 1 : (c + 1) * n_gs]:
                    g_all = g_all + extra[...]
                num, psq, tsq = g_all[0:3], g_all[3:6], g_all[6:9]
                p_floor, t_floor = jnp.maximum(psq, 1.0), jnp.maximum(tsq, 1.0)
                root = jnp.sqrt(p_floor * t_floor)
                cosine = num / root
                w_t = scale / root
                w_p = jnp.where(psq > 1.0, -scale * cosine / p_floor, 0.0)
                gene_rows.append((w_t, w_p))
                gene_sum += jnp.sum(cosine[:, 0 : WIDTHS[c]])
                if c == 0:
                    valid_total = jnp.maximum(g_all[9, 0], 1.0)
            spot_sum = jnp.zeros((), F32)
            for b in range(n_blk):
                mb = slice(b * quarter, (b + 1) * quarter)
                s_num = sp[mb, 0:1]
                s_p, s_t = sp[mb, 1:2] + 1e-06, sp[mb, 2:3] + 1e-06
                root = jnp.sqrt(s_p * s_t)
                cos_spot = s_num / root
                valid = memb[mb, SLIDES : SLIDES + 1]
                coef = -valid / valid_total
                spot_sum += jnp.sum(valid * cos_spot)
                c_t, c_p = coef / root, -coef * cos_spot / s_p
                cols = [memb[mb, k : k + 1] for k in range(SLIDES)]
                to = pl.ds(pl.multiple_of((fl[2] ^ b) * quarter, quarter), quarter)
                for c in range(n_ch):
                    w = WIDTHS[c]
                    w_t, w_p = gene_rows[c]
                    for s in range(slots):
                        at = slice(s * w, (s + 1) * w)
                        f_t, f_p = c_t, c_p
                        for k in range(SLIDES):
                            f_t = f_t + cols[k] * w_t[k : k + 1, at]
                            f_p = f_p + cols[k] * w_p[k : k + 1, at]
                        ta = targets[b][s, :, offsets[c] : offsets[c] + w].astype(F32)
                        pr = preds[c * n_blk + b][:, at]
                        grads[c][to, at] = (f_t * ta + f_p * pr).astype(BF)
            out[1][...] = jnp.zeros((8, spots), F32)
            lane = lax.broadcasted_iota(jnp.int32, (1, spots), 1)
            out[1][1:2, :] = jnp.where(lane == 0, gene_sum, jnp.where(lane == 1, spot_sum, 0.0))

        acc = jnp.zeros((row_blk, spots), F32)
        for c in range(n_ch):
            acc += lax.dot_general(
                efs[c][...], grads[c][...], (((1,), (1,)), ((), ())), preferred_element_type=F32
            )
        acc = acc - column(sm[0:1, :])[:, 0:1]
        out[0][...] = acc
        prob = jnp.exp(lg[...].astype(F32)) * (1.0 / tot[0:1, :])
        out[1][0:1, :] += jnp.sum(prob * acc, axis=0, keepdims=True)

    ins = [
        (logits, pl.BlockSpec((row_blk, spots), lambda g, f: (g, 0))),
        (st["tot"], whole((8, spots))),
        (st["sm"], pl.BlockSpec((8, row_blk), lambda g, f: (0, g))),
        (member, whole((spots, LANES))),
        (st["sp"], whole((spots, LANES))),
    ]
    ins += [(st["e", c], pl.BlockSpec((row_blk, slots * WIDTHS[c]), lambda g, f: (g, 0))) for c in chunks]
    ins += [(a, whole(a.shape)) for c in chunks for a in st["gs", c]]
    ins += [(a, whole(a.shape)) for c in chunks for a in st["p", c]]
    ins += [(a, whole(a.shape)) for a in st["t"]]
    grad_probs, part = run(
        "backward", backward_body, ins,
        [
            (sds((rows, spots), F32), pl.BlockSpec((row_blk, spots), lambda g, f: (g, 0))),
            (sds((8, spots), F32), whole((8, spots))),
        ],
        grid=(rows // row_blk,),
        scratch=[pltpu.VMEM((spots, slots * w), BF) for w in WIDTHS],
    )

    firsts = [jnp.where(a == 0, 1.0, 0.0) for a in (cell, spot, gene)]
    terms = jnp.stack(
        [
            part[1, 0] * firsts[0] * firsts[1],
            part[1, 1] * firsts[0] * firsts[2],
            st["kl"][0, 0] * firsts[1],
            st["ent"][0, 0],
        ]
    )
    v = jnp.concatenate([part[0], terms, jnp.zeros((4,), F32)])
    v = v + over_core(v)
    v = v + over_x(v)
    v = (v + over_gene(v, 1)) + (over_gene(v, 2) + over_gene(v, 3))
    inner = jnp.broadcast_to(v[None, :spots], (8, spots))

    def final_body(fl, i, out):
        prob = jnp.exp(i[0][...].astype(F32)) * (1.0 / i[1][0:1, :])
        out[0][...] = prob * (i[2][...] - i[3][0:1, :])

    blk = pl.BlockSpec((row_blk, spots), lambda g, f: (g, 0))
    (grad_logits,) = run(
        "final", final_body,
        [(logits, blk), (st["tot"], whole((8, spots))), (grad_probs, blk), (inner, whole((8, spots)))],
        [(sds((rows, spots), F32), blk)], grid=(rows // row_blk,),
    )
    sums = sum_spot(v[spots : spots + 4])
    valid_total = jnp.maximum(sum_spot(jnp.sum(mask_f)), 1.0)
    gene_term = sums[0] / (SLIDES * genes_all)
    spot_term = sums[1] / valid_total
    divergence = sums[2]
    entropy = sums[3] / spots_all
    loss_terms = jnp.stack([divergence - gene_term - spot_term, gene_term, spot_term, divergence, entropy])
    return (loss_terms, grad_logits)


def solution(mesh):
    return jax.shard_map(
        functools.partial(per_device, dict(mesh.shape)),
        mesh=mesh,
        in_specs=(
            P(("cell", "gene"), "spot"),
            P(("cell", "spot"), "gene"),
            P("spot", "gene"),
            P("spot"),
            P("spot"),
            P(("cell", "gene")),
        ),
        out_specs=(P(), P(("cell", "gene"), "spot")),
        check_vma=False,
    )
```

```python
import functools
import jax
import jax.numpy as jnp
from jax import lax
from jax.experimental import pallas as pl
from jax.experimental.pallas import tpu as pltpu
from jax.sharding import PartitionSpec as P

SLIDES = 3
LANES = 128
ANY = pl.BlockSpec(memory_space=pl.ANY)
BF = jnp.bfloat16
F32 = jnp.float32
VMEM_BYTES = 64 * 1024 * 1024
WIDTHS = (128, 128, 128, 128)
GROUPS = ((0, 1), (2, 3))
ORDER = (
    "Y0 e0 Y1 w:ez1+ez2+ez3",
    "Y2 A0 a0 e3",
    "b0 A1 Y3 w:f20+f30+n0",
    "a1 A2 w:f21+f31+n1 a2",
    "S0 A3 w:f22+f32+n2 a3",
    "S1 w:s0 S2 w:s1",
    "F0 w:f23+f33+n3 S3 f0",
    "t0 P0 w:s2 t1",
    "Q0 w:s3 F1 f1",
    "P1 R0 t2 Q1",
    "W0 R1 H0 W1",
    "T0 H1 m0 T1",
)


def sds(shape, dtype):
    return jax.ShapeDtypeStruct(shape, dtype)


def whole(shape):
    zeros = (0,) * len(shape)
    return pl.BlockSpec(shape, lambda *_: zeros)


def xor_pairs(size, step):
    return [(n, n ^ step) for n in range(size)]


class Chain:
    def __init__(self, flags):
        self.flags = flags
        self.token = jnp.zeros((8, LANES), F32)

    def run(self, name, body, ins=(), outs=(), after=(), through=(), grid=(1,), scratch=()):
        ins = [*ins, *((a, ANY) for a in after)]
        carried = (*through, self.token)
        n_in, n_out, n_thr = len(ins), len(outs), len(carried)

        def kernel(flags, *refs):
            in_refs = refs[:n_in]
            out_refs = refs[n_in + n_thr : n_in + n_thr + n_out]
            scratch_refs = refs[n_in + 2 * n_thr + n_out :]
            if body is not None:
                body(flags, in_refs, out_refs, *scratch_refs)

        results = pl.pallas_call(
            kernel,
            out_shape=[s for s, _ in outs] + [sds(a.shape, a.dtype) for a in carried],
            grid_spec=pltpu.PrefetchScalarGridSpec(
                num_scalar_prefetch=1,
                grid=grid,
                in_specs=[s for _, s in ins] + [ANY] * n_thr,
                out_specs=[s for _, s in outs] + [ANY] * n_thr,
                scratch_shapes=list(scratch),
            ),
            input_output_aliases={1 + n_in + j: n_out + j for j in range(n_thr)},
            compiler_params=pltpu.CompilerParams(vmem_limit_bytes=VMEM_BYTES),
            cost_estimate=pl.CostEstimate(flops=0, bytes_accessed=0, transcendentals=0),
            name=name,
        )(self.flags, *[a for a, _ in ins], *carried)
        self.token = results[-1]
        return results[:-1]


def copy_all(copies, sems):
    made = [(c, pltpu.make_async_copy(s, d, sems.at[n])) for n, (c, s, d) in enumerate(copies)]
    for act in ("start", "wait"):
        for cond, copy in made:
            if cond is None:
                getattr(copy, act)()
            else:
                pl.when(cond)(getattr(copy, act))


def column(row):
    return jnp.transpose(jnp.broadcast_to(row, (LANES, row.shape[1])))


def per_device(sizes, logits, expression, spatial, slide_ids, spot_mask, densities):
    spot_size = sizes["spot"]
    rows, spots = logits.shape
    genes = spatial.shape[1]
    spots_all = spots * spot_size
    genes_all = genes * sizes["gene"]
    slots = sizes["gene"]
    quarter = spots // sizes["cell"]
    half = rows // 2
    cell, spot, gene = (lax.axis_index(a) for a in ("cell", "spot", "gene"))
    home = (gene // 2 == spot).astype(jnp.int32)
    side = (gene % 2).astype(jnp.int32)
    chain = Chain(jnp.stack([home, side, cell, gene, spot]).astype(jnp.int32))
    run = chain.run
    offsets = [sum(WIDTHS[:n]) for n in range(len(WIDTHS))]
    chunks = range(len(WIDTHS))
    group_width = [sum(WIDTHS[c] for c in g) for g in GROUPS]

    def over_core(v):
        return lax.ppermute(v, "cell", xor_pairs(4, 1))

    def over_x(v):
        return lax.ppermute(v, "cell", xor_pairs(4, 2))

    def over_gene(v, step):
        return lax.ppermute(v, "gene", xor_pairs(4, step))

    def over_spot(v, step=1):
        return lax.ppermute(v, "spot", xor_pairs(spot_size, step))

    def sum_spot(v):
        step = 1
        while step < spot_size:
            v = v + over_spot(v, step)
            step *= 2
        return v

    ids_row, mask_row = slide_ids.reshape(1, spots), spot_mask.reshape(1, spots)
    dens_row = densities.reshape(1, rows)

    expr = expression.reshape(2, half * 2, genes) if spot_size == 2 else None
    st, sent = {}, {}

    def start_swap(c):
        w, o = WIDTHS[c], offsets[c] // WIDTHS[c]

        def body(fl, i, out):
            out[0][...] = i[0][...]

        (v,) = run(
            f"swap{c}", body, [(expr, pl.BlockSpec((1, rows, w), lambda g, f: (g, 0, o)))],
            [(sds((2, rows, w), BF), pl.BlockSpec((1, rows, w), lambda g, f: (g, 0, 0)))], grid=(2,),
        )
        sent[f"y{c}"] = over_spot(v)

    def start_along(c):
        w, o = WIDTHS[c], offsets[c] // WIDTHS[c]
        blk, one = (1, half, w), (half, w)

        def body(fl, i, out):
            @pl.when(fl[0] == 1)
            def _():
                out[0][...] = i[0][0]
                out[1][...] = i[1][0]
                out[2][0] = i[2][0]
                out[2][1] = i[3][0]

            @pl.when(fl[0] == 0)
            def _():
                out[0][...] = i[4][0]
                out[1][...] = i[5][0]
                out[2][0] = i[6][0]
                out[2][1] = i[7][0]

        def at(same, part, col):
            return pl.BlockSpec(blk, lambda g, f: (f[1] if same else 1 - f[1], part, col))

        y = sent[f"y{c}"]
        ins = [(y, at(True, 0, 0)), (y, at(False, 0, 0)), (expr, at(False, 0, o)), (expr, at(False, 1, o))]
        ins += [(expr, at(True, 1, o)), (expr, at(False, 1, o)), (y, at(False, 0, 0)), (y, at(False, 1, 0))]
        outs = [(sds(one, BF), whole(one))] * 2 + [(sds((2, half, w), BF), whole((2, half, w)))]
        st["along", c] = run(f"along{c}", body, ins, outs)

    def along_send(c):
        a, b, n = run(f"alongsend{c}", None, through=st["along", c])
        sent[f"f2{c}"], sent[f"f3{c}"], sent[f"n{c}"] = over_gene(a, 2), over_gene(b, 3), over_gene(n, 1)

    def start_back(c):
        w = WIDTHS[c]

        def body(fl, i, out):
            out[0][0] = i[0][...]
            out[0][1] = i[1][...]

        one = whole((half, w))
        (st["f", c],) = run(
            f"back{c}", body, [(sent[f"f2{c}"], one), (sent[f"f3{c}"], one)], [(sds((2, half, w), BF), whole((2, half, w)))]
        )
        sent[f"s{c}"] = over_spot(st["f", c])

    def wait_for(name):
        run("wait", None, after=[sent[n] for n in name.split("+")])

    def members_of(_):
        def body(fl, i, out):
            ids, valid = column(i[0][...].astype(F32)), column(i[1][...].astype(F32))
            lane = lax.broadcasted_iota(jnp.int32, (spots, LANES), 1)
            inside = (lane < SLIDES) & (lane.astype(F32) == ids) & (valid == 1.0)
            value = jnp.where(inside, 1.0, jnp.where(lane == SLIDES, valid, 0.0))
            for q in range(sizes["cell"]):
                at = pl.multiple_of((fl[2] ^ q) * quarter, quarter)
                out[0][pl.ds(at, quarter), :] = value[q * quarter : (q + 1) * quarter]

        row, tall = whole((1, spots)), whole((spots, LANES))
        (st["member"],) = run("member", body, [(ids_row, row), (mask_row, row)], [(sds((spots, LANES), F32), tall)])

    def totals(n):
        sp = whole((8, spots))
        if n == 0:

            def body(fl, i, out):
                out[0][...] = jnp.zeros((8, spots), F32)
                out[0][0:1, :] = jnp.sum(jnp.exp(i[0][...].astype(F32)), axis=0, keepdims=True)
                out[0][1:2, :] = jnp.broadcast_to(jnp.sum(i[1][...]), (1, spots))

            ins = [(logits, whole(logits.shape)), (dens_row, whole(dens_row.shape))]
            (v,) = run("totals", body, ins, [(sds((8, spots), F32), sp)])
            st["tot"] = lax.psum(v, "cell")
            for s in (1, 2, 3):
                sent[f"ez{s}"] = over_gene(st["tot"], s)
        else:
            blk = 2 * LANES

            def body(fl, i, out):
                tot = (i[1][...] + i[2][...]) + (i[3][...] + i[4][...])
                out[3][...] = tot
                inv = 1.0 / tot[0:1, :]
                log_tot = jnp.log(tot[0:1, :])
                vals = i[0][...].astype(F32)
                prob = jnp.exp(vals) * inv
                prob_t = jnp.transpose(prob.astype(BF))
                for q in range(sizes["cell"]):
                    at = pl.multiple_of((fl[2] ^ q) * quarter, quarter)
                    out[0][pl.ds(at, quarter), :] = prob_t[q * quarter : (q + 1) * quarter]
                folded = sum(prob[:, n : n + LANES] for n in range(0, spots, LANES))
                row_sums = jnp.sum(jnp.transpose(folded), axis=0, keepdims=True)
                out[1][...] = jnp.broadcast_to(row_sums, (8, blk))

                @pl.when(pl.program_id(0) == 0)
                def _():
                    out[2][...] = jnp.zeros((8, spots), F32)

                out[2][0:1, :] -= jnp.sum(prob * (vals - log_tot), axis=0, keepdims=True)

            parts = [st["tot"]] + [sent[f"ez{s}"] for s in (1, 2, 3)]
            pt, mass, ent, st["tot"] = run(
                "prob", body,
                [(logits, pl.BlockSpec((blk, spots), lambda g, f: (g, 0)))] + [(a, sp) for a in parts],
                [
                    (sds((spots, rows), BF), pl.BlockSpec((spots, blk), lambda g, f: (0, g))),
                    (sds((8, rows), F32), pl.BlockSpec((8, blk), lambda g, f: (0, g))),
                    (sds((8, spots), F32), sp),
                    (sds((8, spots), F32), sp),
                ],
                grid=(rows // blk,),
            )
            st["pt"], st["ent"] = pt, ent
            st["mass"] = mass if spot_size == 2 else sum_spot(mass)
            if spot_size == 2:
                sent["my"] = over_spot(mass)

    def shares(_):
        masses = [st["mass"]] + ([sent["my"]] if spot_size == 2 else [])

        def body(fl, i, out):
            mass = i[2][0:1, :]
            for extra in i[3:]:
                mass = mass + extra[0:1, :]
            share = i[0][...] / i[1][1:2, 0:1]
            out[0][...] = column(share / mass)
            kl = jnp.sum(share * (jnp.log(share) - jnp.log(mass / spots_all)))
            out[1][...] = jnp.broadcast_to(kl, (8, LANES))

        st["sm"], st["kl"] = run(
            "shares", body,
            [(dens_row, whole(dens_row.shape)), (st["tot"], whole((8, spots)))]
            + [(m, whole((8, rows))) for m in masses],
            [(sds((rows, LANES), F32), whole((rows, LANES))), (sds((8, LANES), F32), whole((8, LANES)))],
        )

    def target(n):
        blk = (quarter, genes)
        if n == 0:

            def body(fl, i, out):
                out[0][...] = i[0][...]

            (v,) = run(
                "target", body, [(spatial, pl.BlockSpec(blk, lambda g, f: (f[2], 0)))], [(sds(blk, BF), whole(blk))]
            )
            st["t"] = v
            for s in (1, 2, 3):
                sent[f"tz{s}"] = over_gene(v, s)
        elif n == 1:
            shape = (slots, *blk)

            def body(fl, i, out):
                for s in range(slots):
                    out[0][s] = i[s][...]

            parts = [st["t"]] + [sent[f"tz{s}"] for s in (1, 2, 3)]
            (v,) = run("target1", body, [(a, whole(blk)) for a in parts], [(sds(shape, BF), whole(shape))])
            st["t"], sent["tc"], sent["tx"] = v, over_core(v), over_x(v)
        else:
            run("target2", None, after=[sent["tx"]])
            sent["tc2"] = over_core(sent["tx"])

    def forward(g):
        members, wide_all = GROUPS[g], group_width[g] * slots
        shape = (2, quarter, wide_all)
        outs = [(sds((rows, slots * WIDTHS[c]), BF), whole((rows, slots * WIDTHS[c]))) for c in members]
        outs += [(sds(shape, F32), whole(shape))] * 2

        def product(pt, efs, keep, send):
            done = 0
            for c, ef in zip(members, efs):
                w = WIDTHS[c]
                acc = jnp.dot(pt[...], ef[...], preferred_element_type=F32)
                for q, ref in enumerate((keep, send, keep, send)):
                    rows_q = acc[q * quarter : (q + 1) * quarter]
                    for s in range(slots):
                        base = s * group_width[g] + done
                        ref[q // 2, :, base : base + w] = rows_q[:, s * w : (s + 1) * w]
                done += w

        if spot_size == 2:

            def body(fl, i, out, sems):
                pt, e = i[:2]
                at_home, away = fl[0] == 1, fl[0] == 0
                top, low = pl.ds(0, half), pl.ds(half, half)
                copies = []
                for m, c in enumerate(members):
                    w, ef = WIDTHS[c], out[m]
                    y, n, f, s = i[2 + 4 * m : 6 + 4 * m]
                    copies += [
                        (at_home, e.at[fl[1], :, pl.ds(offsets[c], w)], ef.at[:, pl.ds(0, w)]),
                        (away, y.at[fl[1]], ef.at[:, pl.ds(0, w)]),
                        (None, n.at[0], ef.at[top, pl.ds(w, w)]),
                        (None, n.at[1], ef.at[low, pl.ds(w, w)]),
                    ]
                    for part in (0, 1):
                        cols = pl.ds((2 + part) * w, w)
                        copies += [
                            (at_home, f.at[part], ef.at[low, cols]),
                            (at_home, s.at[part], ef.at[top, cols]),
                            (away, f.at[part], ef.at[top, cols]),
                            (away, s.at[part], ef.at[low, cols]),
                        ]
                copy_all(copies, sems)
                product(pt, out[: len(members)], *out[len(members) :])

            ins = [(st["pt"], whole((spots, rows))), (expr, ANY)]
            ins += [
                (a, ANY)
                for c in members
                for a in (sent[f"y{c}"], sent[f"n{c}"], st["f", c], sent[f"s{c}"])
            ]
            scratch = [pltpu.SemaphoreType.DMA((12 * len(members),))]
        else:

            def body(fl, i, out):
                for m, c in enumerate(members):
                    w = WIDTHS[c]
                    for s in range(slots):
                        out[m][:, s * w : (s + 1) * w] = i[1 + m * slots + s][...]
                product(i[0], out[: len(members)], *out[len(members) :])

            def at_chunk(c):
                return pl.BlockSpec((rows, WIDTHS[c]), lambda *_: (0, offsets[c] // WIDTHS[c]))

            ins = [(st["pt"], whole((spots, rows)))] + [(a, at_chunk(c)) for c in members for a in st["pieces"]]
            scratch = []
        *efs, keep, send = run(f"forward{g}", body, ins, outs, scratch=scratch)
        for c, ef in zip(members, efs):
            st["e", c] = ef
        st["r", g], st["send", g] = keep, send

    def forward_send(g):
        (send,) = run(f"send{g}", None, through=[st["send", g]])
        sent[f"rc{g}"] = over_core(send)

    def reduce_core(g):
        wide = slots * group_width[g]
        shape, one = (2, quarter, wide), (quarter, wide)

        def body(fl, i, out):
            out[0][...] = i[0][0] + i[1][0]
            out[1][...] = i[0][1] + i[1][1]

        ins = [(st["r", g], whole(shape)), (sent[f"rc{g}"], whole(shape))]
        st["r", g], b = run(f"core{g}", body, ins, [(sds(one, F32), whole(one))] * 2)
        sent[f"rx{g}"] = over_x(b)

    def reduce_x(g):
        w = group_width[g]
        one, part = (quarter, slots * w), (quarter, w)

        def body(fl, i, out):
            for s in range(slots):
                at = slice(s * w, (s + 1) * w)
                out[s][...] = i[0][:, at] + i[1][:, at]

        ins = [(st["r", g], whole(one)), (sent[f"rx{g}"], whole(one))]
        st["r", g], *parts = run(f"x{g}", body, ins, [(sds(part, F32), whole(part))] * slots)
        for s in (1, 2, 3):
            sent[f"rz{s}{g}"] = over_gene(parts[s - 1], s)

    def reduce_gene(g):
        part = (quarter, group_width[g])

        def body(fl, i, out):
            out[0][...] = (i[0][...] + i[1][...]) + (i[2][...] + i[3][...])

        parts = [st["r", g]] + [sent[f"rz{s}{g}"] for s in (1, 2, 3)]
        (v,) = run(f"gene{g}", body, [(a, whole(part)) for a in parts], [(sds(part, F32), whole(part))])
        st["r", g] = v
        for s in (1, 2, 3):
            sent[f"gz{s}{g}"] = over_gene(v, s)

    def gather_x(g):
        w = group_width[g]
        one, part = (quarter, slots * w), (quarter, w)

        def body(fl, i, out):
            for s in range(slots):
                out[0][:, s * w : (s + 1) * w] = i[s][...]

        parts = [st["r", g]] + [sent[f"gz{s}{g}"] for s in (1, 2, 3)]
        (v,) = run(f"gather{g}", body, [(a, whole(part)) for a in parts], [(sds(one, F32), whole(one))])
        st["p", g], sent[f"gc{g}"], sent[f"gx{g}"] = v, over_core(v), over_x(v)

    def gather_core(g):
        v = sent[f"gx{g}"]
        run(f"gathercore{g}", None, after=[v])
        sent[f"gd{g}"] = over_core(v)

    def blocks_of(g):
        return [st["p", g], sent[f"gc{g}"], sent[f"gx{g}"], sent[f"gd{g}"]]

    def blocks_of_target():
        return [st["t"], sent["tc"], sent["tx"], sent["tc2"]]

    def stats(c):
        w = group_width[c]
        wide, o = slots * w, offsets[GROUPS[c][0]] // w
        n_blk = sizes["cell"]
        first = c == 0

        def body(fl, i, out):
            preds, targets, memb = i[:n_blk], i[n_blk : 2 * n_blk], i[2 * n_blk]
            lane = lax.broadcasted_iota(jnp.int32, (quarter, LANES), 1)
            valid = jnp.sum(memb[:, SLIDES : SLIDES + 1])
            out[0][9:16, :] = jnp.broadcast_to(valid, (7, wide))
            for s in range(slots):
                at = slice(s * w, (s + 1) * w)
                rows_k = [jnp.zeros((1, w), F32) for _ in range(9)]
                for b in range(n_blk):
                    pr, ta = preds[b][:, at], targets[b][s].astype(F32)
                    prods = (pr * ta, pr * pr, ta * ta)
                    mb = slice(b * quarter, (b + 1) * quarter)
                    spot_vals = [jnp.sum(v, axis=1, keepdims=True) for v in prods]
                    new = jnp.where(lane == 0, spot_vals[0], 0.0)
                    new = jnp.where(lane == 1, spot_vals[1], new)
                    new = jnp.where(lane == 2, spot_vals[2], new)
                    if s > 0:
                        new = new + out[1][mb, :]
                    elif not first:
                        new = new + i[2 * n_blk + 1][mb, :]
                    out[1][mb, :] = new
                    for k in range(SLIDES):
                        col = memb[mb, k : k + 1]
                        for j, v in enumerate(prods):
                            rows_k[3 * j + k] += jnp.sum(col * v, axis=0, keepdims=True)
                for n, v in enumerate(rows_k):
                    out[0][n : n + 1, at] = v

        ins = [(a, whole((quarter, wide))) for a in blocks_of(c)]
        ins += [(a, pl.BlockSpec((slots, quarter, w), lambda *_: (0, 0, o))) for a in blocks_of_target()]
        ins += [(st["member"], whole((spots, LANES)))]
        if not first:
            ins += [(st["sp"], whole((spots, LANES)))]
        gs, st["sp"] = run(
            f"stats{c}", body, ins,
            [(sds((16, wide), F32), whole((16, wide))), (sds((spots, LANES), F32), whole((spots, LANES)))],
        )
        if spot_size == 2:
            sent[f"gs{c}"] = over_spot(gs)
        st["gs", c] = [gs, sent[f"gs{c}"]] if spot_size == 2 else [sum_spot(gs)]

    steps = {
        "Y": start_swap, "A": start_along, "a": along_send, "S": start_back,
        "e": totals, "m": shares, "t": target, "F": forward, "f": forward_send, "b": members_of, "P": reduce_core, "Q": reduce_x, "R": reduce_gene,
        "W": gather_x, "H": gather_core, "T": stats,
    }
    if spot_size != 2:
        full = lax.all_gather(expression, "spot", axis=0, tiled=True).reshape(slots, rows, genes)
        pieces = [lax.dynamic_index_in_dim(full, gene ^ s, 0, False) for s in range(slots)]
        st["pieces"] = [pieces[0]] + [over_gene(pieces[s], s) for s in (1, 2, 3)]
    for word in " ".join(ORDER).split():
        if word[:2] == "w:":
            if spot_size == 2 or word == "w:ez1+ez2+ez3":
                wait_for(word[2:])
        elif spot_size == 2 or word[0] not in "YAaS":
            steps[word[0]](int(word[1]))

    n_blk = sizes["cell"]
    n_ch, n_gr = len(WIDTHS), len(GROUPS)
    n_gs = len(st["gs", 0])

    def grads_body(fl, i, out, coef_t, coef_p):
        i = list(i)
        memb, sp, kl, ent = i[:4]
        i = i[4:]
        gss, i = i[: n_gr * n_gs], i[n_gr * n_gs :]
        preds, targets = i[: n_gr * n_blk], i[n_gr * n_blk :]
        scale = -1.0 / (SLIDES * genes_all)
        sums, weights = [], []
        for g in range(n_gr):
            sums.append(sum(ref[...] for ref in gss[g * n_gs : (g + 1) * n_gs]))
            num, psq, tsq = sums[g][0:3], sums[g][3:6], sums[g][6:9]
            p_floor, t_floor = jnp.maximum(psq, 1.0), jnp.maximum(tsq, 1.0)
            root = jnp.sqrt(p_floor * t_floor)
            cosine = num / root
            weights.append((scale / root, jnp.where(psq > 1.0, -scale * cosine / p_floor, 0.0), cosine))

        @pl.when(pl.program_id(0) == 0)
        def _():
            valid_total = jnp.maximum(sums[0][9, 0], 1.0)
            s_num = sp[:, 0:1]
            s_p, s_t = sp[:, 1:2] + 1e-06, sp[:, 2:3] + 1e-06
            root = jnp.sqrt(s_p * s_t)
            cos_spot = s_num / root
            valid = memb[:, SLIDES : SLIDES + 1]
            coef = -valid / valid_total
            coef_t[...] = jnp.broadcast_to(coef / root, (spots, LANES))
            coef_p[...] = jnp.broadcast_to(-coef * cos_spot / s_p, (spots, LANES))
            first = [(fl[n] == 0).astype(F32) for n in (2, 4, 3)]
            terms = [
                sum(jnp.sum(w[2]) for w in weights) * first[0] * first[1],
                jnp.sum(valid * cos_spot) * first[0] * first[2],
                kl[0, 0] * first[1],
                jnp.sum(ent[0:1, :]),
                valid_total * first[0] * first[1] * first[2],
            ]
            lane = lax.broadcasted_iota(jnp.int32, (8, spots), 1)
            value = jnp.zeros((8, spots), F32)
            for n, term in enumerate(terms):
                value = jnp.where(lane == n, term, value)
            out[n_ch][...] = value

        for b in range(n_blk):
            mb = slice(b * quarter, (b + 1) * quarter)
            cols = [jnp.broadcast_to(memb[mb, k : k + 1], (quarter, LANES)) for k in range(SLIDES)]
            to = pl.ds(pl.multiple_of((fl[2] ^ b) * quarter, quarter), quarter)
            for g in range(n_gr):
                w_t, w_p, _ = weights[g]
                base = 0
                for c in GROUPS[g]:
                    for o in range(0, WIDTHS[c], LANES):
                        at = slice(base + o, base + o + LANES)
                        f_t, f_p = coef_t[mb, :], coef_p[mb, :]
                        for k in range(SLIDES):
                            f_t = f_t + cols[k] * w_t[k : k + 1, at]
                            f_p = f_p + cols[k] * w_p[k : k + 1, at]
                        start = offsets[c] + o
                        ta = targets[b][0, :, start : start + LANES].astype(F32)
                        pr = preds[g * n_blk + b][:, at]
                        out[c][to, o : o + LANES] = (f_t * ta + f_p * pr).astype(BF)
                    base += WIDTHS[c]

    def by_slot(rows_in, g):
        return pl.BlockSpec((rows_in, group_width[g]), lambda s, f: (0, s))

    tall, row8, flat = whole((spots, LANES)), whole((8, spots)), whole((8, LANES))
    ins = [(st["member"], tall), (st["sp"], tall), (st["kl"], flat), (st["ent"], row8)]
    ins += [(a, by_slot(16, g)) for g in range(n_gr) for a in st["gs", g]]
    ins += [(a, by_slot(quarter, g)) for g in range(n_gr) for a in blocks_of(g)]
    ins += [(a, pl.BlockSpec((1, quarter, genes), lambda s, f: (s, 0, 0))) for a in blocks_of_target()]
    outs = [(sds((spots, slots * w), BF), pl.BlockSpec((spots, w), lambda s, f: (0, s))) for w in WIDTHS]
    outs += [(sds((8, spots), F32), row8)]
    *grads, terms = run(
        "grads", grads_body, ins, outs, grid=(slots,), scratch=[pltpu.VMEM((spots, LANES), F32)] * 2
    )

    row_blk = rows // 4

    def backward_body(fl, i, out):
        lg, tot, sm, terms = i[:4]
        efs, gs = i[4 : 4 + n_ch], i[4 + n_ch :]

        @pl.when(pl.program_id(0) == 0)
        def _():
            row = lax.broadcasted_iota(jnp.int32, (8, spots), 0)
            out[1][...] = jnp.where(row == 0, 0.0, terms[...])

        acc = -jnp.broadcast_to(sm[:, 0:1], (row_blk, spots))
        for ef, grad in zip(efs, gs):
            acc += lax.dot_general(ef[...], grad[...], (((1,), (1,)), ((), ())), preferred_element_type=F32)
        out[0][...] = acc
        prob = jnp.exp(lg[...].astype(F32)) * (1.0 / tot[0:1, :])
        out[1][0:1, :] += jnp.sum(prob * acc, axis=0, keepdims=True)

    def by_rows(width, size=row_blk):
        return pl.BlockSpec((size, width), lambda g, f: (g, 0))

    ins = [(logits, by_rows(spots)), (st["tot"], row8), (st["sm"], by_rows(LANES)), (terms, row8)]
    ins += [(st["e", c], by_rows(slots * WIDTHS[c])) for c in chunks]
    ins += [(a, whole(a.shape)) for a in grads]
    grad_probs, v = run(
        "backward", backward_body, ins,
        [(sds((rows, spots), F32), by_rows(spots)), (sds((8, spots), F32), row8)],
        grid=(rows // row_blk,),
    )

    v = v + over_core(v)
    v = v + over_x(v)
    v = (v + over_gene(v, 1)) + (over_gene(v, 2) + over_gene(v, 3))
    sums = sum_spot(v)[1, :5]

    def final_body(fl, i, out):
        prob = jnp.exp(i[0][...].astype(F32)) * (1.0 / i[1][0:1, :])
        out[0][...] = prob * (i[2][...] - i[3][0:1, :])

    last_blk = rows // 2
    blk = by_rows(spots, last_blk)
    (grad_logits,) = run(
        "final", final_body, [(logits, blk), (st["tot"], row8), (grad_probs, blk), (v, row8)],
        [(sds((rows, spots), F32), blk)], grid=(rows // last_blk,),
    )
    gene_term = sums[0] / (SLIDES * genes_all)
    spot_term = sums[1] / sums[4]
    divergence = sums[2]
    entropy = sums[3] / spots_all
    loss_terms = jnp.stack([divergence - gene_term - spot_term, gene_term, spot_term, divergence, entropy])
    return (loss_terms, grad_logits)


def solution(mesh):
    return jax.shard_map(
        functools.partial(per_device, dict(mesh.shape)),
        mesh=mesh,
        in_specs=(
            P(("cell", "gene"), "spot"),
            P(("cell", "spot"), "gene"),
            P("spot", "gene"),
            P("spot"),
            P("spot"),
            P(("cell", "gene")),
        ),
        out_specs=(P(), P(("cell", "gene"), "spot")),
        check_vma=False,
    )
```

```python
import functools
import jax
import jax.numpy as jnp
from jax import lax
from jax.experimental import pallas as pl
from jax.experimental.pallas import tpu as pltpu
from jax.sharding import PartitionSpec as P

SLIDES = 3
LANES = 128
ANY = pl.BlockSpec(memory_space=pl.ANY)
BF = jnp.bfloat16
F32 = jnp.float32
VMEM_BYTES = 30 * 1024 * 1024
WIDTHS = (128, 128, 128, 128)
GROUPS = ((0, 1), (2, 3))
ORDER = (
    "Y0 e0 Y1 w:ez1+ez2+ez3",
    "Y2 A0 a0 e3",
    "b0 A1 Y3 w:f20+f30+n0",
    "a1 A2 w:f21+f31+n1 a2",
    "S0 A3 w:f22+f32+n2 a3",
    "S1 w:s0 S2 w:s1",
    "F0 w:s2+f23+f33+n3 S3 f0",
    "P0 w:s3 F1 w:rx0",
    "f1 P1 Q0 m0",
    "R0 Q1 R1",
)


def sds(shape, dtype):
    return jax.ShapeDtypeStruct(shape, dtype)


def whole(shape):
    zeros = (0,) * len(shape)
    return pl.BlockSpec(shape, lambda *_: zeros)


def xor_pairs(size, step):
    return [(n, n ^ step) for n in range(size)]


class Chain:
    def __init__(self, flags):
        self.flags = flags
        self.token = jnp.zeros((8, LANES), F32)

    def run(self, name, body, ins=(), outs=(), after=(), through=(), grid=(1,), scratch=()):
        ins = [*ins, *((a, ANY) for a in after)]
        carried = (*through, self.token)
        n_in, n_out, n_thr = len(ins), len(outs), len(carried)

        def kernel(flags, *refs):
            in_refs = refs[:n_in]
            out_refs = refs[n_in + n_thr : n_in + n_thr + n_out]
            scratch_refs = refs[n_in + 2 * n_thr + n_out :]
            if body is not None:
                body(flags, in_refs, out_refs, *scratch_refs)

        results = pl.pallas_call(
            kernel,
            out_shape=[s for s, _ in outs] + [sds(a.shape, a.dtype) for a in carried],
            grid_spec=pltpu.PrefetchScalarGridSpec(
                num_scalar_prefetch=1,
                grid=grid,
                in_specs=[s for _, s in ins] + [ANY] * n_thr,
                out_specs=[s for _, s in outs] + [ANY] * n_thr,
                scratch_shapes=list(scratch),
            ),
            input_output_aliases={1 + n_in + j: n_out + j for j in range(n_thr)},
            compiler_params=pltpu.CompilerParams(vmem_limit_bytes=VMEM_BYTES),
            cost_estimate=pl.CostEstimate(flops=0, bytes_accessed=0, transcendentals=0),
            name=name,
        )(self.flags, *[a for a, _ in ins], *carried)
        self.token = results[-1]
        return results[:-1]


def copy_all(copies, sems):
    made = [(c, pltpu.make_async_copy(s, d, sems.at[n])) for n, (c, s, d) in enumerate(copies)]
    for act in ("start", "wait"):
        for cond, copy in made:
            if cond is None:
                getattr(copy, act)()
            else:
                pl.when(cond)(getattr(copy, act))


def column(row):
    return jnp.transpose(jnp.broadcast_to(row, (LANES, row.shape[1])))


def per_device(sizes, logits, expression, spatial, slide_ids, spot_mask, densities):
    spot_size = sizes["spot"]
    rows, spots = logits.shape
    genes = spatial.shape[1]
    spots_all = spots * spot_size
    genes_all = genes * sizes["gene"]
    slots = sizes["gene"]
    quarter = spots // sizes["cell"]
    half = rows // 2
    cell, spot, gene = (lax.axis_index(a) for a in ("cell", "spot", "gene"))
    home = (gene // 2 == spot).astype(jnp.int32)
    side = (gene % 2).astype(jnp.int32)
    chain = Chain(jnp.stack([home, side, cell, gene, spot]).astype(jnp.int32))
    run = chain.run
    offsets = [sum(WIDTHS[:n]) for n in range(len(WIDTHS))]
    chunks = range(len(WIDTHS))
    group_width = [sum(WIDTHS[c] for c in g) for g in GROUPS]

    def over_core(v):
        return lax.ppermute(v, "cell", xor_pairs(4, 1))

    def over_x(v):
        return lax.ppermute(v, "cell", xor_pairs(4, 2))

    def over_gene(v, step):
        return lax.ppermute(v, "gene", xor_pairs(4, step))

    def over_spot(v, step=1):
        return lax.ppermute(v, "spot", xor_pairs(spot_size, step))

    def sum_spot(v):
        step = 1
        while step < spot_size:
            v = v + over_spot(v, step)
            step *= 2
        return v

    ids_row, mask_row = slide_ids.reshape(1, spots), spot_mask.reshape(1, spots)
    dens_row = densities.reshape(1, rows)

    expr = expression.reshape(2, half * 2, genes) if spot_size == 2 else None
    st, sent = {}, {}

    def start_swap(c):
        w, o = WIDTHS[c], offsets[c] // WIDTHS[c]

        def body(fl, i, out):
            out[0][...] = i[0][...]

        (v,) = run(
            f"swap{c}", body, [(expr, pl.BlockSpec((1, rows, w), lambda g, f: (g, 0, o)))],
            [(sds((2, rows, w), BF), pl.BlockSpec((1, rows, w), lambda g, f: (g, 0, 0)))], grid=(2,),
        )
        sent[f"y{c}"] = over_spot(v)

    def start_along(c):
        w, o = WIDTHS[c], offsets[c] // WIDTHS[c]
        blk, one = (1, half, w), (half, w)

        def body(fl, i, out):
            @pl.when(fl[0] == 1)
            def _():
                out[0][...] = i[0][0]
                out[1][...] = i[1][0]
                out[2][0] = i[2][0]
                out[2][1] = i[3][0]

            @pl.when(fl[0] == 0)
            def _():
                out[0][...] = i[4][0]
                out[1][...] = i[5][0]
                out[2][0] = i[6][0]
                out[2][1] = i[7][0]

        def at(same, part, col):
            return pl.BlockSpec(blk, lambda g, f: (f[1] if same else 1 - f[1], part, col))

        y = sent[f"y{c}"]
        ins = [(y, at(True, 0, 0)), (y, at(False, 0, 0)), (expr, at(False, 0, o)), (expr, at(False, 1, o))]
        ins += [(expr, at(True, 1, o)), (expr, at(False, 1, o)), (y, at(False, 0, 0)), (y, at(False, 1, 0))]
        outs = [(sds(one, BF), whole(one))] * 2 + [(sds((2, half, w), BF), whole((2, half, w)))]
        st["along", c] = run(f"along{c}", body, ins, outs)

    def along_send(c):
        a, b, n = run(f"alongsend{c}", None, through=st["along", c])
        sent[f"f2{c}"], sent[f"f3{c}"], sent[f"n{c}"] = over_gene(a, 2), over_gene(b, 3), over_gene(n, 1)

    def start_back(c):
        w = WIDTHS[c]

        def body(fl, i, out):
            out[0][0] = i[0][...]
            out[0][1] = i[1][...]

        one = whole((half, w))
        (st["f", c],) = run(
            f"back{c}", body, [(sent[f"f2{c}"], one), (sent[f"f3{c}"], one)], [(sds((2, half, w), BF), whole((2, half, w)))]
        )
        sent[f"s{c}"] = over_spot(st["f", c])

    def wait_for(name):
        run("wait", None, after=[sent[n] for n in name.split("+")])

    def members_of(_):
        def body(fl, i, out):
            ids, valid = column(i[0][...].astype(F32)), column(i[1][...].astype(F32))
            lane = lax.broadcasted_iota(jnp.int32, (quarter, LANES), 1)
            inside = (lane < SLIDES) & (lane.astype(F32) == ids) & (valid == 1.0)
            out[0][...] = jnp.where(inside, 1.0, jnp.where(lane == SLIDES, valid, 0.0))

        row, tall = pl.BlockSpec((1, quarter), lambda g, f: (0, f[2])), whole((quarter, LANES))
        (st["member"],) = run("member", body, [(ids_row, row), (mask_row, row)], [(sds((quarter, LANES), F32), tall)])

    def totals(n):
        sp = whole((8, spots))
        if n == 0:

            def body(fl, i, out):
                out[0][...] = jnp.zeros((8, spots), F32)
                out[0][0:1, :] = jnp.sum(jnp.exp(i[0][...].astype(F32)), axis=0, keepdims=True)
                out[0][1:2, :] = jnp.broadcast_to(jnp.sum(i[1][...]), (1, spots))

            ins = [(logits, whole(logits.shape)), (dens_row, whole(dens_row.shape))]
            (v,) = run("totals", body, ins, [(sds((8, spots), F32), sp)])
            st["tot"] = lax.psum(v, "cell")
            for s in (1, 2, 3):
                sent[f"ez{s}"] = over_gene(st["tot"], s)
        else:
            blk = 2 * LANES

            def body(fl, i, out):
                tot = (i[1][...] + i[2][...]) + (i[3][...] + i[4][...])
                out[3][...] = tot
                inv = 1.0 / tot[0:1, :]
                log_tot = jnp.log(tot[0:1, :])
                vals = i[0][...].astype(F32)
                prob = jnp.exp(vals) * inv
                prob_t = jnp.transpose(prob.astype(BF))
                for q in range(sizes["cell"]):
                    at = pl.multiple_of((fl[2] ^ q) * quarter, quarter)
                    out[0][pl.ds(at, quarter), :] = prob_t[q * quarter : (q + 1) * quarter]
                folded = sum(prob[:, n : n + LANES] for n in range(0, spots, LANES))
                row_sums = jnp.sum(jnp.transpose(folded), axis=0, keepdims=True)
                out[1][...] = jnp.broadcast_to(row_sums, (8, blk))

                @pl.when(pl.program_id(0) == 0)
                def _():
                    out[2][...] = jnp.zeros((8, spots), F32)

                out[2][0:1, :] -= jnp.sum(prob * (vals - log_tot), axis=0, keepdims=True)

            parts = [st["tot"]] + [sent[f"ez{s}"] for s in (1, 2, 3)]
            pt, mass, ent, st["tot"] = run(
                "prob", body,
                [(logits, pl.BlockSpec((blk, spots), lambda g, f: (g, 0)))] + [(a, sp) for a in parts],
                [
                    (sds((spots, rows), BF), pl.BlockSpec((spots, blk), lambda g, f: (0, g))),
                    (sds((8, rows), F32), pl.BlockSpec((8, blk), lambda g, f: (0, g))),
                    (sds((8, spots), F32), sp),
                    (sds((8, spots), F32), sp),
                ],
                grid=(rows // blk,),
            )
            st["pt"], st["ent"] = pt, ent
            st["mass"] = mass if spot_size == 2 else sum_spot(mass)
            if spot_size == 2:
                sent["my"] = over_spot(mass)

    def shares(_):
        masses = [st["mass"]] + ([sent["my"]] if spot_size == 2 else [])

        def body(fl, i, out):
            mass = i[2][0:1, :]
            for extra in i[3:]:
                mass = mass + extra[0:1, :]
            share = i[0][...] / i[1][1:2, 0:1]
            out[0][...] = column(share / mass)
            kl = jnp.sum(share * (jnp.log(share) - jnp.log(mass / spots_all)))
            out[1][...] = jnp.broadcast_to(kl, (8, LANES))

        st["sm"], st["kl"] = run(
            "shares", body,
            [(dens_row, whole(dens_row.shape)), (st["tot"], whole((8, spots)))]
            + [(m, whole((8, rows))) for m in masses],
            [(sds((rows, LANES), F32), whole((rows, LANES))), (sds((8, LANES), F32), whole((8, LANES)))],
        )

    def forward(g):
        members, wide_all = GROUPS[g], group_width[g] * slots
        shape = (2, quarter, wide_all)
        outs = [(sds((rows, slots * WIDTHS[c]), BF), whole((rows, slots * WIDTHS[c]))) for c in members]
        outs += [(sds(shape, F32), whole(shape))] * 2

        def product(pt, efs, keep, send):
            done = 0
            for c, ef in zip(members, efs):
                w = WIDTHS[c]
                acc = jnp.dot(pt[...], ef[...], preferred_element_type=F32)
                for q, ref in enumerate((keep, send, keep, send)):
                    rows_q = acc[q * quarter : (q + 1) * quarter]
                    for s in range(slots):
                        base = s * group_width[g] + done
                        ref[q // 2, :, base : base + w] = rows_q[:, s * w : (s + 1) * w]
                done += w

        if spot_size == 2:

            def body(fl, i, out, sems):
                pt, e = i[:2]
                at_home, away = fl[0] == 1, fl[0] == 0
                top, low = pl.ds(0, half), pl.ds(half, half)
                copies = []
                for m, c in enumerate(members):
                    w, ef = WIDTHS[c], out[m]
                    y, n, f, s = i[2 + 4 * m : 6 + 4 * m]
                    copies += [
                        (at_home, e.at[fl[1], :, pl.ds(offsets[c], w)], ef.at[:, pl.ds(0, w)]),
                        (away, y.at[fl[1]], ef.at[:, pl.ds(0, w)]),
                        (None, n.at[0], ef.at[top, pl.ds(w, w)]),
                        (None, n.at[1], ef.at[low, pl.ds(w, w)]),
                    ]
                    for part in (0, 1):
                        cols = pl.ds((2 + part) * w, w)
                        copies += [
                            (at_home, f.at[part], ef.at[low, cols]),
                            (at_home, s.at[part], ef.at[top, cols]),
                            (away, f.at[part], ef.at[top, cols]),
                            (away, s.at[part], ef.at[low, cols]),
                        ]
                copy_all(copies, sems)
                product(pt, out[: len(members)], *out[len(members) :])

            ins = [(st["pt"], whole((spots, rows))), (expr, ANY)]
            ins += [
                (a, ANY)
                for c in members
                for a in (sent[f"y{c}"], sent[f"n{c}"], st["f", c], sent[f"s{c}"])
            ]
            scratch = [pltpu.SemaphoreType.DMA((12 * len(members),))]
        else:

            def body(fl, i, out):
                for m, c in enumerate(members):
                    w = WIDTHS[c]
                    for s in range(slots):
                        out[m][:, s * w : (s + 1) * w] = i[1 + m * slots + s][...]
                product(i[0], out[: len(members)], *out[len(members) :])

            def at_chunk(c):
                return pl.BlockSpec((rows, WIDTHS[c]), lambda *_: (0, offsets[c] // WIDTHS[c]))

            ins = [(st["pt"], whole((spots, rows)))] + [(a, at_chunk(c)) for c in members for a in st["pieces"]]
            scratch = []
        *efs, keep, send = run(f"forward{g}", body, ins, outs, scratch=scratch)
        for c, ef in zip(members, efs):
            st["e", c] = ef
        st["r", g], st["send", g] = keep, send

    def forward_send(g):
        (send,) = run(f"send{g}", None, through=[st["send", g]])
        sent[f"rc{g}"] = over_core(send)

    def reduce_core(g):
        wide = slots * group_width[g]
        shape, one = (2, quarter, wide), (quarter, wide)

        def body(fl, i, out):
            out[0][...] = i[0][0] + i[1][0]
            out[1][...] = i[0][1] + i[1][1]

        ins = [(st["r", g], whole(shape)), (sent[f"rc{g}"], whole(shape))]
        st["r", g], b = run(f"core{g}", body, ins, [(sds(one, F32), whole(one))] * 2)
        sent[f"rx{g}"] = over_x(b)

    def reduce_x(g):
        w = group_width[g]
        one, part = (quarter, slots * w), (quarter, w)

        def body(fl, i, out):
            for s in range(slots):
                at = slice(s * w, (s + 1) * w)
                out[s][...] = i[0][:, at] + i[1][:, at]

        ins = [(st["r", g], whole(one)), (sent[f"rx{g}"], whole(one))]
        st["r", g], *parts = run(f"x{g}", body, ins, [(sds(part, F32), whole(part))] * slots)
        for s in (1, 2, 3):
            sent[f"rz{s}{g}"] = over_gene(parts[s - 1], s)

    def reduce_gene(g):
        part = (quarter, group_width[g])

        def body(fl, i, out):
            out[0][...] = (i[0][...] + i[1][...]) + (i[2][...] + i[3][...])

        parts = [st["r", g]] + [sent[f"rz{s}{g}"] for s in (1, 2, 3)]
        (v,) = run(f"gene{g}", body, [(a, whole(part)) for a in parts], [(sds(part, F32), whole(part))])
        st["r", g] = v

    steps = {
        "Y": start_swap, "A": start_along, "a": along_send, "S": start_back,
        "e": totals, "m": shares, "F": forward, "f": forward_send, "b": members_of, "P": reduce_core, "Q": reduce_x, "R": reduce_gene,
    }
    if spot_size != 2:
        full = lax.all_gather(expression, "spot", axis=0, tiled=True).reshape(slots, rows, genes)
        pieces = [lax.dynamic_index_in_dim(full, gene ^ s, 0, False) for s in range(slots)]
        st["pieces"] = [pieces[0]] + [over_gene(pieces[s], s) for s in (1, 2, 3)]
    for word in " ".join(ORDER).split():
        if word[:2] == "w:":
            if spot_size == 2 or word == "w:ez1+ez2+ez3":
                wait_for(word[2:])
        elif spot_size == 2 or word[0] not in "YAaS":
            steps[word[0]](int(word[1]))

    n_ch, n_gr = len(WIDTHS), len(GROUPS)
    starts = [offsets[g[0]] for g in GROUPS]
    preds = [(st["r", g], whole((quarter, group_width[g]))) for g in range(n_gr)]
    mine = (spatial, pl.BlockSpec((quarter, genes), lambda g, f: (f[2], 0)))
    memb = (st["member"], whole((quarter, LANES)))
    gene_spec, spot_spec = whole((16, genes)), whole((8, quarter))

    def stats_body(fl, i, out):
        memb = i[0]
        cols = [jnp.broadcast_to(memb[:, k : k + 1], (quarter, LANES)) for k in range(SLIDES)]
        valid = jnp.sum(memb[:, SLIDES : SLIDES + 1])
        out[0][...] = jnp.broadcast_to(valid, (16, genes))
        totals = [jnp.zeros((quarter, LANES), F32) for _ in range(3)]
        for g in range(n_gr):
            for o in range(0, group_width[g], LANES):
                at = slice(starts[g] + o, starts[g] + o + LANES)
                pr, ta = i[2 + g][:, o : o + LANES], i[1][:, at].astype(F32)
                for j, v in enumerate((pr * ta, pr * pr, ta * ta)):
                    totals[j] += v
                    for k in range(SLIDES):
                        n = 3 * j + k
                        out[0][n : n + 1, at] = jnp.sum(cols[k] * v, axis=0, keepdims=True)
        out[1][...] = jnp.zeros((8, quarter), F32)
        for j in range(3):
            out[1][j : j + 1, :] = jnp.sum(jnp.transpose(totals[j]), axis=0, keepdims=True)

    gene_sums, spot_sums = run(
        "stats", stats_body, [memb, mine, *preds],
        [(sds((16, genes), F32), gene_spec), (sds((8, quarter), F32), spot_spec)],
    )
    spot_parts = [spot_sums] + [over_gene(spot_sums, s) for s in (1, 2, 3)]
    gene_sums = gene_sums + over_core(gene_sums)
    gene_sums = gene_sums + over_x(gene_sums)
    gene_parts = [gene_sums, over_spot(gene_sums)] if spot_size == 2 else [sum_spot(gene_sums)]

    def grads_body(fl, i, out):
        memb, ta_ref, kl, ent = i[:4]
        i = i[4:]
        spot_in, gene_in, preds_in = i[:4], i[4 : 4 + len(gene_parts)], i[4 + len(gene_parts) :]
        scale = -1.0 / (SLIDES * genes_all)
        sums = sum(ref[...] for ref in gene_in)
        num, psq, tsq = sums[0:3], sums[3:6], sums[6:9]
        p_floor, t_floor = jnp.maximum(psq, 1.0), jnp.maximum(tsq, 1.0)
        root = jnp.sqrt(p_floor * t_floor)
        cosine = num / root
        w_t = scale / root
        w_p = jnp.where(psq > 1.0, -scale * cosine / p_floor, 0.0)
        valid_total = jnp.maximum(sums[9, 0], 1.0)
        spot_all = (spot_in[0][...] + spot_in[1][...]) + (spot_in[2][...] + spot_in[3][...])
        s_num, s_p, s_t = [column(spot_all[n : n + 1, :]) for n in range(3)]
        s_p, s_t = s_p + 1e-06, s_t + 1e-06
        root = jnp.sqrt(s_p * s_t)
        cos_spot = s_num / root
        valid = jnp.broadcast_to(memb[:, SLIDES : SLIDES + 1], (quarter, LANES))
        coef = -valid / valid_total
        coef_t, coef_p = coef / root, -coef * cos_spot / s_p
        first = [(fl[n] == 0).astype(F32) for n in (2, 4, 3)]
        terms = [
            jnp.sum(cosine) * first[0] * first[1],
            jnp.sum((valid * cos_spot)[:, 0:1]) * first[2],
            kl[0, 0] * first[1],
            jnp.sum(ent[0:1, :]),
            valid_total * first[0] * first[1] * first[2],
        ]
        lane = lax.broadcasted_iota(jnp.int32, (8, spots), 1)
        value = jnp.zeros((8, spots), F32)
        for n, term in enumerate(terms):
            value = jnp.where(lane == n, term, value)
        out[1][...] = value
        cols = [jnp.broadcast_to(memb[:, k : k + 1], (quarter, LANES)) for k in range(SLIDES)]
        for g in range(n_gr):
            for o in range(0, group_width[g], LANES):
                at = slice(starts[g] + o, starts[g] + o + LANES)
                f_t, f_p = coef_t, coef_p
                for k in range(SLIDES):
                    f_t = f_t + cols[k] * w_t[k : k + 1, at]
                    f_p = f_p + cols[k] * w_p[k : k + 1, at]
                out[0][:, at] = (f_t * ta_ref[:, at].astype(F32) + f_p * preds_in[g][:, o : o + LANES]).astype(BF)

    row8, flat = whole((8, spots)), whole((8, LANES))
    ins = [memb, mine, (st["kl"], flat), (st["ent"], row8)]
    ins += [(a, spot_spec) for a in spot_parts] + [(a, gene_spec) for a in gene_parts] + preds
    grad, terms = run(
        "grads", grads_body, ins,
        [(sds((quarter, genes), BF), whole((quarter, genes))), (sds((8, spots), F32), row8)],
    )
    grad = jnp.stack([grad] + [over_gene(grad, s) for s in (1, 2, 3)])
    grad_x = over_x(grad)
    grads = [grad, over_core(grad), grad_x, over_core(grad_x)]

    row_blk = rows // 4

    def backward_body(fl, i, out, held, sems):
        lg, tot, sm, terms = i[:4]
        efs, gs = i[4 : 4 + n_ch], i[4 + n_ch :]

        @pl.when(pl.program_id(0) == 0)
        def _():
            row = lax.broadcasted_iota(jnp.int32, (8, spots), 0)
            out[1][...] = jnp.where(row == 0, 0.0, terms[...])
            copies = []
            for b, ref in enumerate(gs):
                at = pl.multiple_of((fl[2] ^ b) * quarter, quarter)
                copies.append((None, ref, held.at[:, pl.ds(at, quarter), :]))
            copy_all(copies, sems)

        acc = -jnp.broadcast_to(sm[:, 0:1], (row_blk, spots))
        for s in range(slots):
            left = jnp.concatenate([ef[:, s * w : (s + 1) * w] for w, ef in zip(WIDTHS, efs)], axis=1)
            acc += lax.dot_general(left, held[s], (((1,), (1,)), ((), ())), preferred_element_type=F32)
        out[0][...] = acc
        prob = jnp.exp(lg[...].astype(F32)) * (1.0 / tot[0:1, :])
        out[1][0:1, :] += jnp.sum(prob * acc, axis=0, keepdims=True)

    def by_rows(width, size=row_blk):
        return pl.BlockSpec((size, width), lambda g, f: (g, 0))

    ins = [(logits, by_rows(spots)), (st["tot"], row8), (st["sm"], by_rows(LANES)), (terms, row8)]
    ins += [(st["e", c], by_rows(slots * WIDTHS[c])) for c in chunks]
    ins += [(a, ANY) for a in grads]
    grad_probs, v = run(
        "backward", backward_body, ins,
        [(sds((rows, spots), F32), by_rows(spots)), (sds((8, spots), F32), row8)],
        grid=(rows // row_blk,),
        scratch=[pltpu.VMEM((slots, spots, genes), BF), pltpu.SemaphoreType.DMA((len(grads),))],
    )

    v = v + over_core(v)
    v = v + over_x(v)
    v = (v + over_gene(v, 1)) + (over_gene(v, 2) + over_gene(v, 3))
    sums = sum_spot(v)[1, :5]

    def final_body(fl, i, out):
        prob = jnp.exp(i[0][...].astype(F32)) * (1.0 / i[1][0:1, :])
        out[0][...] = prob * (i[2][...] - i[3][0:1, :])

    last_blk = rows // 2
    blk = by_rows(spots, last_blk)
    (grad_logits,) = run(
        "final", final_body, [(logits, blk), (st["tot"], row8), (grad_probs, blk), (v, row8)],
        [(sds((rows, spots), F32), blk)], grid=(rows // last_blk,),
    )
    gene_term = sums[0] / (SLIDES * genes_all)
    spot_term = sums[1] / sums[4]
    divergence = sums[2]
    entropy = sums[3] / spots_all
    loss_terms = jnp.stack([divergence - gene_term - spot_term, gene_term, spot_term, divergence, entropy])
    return (loss_terms, grad_logits)


def solution(mesh):
    return jax.shard_map(
        functools.partial(per_device, dict(mesh.shape)),
        mesh=mesh,
        in_specs=(
            P(("cell", "gene"), "spot"),
            P(("cell", "spot"), "gene"),
            P("spot", "gene"),
            P("spot"),
            P("spot"),
            P(("cell", "gene")),
        ),
        out_specs=(P(), P(("cell", "gene"), "spot")),
        check_vma=False,
    )
```

```python
import functools
import jax
import jax.numpy as jnp
from jax import lax
from jax.experimental import pallas as pl
from jax.experimental.pallas import tpu as pltpu
from jax.sharding import PartitionSpec as P

SLIDES = 3
LANES = 128
ANY = pl.BlockSpec(memory_space=pl.ANY)
BF = jnp.bfloat16
F32 = jnp.float32
VMEM_BYTES = 20 * 1024 * 1024
BACK_COST = 6 * 10**9
WIDTHS = (128, 128, 128, 128)
GROUPS = ((0, 1), (2, 3))
ORDER = (
    "Y0 e0 Y1 w:ez1+ez2+ez3",
    "Y2 A0 a0 e3",
    "b0 A1 Y3 w:f20+f30+n0",
    "a1 A2 w:f21+f31+n1 a2",
    "S0 A3 w:f22+f32+n2 a3",
    "S1 w:s0 S2 w:s1",
    "F0 w:f23+f33+n3 S3 w:s2",
    "f0 P0 F1 w:rx0",
    "G1 P1 Q0 m0",
    "R0 Q1 R1",
)


def sds(shape, dtype):
    return jax.ShapeDtypeStruct(shape, dtype)


def whole(shape):
    zeros = (0,) * len(shape)
    return pl.BlockSpec(shape, lambda *_: zeros)


def xor_pairs(size, step):
    return [(n, n ^ step) for n in range(size)]


class Chain:
    def __init__(self, flags):
        self.flags = flags
        self.token = jnp.zeros((8, LANES), F32)

    def run(self, name, body, ins=(), outs=(), after=(), through=(), grid=(1,), scratch=(), cost=0, vmem=VMEM_BYTES):
        ins = [*ins, *((a, ANY) for a in after)]
        carried = (*through, self.token)
        n_in, n_out, n_thr = len(ins), len(outs), len(carried)

        def kernel(flags, *refs):
            in_refs = refs[:n_in]
            out_refs = refs[n_in + n_thr : n_in + 2 * n_thr + n_out - 1]
            scratch_refs = refs[n_in + 2 * n_thr + n_out :]
            if body is not None:
                body(flags, in_refs, out_refs, *scratch_refs)

        results = pl.pallas_call(
            kernel,
            out_shape=[s for s, _ in outs] + [sds(a.shape, a.dtype) for a in carried],
            grid_spec=pltpu.PrefetchScalarGridSpec(
                num_scalar_prefetch=1,
                grid=grid,
                in_specs=[s for _, s in ins] + [ANY] * n_thr,
                out_specs=[s for _, s in outs] + [ANY] * n_thr,
                scratch_shapes=list(scratch),
            ),
            input_output_aliases={1 + n_in + j: n_out + j for j in range(n_thr)},
            compiler_params=pltpu.CompilerParams(vmem_limit_bytes=vmem),
            cost_estimate=pl.CostEstimate(flops=cost, bytes_accessed=0, transcendentals=0),
            name=name,
        )(self.flags, *[a for a, _ in ins], *carried)
        self.token = results[-1]
        return results[:-1]


def copy_all(copies, sems):
    made = [(c, pltpu.make_async_copy(s, d, sems.at[n])) for n, (c, s, d) in enumerate(copies)]
    for act in ("start", "wait"):
        for cond, copy in made:
            if cond is None:
                getattr(copy, act)()
            else:
                pl.when(cond)(getattr(copy, act))


def column(row):
    return jnp.transpose(jnp.broadcast_to(row, (LANES, row.shape[1])))


def per_device(sizes, logits, expression, spatial, slide_ids, spot_mask, densities):
    spot_size = sizes["spot"]
    rows, spots = logits.shape
    genes = spatial.shape[1]
    spots_all = spots * spot_size
    genes_all = genes * sizes["gene"]
    slots = sizes["gene"]
    quarter = spots // sizes["cell"]
    half = rows // 2
    cell, spot, gene = (lax.axis_index(a) for a in ("cell", "spot", "gene"))
    home = (gene // 2 == spot).astype(jnp.int32)
    side = (gene % 2).astype(jnp.int32)
    chain = Chain(jnp.stack([home, side, cell, gene, spot]).astype(jnp.int32))
    run = chain.run
    offsets = [sum(WIDTHS[:n]) for n in range(len(WIDTHS))]
    chunks = range(len(WIDTHS))
    group_width = [sum(WIDTHS[c] for c in g) for g in GROUPS]

    def over_core(v):
        return lax.ppermute(v, "cell", xor_pairs(4, 1))

    def over_x(v):
        return lax.ppermute(v, "cell", xor_pairs(4, 2))

    def over_gene(v, step):
        return lax.ppermute(v, "gene", xor_pairs(4, step))

    def over_spot(v, step=1):
        return lax.ppermute(v, "spot", xor_pairs(spot_size, step))

    def sum_spot(v):
        step = 1
        while step < spot_size:
            v = v + over_spot(v, step)
            step *= 2
        return v

    ids_row, mask_row = slide_ids.reshape(1, spots), spot_mask.reshape(1, spots)
    dens_row = densities.reshape(1, rows)

    expr = expression.reshape(2, half * 2, genes) if spot_size == 2 else None
    st, sent = {}, {}

    def start_swap(c):
        w = WIDTHS[c]

        def body(fl, i, out, sems):
            copy_all([(None, i[0].at[p, :, pl.ds(offsets[c], w)], out[0].at[p]) for p in range(2)], sems)

        shape = (2, rows, w)
        (v,) = run(
            f"swap{c}", body, [(expr, pl.BlockSpec(memory_space=pltpu.HBM))], [(sds(shape, BF), whole(shape))],
            scratch=[pltpu.SemaphoreType.DMA((2,))],
        )
        sent[f"y{c}"] = over_spot(v)

    def start_along(c):
        w, o = WIDTHS[c], offsets[c] // WIDTHS[c]
        blk, one = (1, half, w), (half, w)

        def body(fl, i, out):
            @pl.when(fl[0] == 1)
            def _():
                out[0][...] = i[0][0]
                out[1][...] = i[1][0]
                out[2][0] = i[2][0]
                out[2][1] = i[3][0]

            @pl.when(fl[0] == 0)
            def _():
                out[0][...] = i[4][0]
                out[1][...] = i[5][0]
                out[2][0] = i[6][0]
                out[2][1] = i[7][0]

        def at(same, part, col):
            return pl.BlockSpec(blk, lambda g, f: (f[1] if same else 1 - f[1], part, col))

        y = sent[f"y{c}"]
        ins = [(y, at(True, 0, 0)), (y, at(False, 0, 0)), (expr, at(False, 0, o)), (expr, at(False, 1, o))]
        ins += [(expr, at(True, 1, o)), (expr, at(False, 1, o)), (y, at(False, 0, 0)), (y, at(False, 1, 0))]
        outs = [(sds(one, BF), whole(one))] * 2 + [(sds((2, half, w), BF), whole((2, half, w)))]
        st["along", c] = run(f"along{c}", body, ins, outs)

    def along_send(c):
        a, b, n = run(f"alongsend{c}", None, through=st["along", c])
        sent[f"f2{c}"], sent[f"f3{c}"], sent[f"n{c}"] = over_gene(a, 2), over_gene(b, 3), over_gene(n, 1)

    def start_back(c):
        w = WIDTHS[c]

        def body(fl, i, out):
            out[0][0] = i[0][...]
            out[0][1] = i[1][...]

        one = whole((half, w))
        (st["f", c],) = run(
            f"back{c}", body, [(sent[f"f2{c}"], one), (sent[f"f3{c}"], one)], [(sds((2, half, w), BF), whole((2, half, w)))],
            cost=BACK_COST if c == len(WIDTHS) - 1 else 0,
        )
        sent[f"s{c}"] = over_spot(st["f", c])

    def wait_for(name):
        run("wait", None, after=[sent[n] for n in name.split("+")])

    def members_of(_):
        def body(fl, i, out):
            ids, valid = column(i[0][...].astype(F32)), column(i[1][...].astype(F32))
            lane = lax.broadcasted_iota(jnp.int32, (quarter, LANES), 1)
            inside = (lane < SLIDES) & (lane.astype(F32) == ids) & (valid == 1.0)
            out[0][...] = jnp.where(inside, 1.0, jnp.where(lane == SLIDES, valid, 0.0))

        row, tall = pl.BlockSpec((1, quarter), lambda g, f: (0, f[2])), whole((quarter, LANES))
        (st["member"],) = run("member", body, [(ids_row, row), (mask_row, row)], [(sds((quarter, LANES), F32), tall)])

    def totals(n):
        sp = whole((8, spots))
        if n == 0:

            def body(fl, i, out):
                out[0][...] = jnp.zeros((8, spots), F32)
                out[0][0:1, :] = jnp.sum(jnp.exp(i[0][...].astype(F32)), axis=0, keepdims=True)
                out[0][1:2, :] = jnp.broadcast_to(jnp.sum(i[1][...]), (1, spots))

            ins = [(logits, whole(logits.shape)), (dens_row, whole(dens_row.shape))]
            (v,) = run("totals", body, ins, [(sds((8, spots), F32), sp)])
            st["tot"] = lax.psum(v, "cell")
            for s in (1, 2, 3):
                sent[f"ez{s}"] = over_gene(st["tot"], s)
        else:
            blk = 2 * LANES

            def body(fl, i, out):
                tot = (i[1][...] + i[2][...]) + (i[3][...] + i[4][...])
                out[3][...] = tot
                inv = 1.0 / tot[0:1, :]
                log_tot = jnp.log(tot[0:1, :])
                vals = i[0][...].astype(F32)
                prob = jnp.exp(vals) * inv
                prob_t = jnp.transpose(prob.astype(BF))
                for q in range(sizes["cell"]):
                    at = pl.multiple_of((fl[2] ^ q) * quarter, quarter)
                    out[0][pl.ds(at, quarter), :] = prob_t[q * quarter : (q + 1) * quarter]
                folded = sum(prob[:, n : n + LANES] for n in range(0, spots, LANES))
                row_sums = jnp.sum(jnp.transpose(folded), axis=0, keepdims=True)
                out[1][...] = jnp.broadcast_to(row_sums, (8, blk))

                @pl.when(pl.program_id(0) == 0)
                def _():
                    out[2][...] = jnp.zeros((8, spots), F32)

                out[2][0:1, :] -= jnp.sum(prob * (vals - log_tot), axis=0, keepdims=True)

            parts = [st["tot"]] + [sent[f"ez{s}"] for s in (1, 2, 3)]
            pt, mass, ent, st["tot"] = run(
                "prob", body,
                [(logits, pl.BlockSpec((blk, spots), lambda g, f: (g, 0)))] + [(a, sp) for a in parts],
                [
                    (sds((spots, rows), BF), pl.BlockSpec((spots, blk), lambda g, f: (0, g))),
                    (sds((8, rows), F32), pl.BlockSpec((8, blk), lambda g, f: (0, g))),
                    (sds((8, spots), F32), sp),
                    (sds((8, spots), F32), sp),
                ],
                grid=(rows // blk,),
            )
            st["pt"], st["ent"] = pt, ent
            st["mass"] = mass if spot_size == 2 else sum_spot(mass)
            if spot_size == 2:
                sent["my"] = over_spot(mass)

    def shares(_):
        masses = [st["mass"]] + ([sent["my"]] if spot_size == 2 else [])

        def body(fl, i, out):
            mass = i[2][0:1, :]
            for extra in i[3:]:
                mass = mass + extra[0:1, :]
            share = i[0][...] / i[1][1:2, 0:1]
            out[0][...] = column(share / mass)
            kl = jnp.sum(share * (jnp.log(share) - jnp.log(mass / spots_all)))
            out[1][...] = jnp.broadcast_to(kl, (8, LANES))

        st["sm"], st["kl"] = run(
            "shares", body,
            [(dens_row, whole(dens_row.shape)), (st["tot"], whole((8, spots)))]
            + [(m, whole((8, rows))) for m in masses],
            [(sds((rows, LANES), F32), whole((rows, LANES))), (sds((8, LANES), F32), whole((8, LANES)))],
        )

    def forward(g):
        members, wide_all = GROUPS[g], group_width[g] * slots
        shape = (2, quarter, wide_all)
        outs = [(sds((rows, slots * WIDTHS[c]), BF), whole((rows, slots * WIDTHS[c]))) for c in members]
        outs += [(sds(shape, F32), whole(shape))] * 2

        late = members[-1] if spot_size == 2 and g == len(GROUPS) - 1 else None

        def product(pt, efs, keep, send, direct=None):
            done = 0
            for c, ef in zip(members, efs):
                w = WIDTHS[c]
                if c == late:
                    near = jnp.dot(pt[...], ef[:, : 2 * w], preferred_element_type=F32)
                    at = pl.ds(pl.multiple_of(direct, LANES), half)
                    far = jnp.dot(pt[:, at], ef[at, 2 * w :], preferred_element_type=F32)
                    acc = jnp.concatenate([near, far], axis=1)
                else:
                    acc = jnp.dot(pt[...], ef[...], preferred_element_type=F32)
                for q, ref in enumerate((keep, send, keep, send)):
                    rows_q = acc[q * quarter : (q + 1) * quarter]
                    for s in range(slots):
                        base = s * group_width[g] + done
                        ref[q // 2, :, base : base + w] = rows_q[:, s * w : (s + 1) * w]
                done += w

        if spot_size == 2:

            def body(fl, i, out, sems):
                pt, e = i[:2]
                at_home, away = fl[0] == 1, fl[0] == 0
                top, low = pl.ds(0, half), pl.ds(half, half)
                copies = []
                for m, c in enumerate(members):
                    w, ef = WIDTHS[c], out[m]
                    y, n, f = i[2 + 4 * m : 5 + 4 * m]
                    copies += [
                        (at_home, e.at[fl[1], :, pl.ds(offsets[c], w)], ef.at[:, pl.ds(0, w)]),
                        (away, y.at[fl[1]], ef.at[:, pl.ds(0, w)]),
                        (None, n.at[0], ef.at[top, pl.ds(w, w)]),
                        (None, n.at[1], ef.at[low, pl.ds(w, w)]),
                    ]
                    for part in (0, 1):
                        cols = pl.ds((2 + part) * w, w)
                        copies += [(at_home, f.at[part], ef.at[low, cols]), (away, f.at[part], ef.at[top, cols])]
                        if c != late:
                            s = i[5 + 4 * m]
                            copies += [(at_home, s.at[part], ef.at[top, cols]), (away, s.at[part], ef.at[low, cols])]
                copy_all(copies, sems)
                product(pt, out[: len(members)], *out[len(members) :], direct=fl[0] * half)

            ins = [(st["pt"], whole((spots, rows))), (expr, ANY)]
            ins += [
                (a, ANY)
                for c in members
                for a in (sent[f"y{c}"], sent[f"n{c}"], st["f", c], *([] if c == late else [sent[f"s{c}"]]))
            ]
            scratch = [pltpu.SemaphoreType.DMA((12 * len(members),))]
        else:

            def body(fl, i, out):
                for m, c in enumerate(members):
                    w = WIDTHS[c]
                    for s in range(slots):
                        out[m][:, s * w : (s + 1) * w] = i[1 + m * slots + s][...]
                product(i[0], out[: len(members)], *out[len(members) :])

            def at_chunk(c):
                return pl.BlockSpec((rows, WIDTHS[c]), lambda *_: (0, offsets[c] // WIDTHS[c]))

            ins = [(st["pt"], whole((spots, rows)))] + [(a, at_chunk(c)) for c in members for a in st["pieces"]]
            scratch = []
        *efs, keep, send = run(f"forward{g}", body, ins, outs, scratch=scratch)
        for c, ef in zip(members, efs):
            st["e", c] = ef
        st["r", g], st["send", g] = keep, send

    def forward_late(g):
        c = GROUPS[g][-1]
        w, wide = WIDTHS[c], slots * group_width[g]
        shape = (2, quarter, wide)

        def body(fl, i, out, sems):
            pt, swapped, keep, send = i
            at = pl.ds(pl.multiple_of((1 - fl[0]) * half, LANES), half)
            copy_all([(None, swapped.at[n], out[2].at[at, pl.ds((2 + n) * w, w)]) for n in (0, 1)], sems)
            both = jnp.concatenate([swapped[0], swapped[1]], axis=1)
            acc = jnp.dot(pt[:, at], both, preferred_element_type=F32)
            out[0][...] = keep[...]
            out[1][...] = send[...]
            for q, ref in enumerate((out[0], out[1], out[0], out[1])):
                for n in (0, 1):
                    base = (3 + n) * group_width[g] - w
                    ref[q // 2, :, base : base + w] += acc[q * quarter : (q + 1) * quarter, n * w : (n + 1) * w]

        ins = [(st["pt"], whole((spots, rows))), (sent[f"s{c}"], whole((2, half, w)))]
        ins += [(st["r", g], whole(shape)), (st["send", g], whole(shape))]
        st["r", g], send, st["e", c] = run(
            f"forwardlate{g}", body, ins, [(sds(shape, F32), whole(shape))] * 2, through=[st["e", c]],
            scratch=[pltpu.SemaphoreType.DMA((2,))],
        )
        sent[f"rc{g}"] = over_core(send)

    def forward_send(g):
        (send,) = run(f"send{g}", None, through=[st["send", g]])
        sent[f"rc{g}"] = over_core(send)

    def reduce_core(g):
        wide = slots * group_width[g]
        shape, one = (2, quarter, wide), (quarter, wide)

        def body(fl, i, out):
            out[0][...] = i[0][0] + i[1][0]
            out[1][...] = i[0][1] + i[1][1]

        ins = [(st["r", g], whole(shape)), (sent[f"rc{g}"], whole(shape))]
        st["r", g], b = run(f"core{g}", body, ins, [(sds(one, F32), whole(one))] * 2)
        sent[f"rx{g}"] = over_x(b)

    def reduce_x(g):
        w = group_width[g]
        one, part = (quarter, slots * w), (quarter, w)

        def body(fl, i, out):
            for s in range(slots):
                at = slice(s * w, (s + 1) * w)
                out[s][...] = i[0][:, at] + i[1][:, at]

        ins = [(st["r", g], whole(one)), (sent[f"rx{g}"], whole(one))]
        st["r", g], *parts = run(f"x{g}", body, ins, [(sds(part, F32), whole(part))] * slots)
        for s in (1, 2, 3):
            sent[f"rz{s}{g}"] = over_gene(parts[s - 1], s)

    def reduce_gene(g):
        part = (quarter, group_width[g])

        def body(fl, i, out):
            out[0][...] = (i[0][...] + i[1][...]) + (i[2][...] + i[3][...])

        parts = [st["r", g]] + [sent[f"rz{s}{g}"] for s in (1, 2, 3)]
        (v,) = run(f"gene{g}", body, [(a, whole(part)) for a in parts], [(sds(part, F32), whole(part))])
        st["r", g] = v

    steps = {
        "Y": start_swap, "A": start_along, "a": along_send, "S": start_back,
        "e": totals, "m": shares, "F": forward, "f": forward_send, "G": forward_late, "b": members_of, "P": reduce_core, "Q": reduce_x, "R": reduce_gene,
    }
    if spot_size != 2:
        full = lax.all_gather(expression, "spot", axis=0, tiled=True).reshape(slots, rows, genes)
        pieces = [lax.dynamic_index_in_dim(full, gene ^ s, 0, False) for s in range(slots)]
        st["pieces"] = [pieces[0]] + [over_gene(pieces[s], s) for s in (1, 2, 3)]
    for word in " ".join(ORDER).split():
        if word[:2] == "w:":
            if spot_size == 2 or word == "w:ez1+ez2+ez3":
                wait_for(word[2:])
        elif spot_size != 2 and word[0] == "G":
            forward_send(int(word[1]))
        elif spot_size == 2 or word[0] not in "YAaS":
            steps[word[0]](int(word[1]))

    n_ch, n_gr = len(WIDTHS), len(GROUPS)
    starts = [offsets[g[0]] for g in GROUPS]
    preds = [(st["r", g], whole((quarter, group_width[g]))) for g in range(n_gr)]
    mine = (spatial, pl.BlockSpec((quarter, genes), lambda g, f: (f[2], 0)))
    memb = (st["member"], whole((quarter, LANES)))
    gene_spec, spot_spec = whole((16, genes)), whole((8, quarter))

    def stats_body(fl, i, out):
        memb = i[0]
        cols = [jnp.broadcast_to(memb[:, k : k + 1], (quarter, LANES)) for k in range(SLIDES)]
        valid = jnp.sum(memb[:, SLIDES : SLIDES + 1])
        out[0][...] = jnp.broadcast_to(valid, (16, genes))
        totals = [jnp.zeros((quarter, LANES), F32) for _ in range(3)]
        for g in range(n_gr):
            for o in range(0, group_width[g], LANES):
                at = slice(starts[g] + o, starts[g] + o + LANES)
                pr, ta = i[2 + g][:, o : o + LANES], i[1][:, at].astype(F32)
                for j, v in enumerate((pr * ta, pr * pr, ta * ta)):
                    totals[j] += v
                    for k in range(SLIDES):
                        n = 3 * j + k
                        out[0][n : n + 1, at] = jnp.sum(cols[k] * v, axis=0, keepdims=True)
        out[1][...] = jnp.zeros((8, quarter), F32)
        for j in range(3):
            out[1][j : j + 1, :] = jnp.sum(jnp.transpose(totals[j]), axis=0, keepdims=True)

    gene_sums, spot_sums = run(
        "stats", stats_body, [memb, mine, *preds],
        [(sds((16, genes), F32), gene_spec), (sds((8, quarter), F32), spot_spec)],
    )
    spot_parts = [spot_sums] + [over_gene(spot_sums, s) for s in (1, 2, 3)]
    gene_sums = gene_sums + over_core(gene_sums)
    gene_sums = gene_sums + over_x(gene_sums)
    gene_parts = [gene_sums, over_spot(gene_sums)] if spot_size == 2 else [sum_spot(gene_sums)]

    def grads_body(fl, i, out):
        memb, ta_ref, kl, ent = i[:4]
        i = i[4:]
        spot_in, gene_in, preds_in = i[:4], i[4 : 4 + len(gene_parts)], i[4 + len(gene_parts) :]
        scale = -1.0 / (SLIDES * genes_all)
        sums = sum(ref[...] for ref in gene_in)
        num, psq, tsq = sums[0:3], sums[3:6], sums[6:9]
        p_floor, t_floor = jnp.maximum(psq, 1.0), jnp.maximum(tsq, 1.0)
        root = jnp.sqrt(p_floor * t_floor)
        cosine = num / root
        w_t = scale / root
        w_p = jnp.where(psq > 1.0, -scale * cosine / p_floor, 0.0)
        valid_total = jnp.maximum(sums[9, 0], 1.0)
        spot_all = (spot_in[0][...] + spot_in[1][...]) + (spot_in[2][...] + spot_in[3][...])
        s_num, s_p, s_t = [column(spot_all[n : n + 1, :]) for n in range(3)]
        s_p, s_t = s_p + 1e-06, s_t + 1e-06
        root = jnp.sqrt(s_p * s_t)
        cos_spot = s_num / root
        valid = jnp.broadcast_to(memb[:, SLIDES : SLIDES + 1], (quarter, LANES))
        coef = -valid / valid_total
        coef_t, coef_p = coef / root, -coef * cos_spot / s_p
        first = [(fl[n] == 0).astype(F32) for n in (2, 4, 3)]
        terms = [
            jnp.sum(cosine) * first[0] * first[1],
            jnp.sum((valid * cos_spot)[:, 0:1]) * first[2],
            kl[0, 0] * first[1],
            jnp.sum(ent[0:1, :]),
            valid_total * first[0] * first[1] * first[2],
        ]
        lane = lax.broadcasted_iota(jnp.int32, (8, spots), 1)
        value = jnp.zeros((8, spots), F32)
        for n, term in enumerate(terms):
            value = jnp.where(lane == n, term, value)
        out[1][...] = value
        cols = [jnp.broadcast_to(memb[:, k : k + 1], (quarter, LANES)) for k in range(SLIDES)]
        for g in range(n_gr):
            for o in range(0, group_width[g], LANES):
                at = slice(starts[g] + o, starts[g] + o + LANES)
                f_t, f_p = coef_t, coef_p
                for k in range(SLIDES):
                    f_t = f_t + cols[k] * w_t[k : k + 1, at]
                    f_p = f_p + cols[k] * w_p[k : k + 1, at]
                out[0][:, at] = (f_t * ta_ref[:, at].astype(F32) + f_p * preds_in[g][:, o : o + LANES]).astype(BF)

    row8, flat = whole((8, spots)), whole((8, LANES))
    ins = [memb, mine, (st["kl"], flat), (st["ent"], row8)]
    ins += [(a, spot_spec) for a in spot_parts] + [(a, gene_spec) for a in gene_parts] + preds
    grad, terms = run(
        "grads", grads_body, ins,
        [(sds((quarter, genes), BF), whole((quarter, genes))), (sds((8, spots), F32), row8)],
    )
    terms = [terms, over_spot(terms)] if spot_size == 2 else [sum_spot(terms)]
    grad = jnp.stack([grad] + [over_gene(grad, s) for s in (1, 2, 3)])
    grad_x = over_x(grad)
    grads = [grad, over_core(grad), grad_x, over_core(grad_x)]

    row_blk = rows // 4

    def backward_body(fl, i, out, held, sems):
        lg, tot, sm = i[:3]
        efs, gs, terms = i[3 : 3 + n_ch], i[3 + n_ch : 7 + n_ch], i[7 + n_ch :]

        @pl.when(pl.program_id(0) == 0)
        def _():
            row = lax.broadcasted_iota(jnp.int32, (8, spots), 0)
            out[1][...] = jnp.where(row == 0, 0.0, sum(ref[...] for ref in terms))
            copies = []
            for b, ref in enumerate(gs):
                at = pl.multiple_of((fl[2] ^ b) * quarter, quarter)
                copies.append((None, ref, held.at[:, pl.ds(at, quarter), :]))
            copy_all(copies, sems)

        acc = -jnp.broadcast_to(sm[:, 0:1], (row_blk, spots))
        for s in range(slots):
            left = jnp.concatenate([ef[:, s * w : (s + 1) * w] for w, ef in zip(WIDTHS, efs)], axis=1)
            acc += lax.dot_general(left, held[s], (((1,), (1,)), ((), ())), preferred_element_type=F32)
        out[0][...] = acc
        prob = jnp.exp(lg[...].astype(F32)) * (1.0 / tot[0:1, :])
        out[1][0:1, :] += jnp.sum(prob * acc, axis=0, keepdims=True)

    def by_rows(width, size=row_blk):
        return pl.BlockSpec((size, width), lambda g, f: (g, 0))

    ins = [(logits, by_rows(spots)), (st["tot"], row8), (st["sm"], by_rows(LANES))]
    ins += [(st["e", c], by_rows(slots * WIDTHS[c])) for c in chunks]
    ins += [(a, ANY) for a in grads] + [(a, row8) for a in terms]
    grad_probs, v = run(
        "backward", backward_body, ins,
        [(sds((rows, spots), F32), by_rows(spots)), (sds((8, spots), F32), row8)],
        grid=(rows // row_blk,),
        scratch=[pltpu.VMEM((slots, spots, genes), BF), pltpu.SemaphoreType.DMA((len(grads),))],
    )

    v = v + over_core(v)
    v = v + over_x(v)
    v = (v + over_gene(v, 1)) + (over_gene(v, 2) + over_gene(v, 3))

    def final_body(fl, i, out):
        prob = jnp.exp(i[0][...].astype(F32)) * (1.0 / i[1][0:1, :])
        out[0][...] = prob * (i[2][...] - i[3][0:1, :])

        @pl.when(pl.program_id(0) == 0)
        def _():
            sums = [i[3][1, n] for n in range(5)]
            gene_term, spot_term = sums[0] / (SLIDES * genes_all), sums[1] / sums[4]
            divergence, entropy = sums[2], sums[3] / spots_all
            values = (divergence - gene_term - spot_term, gene_term, spot_term, divergence, entropy)
            for n, value in enumerate(values):
                out[1][n] = value

    last_blk = rows // 2
    blk = by_rows(spots, last_blk)
    grad_logits, loss_terms = run(
        "final", final_body, [(logits, blk), (st["tot"], row8), (grad_probs, blk), (v, row8)],
        [(sds((rows, spots), F32), blk), (sds((5,), F32), pl.BlockSpec(memory_space=pltpu.SMEM))],
        grid=(rows // last_blk,),
    )
    return (loss_terms, grad_logits)


def solution(mesh):
    return jax.shard_map(
        functools.partial(per_device, dict(mesh.shape)),
        mesh=mesh,
        in_specs=(
            P(("cell", "gene"), "spot"),
            P(("cell", "spot"), "gene"),
            P("spot", "gene"),
            P("spot"),
            P("spot"),
            P(("cell", "gene")),
        ),
        out_specs=(P(), P(("cell", "gene"), "spot")),
        check_vma=False,
    )
```

```python
import functools
import jax
import jax.numpy as jnp
from jax import lax
from jax.experimental import pallas as pl
from jax.experimental.pallas import tpu as pltpu
from jax.sharding import PartitionSpec as P

SLIDES = 3
LANES = 128
PAD = 8
ANY = pl.BlockSpec(memory_space=pl.ANY)
BF = jnp.bfloat16
F32 = jnp.float32
VMEM_BYTES = 20 * 1024 * 1024
COSTS = {"spots": 1, "back3": 6, "addx1": 9, "half0": 3}
WIDTHS = (128, 128, 128, 128)
GROUPS = ((0, 1), (2,), (3,))
SUMS = ((0,), (1, 2))
ORDER = (
    "Y0 e0 Y1 w:ez1+ez2+ez3",
    "Y2 A0 a0 e3",
    "b0 A1 Y3 w:f20+f30+n0",
    "a1 A2 w:f21+f31+n1 a2",
    "S0 A3 w:f22+f32+n2 a3",
    "S1 w:s0 S2 w:s1",
    "F0 w:f23+f33+n3 S3 w:s2",
    "f0 P0 F1 f1",
    "P1 F2 Q0 G2",
    "P2 X1 Q1 U0",
    "m0 R1 R0",
)


def sds(shape, dtype):
    return jax.ShapeDtypeStruct(shape, dtype)


def whole(shape):
    zeros = (0,) * len(shape)
    return pl.BlockSpec(shape, lambda *_: zeros)


def xor_pairs(size, step):
    return [(n, n ^ step) for n in range(size)]


class Chain:
    def __init__(self, flags):
        self.flags = flags
        self.token = jnp.zeros((8, LANES), F32)

    def run(self, name, body, ins=(), outs=(), after=(), through=(), grid=(1,), scratch=()):
        ins = [*ins, *((a, ANY) for a in after)]
        carried = (*through, self.token)
        n_in, n_out, n_thr = len(ins), len(outs), len(carried)

        def kernel(flags, *refs):
            in_refs = refs[:n_in]
            out_refs = refs[n_in + n_thr : n_in + 2 * n_thr + n_out - 1]
            scratch_refs = refs[n_in + 2 * n_thr + n_out :]
            if body is not None:
                body(flags, in_refs, out_refs, *scratch_refs)

        results = pl.pallas_call(
            kernel,
            out_shape=[s for s, _ in outs] + [sds(a.shape, a.dtype) for a in carried],
            grid_spec=pltpu.PrefetchScalarGridSpec(
                num_scalar_prefetch=1,
                grid=grid,
                in_specs=[s for _, s in ins] + [ANY] * n_thr,
                out_specs=[s for _, s in outs] + [ANY] * n_thr,
                scratch_shapes=list(scratch),
            ),
            input_output_aliases={1 + n_in + j: n_out + j for j in range(n_thr)},
            compiler_params=pltpu.CompilerParams(vmem_limit_bytes=VMEM_BYTES),
            cost_estimate=pl.CostEstimate(flops=COSTS.get(name, 0) * 10**9, bytes_accessed=0, transcendentals=0),
            name=name,
        )(self.flags, *[a for a, _ in ins], *carried)
        self.token = results[-1]
        return results[:-1]


def copy_all(copies, sems):
    made = [(c, pltpu.make_async_copy(s, d, sems.at[n])) for n, (c, s, d) in enumerate(copies)]
    for act in ("start", "wait"):
        for cond, copy in made:
            if cond is None:
                getattr(copy, act)()
            else:
                pl.when(cond)(getattr(copy, act))


def column(row):
    return jnp.transpose(jnp.broadcast_to(row, (LANES, row.shape[1])))


def per_device(sizes, logits, expression, spatial, slide_ids, spot_mask, densities):
    spot_size = sizes["spot"]
    rows, spots = logits.shape
    genes = spatial.shape[1]
    spots_all = spots * spot_size
    genes_all = genes * sizes["gene"]
    slots = sizes["gene"]
    quarter = spots // sizes["cell"]
    half = rows // 2
    cell, spot, gene = (lax.axis_index(a) for a in ("cell", "spot", "gene"))
    home = (gene // 2 == spot).astype(jnp.int32)
    side = (gene % 2).astype(jnp.int32)
    chain = Chain(jnp.stack([home, side, cell, gene, spot]).astype(jnp.int32))
    run = chain.run
    offsets = [sum(WIDTHS[:n]) for n in range(len(WIDTHS))]
    chunks = range(len(WIDTHS))
    group_width = [sum(WIDTHS[c] for c in g) for g in GROUPS]

    def over_core(v):
        return lax.ppermute(v, "cell", xor_pairs(4, 1))

    def over_x(v):
        return lax.ppermute(v, "cell", xor_pairs(4, 2))

    def over_gene(v, step):
        return lax.ppermute(v, "gene", xor_pairs(4, step))

    def over_spot(v, step=1):
        return lax.ppermute(v, "spot", xor_pairs(spot_size, step))

    def sum_spot(v):
        step = 1
        while step < spot_size:
            v = v + over_spot(v, step)
            step *= 2
        return v

    ids_row, mask_row = slide_ids.reshape(1, spots), spot_mask.reshape(1, spots)
    dens_row = densities.reshape(1, rows)

    expr = expression.reshape(2, half * 2, genes) if spot_size == 2 else None
    st, sent = {}, {}

    def start_swap(c):
        w = WIDTHS[c]
        if c == 0:
            sent["y0"] = over_spot(expr[:, :, :w])
            return

        def body(fl, i, out, sems):
            copy_all([(None, i[0].at[p, :, pl.ds(offsets[c], w)], out[0].at[p]) for p in range(2)], sems)

        shape = (2, rows, w)
        (v,) = run(
            f"swap{c}", body, [(expr, pl.BlockSpec(memory_space=pltpu.HBM))], [(sds(shape, BF), whole(shape))],
            scratch=[pltpu.SemaphoreType.DMA((2,))],
        )
        sent[f"y{c}"] = over_spot(v)

    def start_along(c):
        w, o = WIDTHS[c], offsets[c] // WIDTHS[c]
        blk, one = (1, half, w), (half, w)

        def body(fl, i, out):
            @pl.when(fl[0] == 1)
            def _():
                out[0][...] = i[0][0]
                out[1][...] = i[1][0]
                out[2][0] = i[2][0]
                out[2][1] = i[3][0]

            @pl.when(fl[0] == 0)
            def _():
                out[0][...] = i[4][0]
                out[1][...] = i[5][0]
                out[2][0] = i[6][0]
                out[2][1] = i[7][0]

        def at(same, part, col):
            return pl.BlockSpec(blk, lambda g, f: (f[1] if same else 1 - f[1], part, col))

        y = sent[f"y{c}"]
        ins = [(y, at(True, 0, 0)), (y, at(False, 0, 0)), (expr, at(False, 0, o)), (expr, at(False, 1, o))]
        ins += [(expr, at(True, 1, o)), (expr, at(False, 1, o)), (y, at(False, 0, 0)), (y, at(False, 1, 0))]
        outs = [(sds(one, BF), whole(one))] * 2 + [(sds((2, half, w), BF), whole((2, half, w)))]
        st["along", c] = run(f"along{c}", body, ins, outs)

    def along_send(c):
        a, b, n = run(f"alongsend{c}", None, through=st["along", c])
        sent[f"f2{c}"], sent[f"f3{c}"], sent[f"n{c}"] = over_gene(a, 2), over_gene(b, 3), over_gene(n, 1)

    def start_back(c):
        w = WIDTHS[c]

        def body(fl, i, out):
            out[0][0] = i[0][...]
            out[0][1] = i[1][...]

        one = whole((half, w))
        (st["f", c],) = run(
            f"back{c}", body, [(sent[f"f2{c}"], one), (sent[f"f3{c}"], one)], [(sds((2, half, w), BF), whole((2, half, w)))],
        )
        sent[f"s{c}"] = over_spot(st["f", c])

    def wait_for(name):
        run("wait", None, after=[sent[n] for n in name.split("+")])

    def members_of(_):
        def body(fl, i, out):
            ids, valid = column(i[0][...].astype(F32)), column(i[1][...].astype(F32))
            lane = lax.broadcasted_iota(jnp.int32, (quarter, LANES), 1)
            inside = (lane < SLIDES) & (lane.astype(F32) == ids) & (valid == 1.0)
            out[0][...] = jnp.where(inside, 1.0, jnp.where(lane == SLIDES, valid, 0.0))

        row, tall = pl.BlockSpec((1, quarter), lambda g, f: (0, f[2])), whole((quarter, LANES))
        (st["member"],) = run("member", body, [(ids_row, row), (mask_row, row)], [(sds((quarter, LANES), F32), tall)])

    def totals(n):
        sp = whole((8, spots))
        if n == 0:

            def body(fl, i, out):
                out[0][...] = jnp.zeros((8, spots), F32)
                out[0][0:1, :] = jnp.sum(jnp.exp(i[0][...].astype(F32)), axis=0, keepdims=True)
                out[0][1:2, :] = jnp.broadcast_to(jnp.sum(i[1][...]), (1, spots))

            ins = [(logits, whole(logits.shape)), (dens_row, whole(dens_row.shape))]
            (v,) = run("totals", body, ins, [(sds((8, spots), F32), sp)])
            st["tot"] = lax.psum(v, "cell")
            for s in (1, 2, 3):
                sent[f"ez{s}"] = over_gene(st["tot"], s)
        else:
            blk = 2 * LANES

            def body(fl, i, out):
                tot = (i[1][...] + i[2][...]) + (i[3][...] + i[4][...])
                out[3][...] = tot
                inv = 1.0 / tot[0:1, :]
                log_tot = jnp.log(tot[0:1, :])
                vals = i[0][...].astype(F32)
                prob = jnp.exp(vals) * inv
                prob_t = jnp.transpose(prob.astype(BF))
                for q in range(sizes["cell"]):
                    at = pl.multiple_of((fl[2] ^ q) * quarter, quarter)
                    out[0][pl.ds(at, quarter), :] = prob_t[q * quarter : (q + 1) * quarter]
                folded = sum(prob[:, n : n + LANES] for n in range(0, spots, LANES))
                row_sums = jnp.sum(jnp.transpose(folded), axis=0, keepdims=True)
                out[1][...] = jnp.broadcast_to(row_sums, (8, blk))

                @pl.when(pl.program_id(0) == 0)
                def _():
                    out[2][...] = jnp.zeros((8, spots), F32)

                out[2][0:1, :] -= jnp.sum(prob * (vals - log_tot), axis=0, keepdims=True)

            parts = [st["tot"]] + [sent[f"ez{s}"] for s in (1, 2, 3)]
            pt, mass, ent, st["tot"] = run(
                "prob", body,
                [(logits, pl.BlockSpec((blk, spots), lambda g, f: (g, 0)))] + [(a, sp) for a in parts],
                [
                    (sds((spots, rows), BF), pl.BlockSpec((spots, blk), lambda g, f: (0, g))),
                    (sds((8, rows), F32), pl.BlockSpec((8, blk), lambda g, f: (0, g))),
                    (sds((8, spots), F32), sp),
                    (sds((8, spots), F32), sp),
                ],
                grid=(rows // blk,),
            )
            st["pt"], st["ent"] = pt, ent
            st["mass"] = mass if spot_size == 2 else sum_spot(mass)
            if spot_size == 2:
                sent["my"] = over_spot(mass)

    def shares(_):
        masses = [st["mass"]] + ([sent["my"]] if spot_size == 2 else [])

        def body(fl, i, out):
            mass = i[2][0:1, :]
            for extra in i[3:]:
                mass = mass + extra[0:1, :]
            share = i[0][...] / i[1][1:2, 0:1]
            out[0][...] = column(share / mass)
            kl = jnp.sum(share * (jnp.log(share) - jnp.log(mass / spots_all)))
            out[1][...] = jnp.broadcast_to(kl, (8, LANES))

        st["sm"], st["kl"] = run(
            "shares", body,
            [(dens_row, whole(dens_row.shape)), (st["tot"], whole((8, spots)))]
            + [(m, whole((8, rows))) for m in masses],
            [(sds((rows, LANES), F32), whole((rows, LANES))), (sds((8, LANES), F32), whole((8, LANES)))],
        )

    def halves_of(g):
        shape = (quarter, slots * group_width[g])
        if len(GROUPS[g]) == 1:
            return [(sds(shape, F32), whole(shape))] * 2
        return [(sds((2, *shape), F32), whole((2, *shape)))]

    def forward(g):
        members, wide_all = GROUPS[g], group_width[g] * slots
        shape = (2, quarter, wide_all)
        outs = [(sds((rows, slots * WIDTHS[c]), BF), whole((rows, slots * WIDTHS[c]))) for c in members]
        outs += [(sds(shape, F32), whole(shape))]
        outs += halves_of(g)

        late = members[-1] if spot_size == 2 and g == len(GROUPS) - 1 else None

        def product(pt, efs, keep, *send, direct=None):
            done = 0
            low, high = send if len(send) == 2 else (send[0].at[0], send[0].at[1])
            for c, ef in zip(members, efs):
                w = WIDTHS[c]
                if c == late:
                    near = jnp.dot(pt[...], ef[:, : 2 * w], preferred_element_type=F32)
                    at = pl.ds(pl.multiple_of(direct, LANES), half)
                    far = jnp.dot(pt[:, at], ef[at, 2 * w :], preferred_element_type=F32)
                    acc = jnp.concatenate([near, far], axis=1)
                else:
                    acc = jnp.dot(pt[...], ef[...], preferred_element_type=F32)
                for q, ref in enumerate((keep.at[0], low, keep.at[1], high)):
                    rows_q = acc[q * quarter : (q + 1) * quarter]
                    for s in range(slots):
                        base = s * group_width[g] + done
                        ref[:, base : base + w] = rows_q[:, s * w : (s + 1) * w]
                done += w

        if spot_size == 2:

            def body(fl, i, out, sems):
                pt, e = i[:2]
                at_home, away = fl[0] == 1, fl[0] == 0
                top, low = pl.ds(0, half), pl.ds(half, half)
                copies = []
                for m, c in enumerate(members):
                    w, ef = WIDTHS[c], out[m]
                    y, n, f = i[2 + 4 * m : 5 + 4 * m]
                    copies += [
                        (at_home, e.at[fl[1], :, pl.ds(offsets[c], w)], ef.at[:, pl.ds(0, w)]),
                        (away, y.at[fl[1]], ef.at[:, pl.ds(0, w)]),
                        (None, n.at[0], ef.at[top, pl.ds(w, w)]),
                        (None, n.at[1], ef.at[low, pl.ds(w, w)]),
                    ]
                    for part in (0, 1):
                        cols = pl.ds((2 + part) * w, w)
                        copies += [(at_home, f.at[part], ef.at[low, cols]), (away, f.at[part], ef.at[top, cols])]
                        if c != late:
                            s = i[5 + 4 * m]
                            copies += [(at_home, s.at[part], ef.at[top, cols]), (away, s.at[part], ef.at[low, cols])]
                copy_all(copies, sems)
                product(pt, out[: len(members)], *out[len(members) :], direct=fl[0] * half)

            ins = [(st["pt"], whole((spots, rows))), (expr, ANY)]
            ins += [
                (a, ANY)
                for c in members
                for a in (sent[f"y{c}"], sent[f"n{c}"], st["f", c], *([] if c == late else [sent[f"s{c}"]]))
            ]
            scratch = [pltpu.SemaphoreType.DMA((12 * len(members),))]
        else:

            def body(fl, i, out):
                for m, c in enumerate(members):
                    w = WIDTHS[c]
                    for s in range(slots):
                        out[m][:, s * w : (s + 1) * w] = i[1 + m * slots + s][...]
                product(i[0], out[: len(members)], *out[len(members) :])

            def at_chunk(c):
                return pl.BlockSpec((rows, WIDTHS[c]), lambda *_: (0, offsets[c] // WIDTHS[c]))

            ins = [(st["pt"], whole((spots, rows)))] + [(a, at_chunk(c)) for c in members for a in st["pieces"]]
            scratch = []
        results = run(f"forward{g}", body, ins, outs, scratch=scratch)
        for c, ef in zip(members, results):
            st["e", c] = ef
        st["r", g], st["send", g] = results[len(members)], results[len(members) + 1 :]

    def forward_late(g):
        c = GROUPS[g][-1]
        w, wide = WIDTHS[c], slots * group_width[g]
        shape = (2, quarter, wide)

        def body(fl, i, out, sems):
            pt, swapped, keep, low, high = i
            at = pl.ds(pl.multiple_of((1 - fl[0]) * half, LANES), half)
            copy_all([(None, swapped.at[n], out[3].at[at, pl.ds((2 + n) * w, w)]) for n in (0, 1)], sems)
            both = jnp.concatenate([swapped[0], swapped[1]], axis=1)
            acc = jnp.dot(pt[:, at], both, preferred_element_type=F32)
            for new, old in zip(out, (keep, low, high)):
                new[...] = old[...]
            for q, ref in enumerate((out[0].at[0], out[1], out[0].at[1], out[2])):
                for n in (0, 1):
                    base = (3 + n) * group_width[g] - w
                    ref[:, base : base + w] += acc[q * quarter : (q + 1) * quarter, n * w : (n + 1) * w]

        one = whole((quarter, wide))
        ins = [(st["pt"], whole((spots, rows))), (sent[f"s{c}"], whole((2, half, w)))]
        ins += [(st["r", g], whole(shape))] + [(a, one) for a in st["send", g]]
        st["r", g], *send, st["e", c] = run(
            f"forwardlate{g}", body, ins, [(sds(shape, F32), whole(shape)), *halves_of(g)], through=[st["e", c]],
            scratch=[pltpu.SemaphoreType.DMA((2,))],
        )
        send_core(g, send)

    def send_core(g, send):
        for n, part in enumerate(send):
            sent[f"rc{n}{g}"] = over_core(part)

    def forward_send(g):
        send_core(g, run(f"send{g}", None, through=st["send", g]))

    def reduce_core(g):
        wide = slots * group_width[g]
        shape, one = (2, quarter, wide), (quarter, wide)

        single = len(GROUPS[g]) == 1

        def body(fl, i, out):
            for n in (0, 1):
                out[n][0:quarter, :] = i[0][n] + (i[1 + n][...] if single else i[1][n])
            if single:
                out[1][quarter:, :] = jnp.zeros((PAD, wide), F32)

        ins = [(st["r", g], whole(shape))]
        ins += [(sent[f"rc{n}{g}"], whole(one)) for n in (0, 1)] if single else [(sent[f"rc0{g}"], whole(shape))]
        more = (quarter + PAD, wide) if single else one
        st["r", g], b = run(f"core{g}", body, ins, [(sds(one, F32), whole(one)), (sds(more, F32), whole(more))])
        sent[f"rx{g}"] = over_x(b)

    sum_groups = [[g for g in z] for z in SUMS]
    sum_width = [sum(group_width[g] for g in z) for z in SUMS]

    def add_x(g):
        one = whole((quarter, slots * group_width[g]))

        def body(fl, i, out):
            out[0][...] = i[0][...] + i[1][0:quarter, :]

        ins = [(st["r", g], one), (sent[f"rx{g}"], whole(sent[f"rx{g}"].shape))]
        (st["added", g],) = run(f"addx{g}", body, ins, [(sds(one.block_shape, F32), one)])

    def reduce_x(z):
        members, w = sum_groups[z], sum_width[z]
        part = (quarter, w)
        in_halves = z < len(SUMS) - 1

        def body(fl, i, out):
            done, i = 0, list(i)
            for g in members:
                v = group_width[g]
                refs = [i.pop(0) for _ in parts_of[g]]
                for s in range(slots):
                    at = slice(s * v, (s + 1) * v)
                    value = sum(ref[0:quarter, at] for ref in refs)
                    if in_halves and s >= 2:
                        out[2][s - 2, 0:quarter, done : done + v] = value
                    else:
                        out[s][:, done : done + v] = value
                done += v
            if in_halves:
                out[2][:, quarter:, :] = jnp.zeros((2, PAD, w), F32)

        parts_of = {g: [st["added", g]] if ("added", g) in st else [st["r", g], sent[f"rx{g}"]] for g in members}
        ins = [(a, whole(a.shape)) for g in members for a in parts_of[g]]
        outs = [(sds(part, F32), whole(part))] * (2 if in_halves else slots)
        if in_halves:
            padded = (2, quarter + PAD, w)
            outs += [(sds(padded, F32), whole(padded))]
        parts = run(f"x{z}", body, ins, outs)
        if in_halves:
            st["z", z] = parts[:2]
            sent[f"rz2{z}"] = over_gene(parts[2], 2)
        else:
            st["z", z] = parts[:1]
            for s in (1, 2, 3):
                sent[f"rz{s}{z}"] = over_gene(parts[s], s)

    def reduce_half(z):
        part = (quarter, sum_width[z])

        def body(fl, i, out):
            for n in (0, 1):
                out[n][...] = i[n][...] + i[2][n, 0:quarter, :]

        ins = [(a, whole(part)) for a in st["z", z]] + [(sent[f"rz2{z}"], whole((2, quarter + PAD, sum_width[z])))]
        a, b = run(f"half{z}", body, ins, [(sds(part, F32), whole(part))] * 2)
        st["z", z], sent[f"rz1{z}"] = [a], over_gene(b, 1)

    def reduce_gene(z):
        part = (quarter, sum_width[z])
        others = [sent[f"rz{s}{z}"] for s in ((1,) if z < len(SUMS) - 1 else (1, 2, 3))]

        def body(fl, i, out):
            out[0][...] = sum(ref[...] for ref in i)

        ins = [(a, whole(part)) for a in (*st["z", z], *others)]
        (st["sum", z],) = run(f"gene{z}", body, ins, [(sds(part, F32), whole(part))])

    steps = {
        "Y": start_swap, "A": start_along, "a": along_send, "S": start_back,
        "e": totals, "m": shares, "F": forward, "f": forward_send, "G": forward_late, "b": members_of,
        "P": reduce_core, "X": add_x, "Q": reduce_x,
        "U": reduce_half, "R": reduce_gene,
    }
    if spot_size != 2:
        full = lax.all_gather(expression, "spot", axis=0, tiled=True).reshape(slots, rows, genes)
        pieces = [lax.dynamic_index_in_dim(full, gene ^ s, 0, False) for s in range(slots)]
        st["pieces"] = [pieces[0]] + [over_gene(pieces[s], s) for s in (1, 2, 3)]
    for word in " ".join(ORDER).split():
        if word[:2] == "w:":
            if spot_size == 2 or word == "w:ez1+ez2+ez3":
                wait_for(word[2:])
        elif spot_size != 2 and word[0] == "G":
            forward_send(int(word[1]))
        elif spot_size == 2 or word[0] not in "YAaS":
            steps[word[0]](int(word[1]))

    n_ch, n_sum = len(WIDTHS), len(SUMS)
    starts = [offsets[GROUPS[z[0]][0]] for z in SUMS]
    preds = [(st["sum", z], whole((quarter, sum_width[z]))) for z in range(n_sum)]
    mine = (spatial, pl.BlockSpec((quarter, genes), lambda g, f: (f[2], 0)))
    memb = (st["member"], whole((quarter, LANES)))
    gene_spec, spot_spec = whole((16, genes)), whole((8, quarter))

    def stats_body(fl, i, out):
        memb = i[0]
        cols = [jnp.broadcast_to(memb[:, k : k + 1], (quarter, LANES)) for k in range(SLIDES)]
        valid = jnp.sum(memb[:, SLIDES : SLIDES + 1])
        out[0][...] = jnp.broadcast_to(valid, (16, genes))
        totals = [jnp.zeros((quarter, LANES), F32) for _ in range(3)]
        for g in range(n_sum):
            for o in range(0, sum_width[g], LANES):
                at = slice(starts[g] + o, starts[g] + o + LANES)
                pr, ta = i[2 + g][:, o : o + LANES], i[1][:, at].astype(F32)
                for j, v in enumerate((pr * ta, pr * pr, ta * ta)):
                    totals[j] += v
                    for k in range(SLIDES):
                        n = 3 * j + k
                        out[0][n : n + 1, at] = jnp.sum(cols[k] * v, axis=0, keepdims=True)
        out[1][...] = jnp.zeros((8, quarter), F32)
        for j in range(3):
            out[1][j : j + 1, :] = jnp.sum(jnp.transpose(totals[j]), axis=0, keepdims=True)

    gene_sums, spot_sums = run(
        "stats", stats_body, [memb, mine, *preds],
        [(sds((16, genes), F32), gene_spec), (sds((8, quarter), F32), spot_spec)],
    )
    spot_parts = [spot_sums] + [over_gene(spot_sums, s) for s in (1, 2, 3)]
    gene_sums = gene_sums + over_core(gene_sums)
    gene_sums = gene_sums + over_x(gene_sums)
    gene_parts = [gene_sums, over_spot(gene_sums)] if spot_size == 2 else [sum_spot(gene_sums)]

    run("spots", None, after=spot_parts)

    def grads_body(fl, i, out):
        memb, ta_ref, kl, ent = i[:4]
        i = i[4:]
        spot_in, gene_in, preds_in = i[:4], i[4 : 4 + len(gene_parts)], i[4 + len(gene_parts) :]
        scale = -1.0 / (SLIDES * genes_all)
        sums = sum(ref[...] for ref in gene_in)
        num, psq, tsq = sums[0:3], sums[3:6], sums[6:9]
        p_floor, t_floor = jnp.maximum(psq, 1.0), jnp.maximum(tsq, 1.0)
        root = jnp.sqrt(p_floor * t_floor)
        cosine = num / root
        w_t = scale / root
        w_p = jnp.where(psq > 1.0, -scale * cosine / p_floor, 0.0)
        valid_total = jnp.maximum(sums[9, 0], 1.0)
        spot_all = (spot_in[0][...] + spot_in[1][...]) + (spot_in[2][...] + spot_in[3][...])
        s_num, s_p, s_t = [column(spot_all[n : n + 1, :]) for n in range(3)]
        s_p, s_t = s_p + 1e-06, s_t + 1e-06
        root = jnp.sqrt(s_p * s_t)
        cos_spot = s_num / root
        valid = jnp.broadcast_to(memb[:, SLIDES : SLIDES + 1], (quarter, LANES))
        coef = -valid / valid_total
        coef_t, coef_p = coef / root, -coef * cos_spot / s_p
        first = [(fl[n] == 0).astype(F32) for n in (2, 4, 3)]
        terms = [
            jnp.sum(cosine) * first[0] * first[1],
            jnp.sum((valid * cos_spot)[:, 0:1]) * first[2],
            kl[0, 0] * first[1],
            jnp.sum(ent[0:1, :]),
            valid_total * first[0] * first[1] * first[2],
        ]
        lane = lax.broadcasted_iota(jnp.int32, (8, spots), 1)
        value = jnp.zeros((8, spots), F32)
        for n, term in enumerate(terms):
            value = jnp.where(lane == n, term, value)
        out[1][...] = value
        cols = [jnp.broadcast_to(memb[:, k : k + 1], (quarter, LANES)) for k in range(SLIDES)]
        for g in range(n_sum):
            for o in range(0, sum_width[g], LANES):
                at = slice(starts[g] + o, starts[g] + o + LANES)
                f_t, f_p = coef_t, coef_p
                for k in range(SLIDES):
                    f_t = f_t + cols[k] * w_t[k : k + 1, at]
                    f_p = f_p + cols[k] * w_p[k : k + 1, at]
                out[0][:, at] = (f_t * ta_ref[:, at].astype(F32) + f_p * preds_in[g][:, o : o + LANES]).astype(BF)

    row8, flat = whole((8, spots)), whole((8, LANES))
    ins = [memb, mine, (st["kl"], flat), (st["ent"], row8)]
    ins += [(a, spot_spec) for a in spot_parts] + [(a, gene_spec) for a in gene_parts] + preds
    grad, terms = run(
        "grads", grads_body, ins,
        [(sds((quarter, genes), BF), whole((quarter, genes))), (sds((8, spots), F32), row8)],
    )
    terms = [terms, over_spot(terms)] if spot_size == 2 else [sum_spot(terms)]
    grad_x = over_x(grad)
    others = [over_gene(grad, s) for s in (1, 2, 3)]
    one, rest = (quarter, genes), (slots - 1, quarter, genes)

    def gather_body(fl, i, out):
        for n in range(slots - 1):
            out[0][n] = i[n][...]

    (rest_z,) = run(
        "gather", gather_body, [(a, whole(one)) for a in others], [(sds(rest, BF), whole(rest))], after=[grad_x]
    )
    rest_x = over_x(rest_z)
    grads = [grad, over_core(grad), grad_x, over_core(grad_x), rest_z, over_core(rest_z), rest_x, over_core(rest_x)]

    row_blk = rows // 4

    def backward_body(fl, i, out, held, sems):
        lg, tot, sm = i[:3]
        efs, gs, terms = i[3 : 3 + n_ch], i[3 + n_ch : 11 + n_ch], i[11 + n_ch :]

        @pl.when(pl.program_id(0) == 0)
        def _():
            row = lax.broadcasted_iota(jnp.int32, (8, spots), 0)
            out[1][...] = jnp.where(row == 0, 0.0, sum(ref[...] for ref in terms))
            copies = []
            for b in range(sizes["cell"]):
                at = pl.ds(pl.multiple_of((fl[2] ^ b) * quarter, quarter), quarter)
                copies.append((None, gs[b], held.at[0, at, :]))
                copies.append((None, gs[4 + b], held.at[pl.ds(1, slots - 1), at, :]))
            copy_all(copies, sems)

        acc = -jnp.broadcast_to(sm[:, 0:1], (row_blk, spots))
        for s in range(slots):
            left = jnp.concatenate([ef[:, s * w : (s + 1) * w] for w, ef in zip(WIDTHS, efs)], axis=1)
            acc += lax.dot_general(left, held[s], (((1,), (1,)), ((), ())), preferred_element_type=F32)
        out[0][...] = acc
        prob = jnp.exp(lg[...].astype(F32)) * (1.0 / tot[0:1, :])
        out[1][0:1, :] += jnp.sum(prob * acc, axis=0, keepdims=True)

    def by_rows(width, size=row_blk):
        return pl.BlockSpec((size, width), lambda g, f: (g, 0))

    ins = [(logits, by_rows(spots)), (st["tot"], row8), (st["sm"], by_rows(LANES))]
    ins += [(st["e", c], by_rows(slots * WIDTHS[c])) for c in chunks]
    ins += [(a, ANY) for a in grads] + [(a, row8) for a in terms]
    grad_probs, v = run(
        "backward", backward_body, ins,
        [(sds((rows, spots), F32), by_rows(spots)), (sds((8, spots), F32), row8)],
        grid=(rows // row_blk,),
        scratch=[pltpu.VMEM((slots, spots, genes), BF), pltpu.SemaphoreType.DMA((len(grads),))],
    )

    v = v + over_core(v)
    v = v + over_x(v)
    v = (v + over_gene(v, 1)) + (over_gene(v, 2) + over_gene(v, 3))

    def final_body(fl, i, out):
        prob = jnp.exp(i[0][...].astype(F32)) * (1.0 / i[1][0:1, :])
        out[0][...] = prob * (i[2][...] - i[3][0:1, :])

        @pl.when(pl.program_id(0) == 0)
        def _():
            sums = [i[3][1, n] for n in range(5)]
            gene_term, spot_term = sums[0] / (SLIDES * genes_all), sums[1] / sums[4]
            divergence, entropy = sums[2], sums[3] / spots_all
            values = (divergence - gene_term - spot_term, gene_term, spot_term, divergence, entropy)
            for n, value in enumerate(values):
                out[1][n] = value

    last_blk = rows // 2
    blk = by_rows(spots, last_blk)
    grad_logits, loss_terms = run(
        "final", final_body, [(logits, blk), (st["tot"], row8), (grad_probs, blk), (v, row8)],
        [(sds((rows, spots), F32), blk), (sds((5,), F32), pl.BlockSpec(memory_space=pltpu.SMEM))],
        grid=(rows // last_blk,),
    )
    return (loss_terms, grad_logits)


def solution(mesh):
    return jax.shard_map(
        functools.partial(per_device, dict(mesh.shape)),
        mesh=mesh,
        in_specs=(
            P(("cell", "gene"), "spot"),
            P(("cell", "spot"), "gene"),
            P("spot", "gene"),
            P("spot"),
            P("spot"),
            P(("cell", "gene")),
        ),
        out_specs=(P(), P(("cell", "gene"), "spot")),
        check_vma=False,
    )
```

```python
import functools
import jax
import jax.numpy as jnp
from jax import lax
from jax.experimental import pallas as pl
from jax.experimental.pallas import tpu as pltpu
from jax.sharding import PartitionSpec as P

SLIDES = 3
LANES = 128
PAD = 8
ANY = pl.BlockSpec(memory_space=pl.ANY)
BF = jnp.bfloat16
F32 = jnp.float32
VMEM_BYTES = 20 * 1024 * 1024
COSTS = {"spots": 1, "back3": 1, "waits2": 3, "addx1": 9, "half0": 3}
WIDTHS = (128, 128, 128, 128)
GROUPS = ((0, 1), (2,), (3,))
SUMS = ((0,), (1, 2))
ORDER = (
    "Y0 e0 Y1 w:ez1+ez2+ez3",
    "Y2 A0 a0 e3",
    "b0 A1 Y3 w:f20+f30+n0",
    "a1 A2 w:f21+f31+n1 a2",
    "S0 A3 w:f22+f32+n2 a3",
    "S1 w:s0 S2 w:s1",
    "F0 w:f23+f33+n3 S3 f0",
    "P0 w:s2 F1 f1",
    "P1 F2 Q0 G2",
    "P2 X1 Q1 U0",
    "m0 R1 R0",
)


def sds(shape, dtype):
    return jax.ShapeDtypeStruct(shape, dtype)


def whole(shape):
    zeros = (0,) * len(shape)
    return pl.BlockSpec(shape, lambda *_: zeros)


def xor_pairs(size, step):
    return [(n, n ^ step) for n in range(size)]


class Chain:
    def __init__(self, flags):
        self.flags = flags
        self.token = jnp.zeros((8, LANES), F32)

    def run(self, name, body, ins=(), outs=(), after=(), through=(), grid=(1,), scratch=()):
        ins = [*ins, *((a, ANY) for a in after)]
        carried = (*through, self.token)
        n_in, n_out, n_thr = len(ins), len(outs), len(carried)

        def kernel(flags, *refs):
            in_refs = refs[:n_in]
            out_refs = refs[n_in + n_thr : n_in + 2 * n_thr + n_out - 1]
            scratch_refs = refs[n_in + 2 * n_thr + n_out :]
            if body is not None:
                body(flags, in_refs, out_refs, *scratch_refs)

        results = pl.pallas_call(
            kernel,
            out_shape=[s for s, _ in outs] + [sds(a.shape, a.dtype) for a in carried],
            grid_spec=pltpu.PrefetchScalarGridSpec(
                num_scalar_prefetch=1,
                grid=grid,
                in_specs=[s for _, s in ins] + [ANY] * n_thr,
                out_specs=[s for _, s in outs] + [ANY] * n_thr,
                scratch_shapes=list(scratch),
            ),
            input_output_aliases={1 + n_in + j: n_out + j for j in range(n_thr)},
            compiler_params=pltpu.CompilerParams(vmem_limit_bytes=VMEM_BYTES),
            cost_estimate=pl.CostEstimate(flops=COSTS.get(name, 0) * 10**9, bytes_accessed=0, transcendentals=0),
            name=name,
        )(self.flags, *[a for a, _ in ins], *carried)
        self.token = results[-1]
        return results[:-1]


def copy_all(copies, sems):
    made = [(c, pltpu.make_async_copy(s, d, sems.at[n])) for n, (c, s, d) in enumerate(copies)]
    for act in ("start", "wait"):
        for cond, copy in made:
            if cond is None:
                getattr(copy, act)()
            else:
                pl.when(cond)(getattr(copy, act))


def column(row):
    return jnp.transpose(jnp.broadcast_to(row, (LANES, row.shape[1])))


def per_device(sizes, logits, expression, spatial, slide_ids, spot_mask, densities):
    spot_size = sizes["spot"]
    rows, spots = logits.shape
    genes = spatial.shape[1]
    spots_all = spots * spot_size
    genes_all = genes * sizes["gene"]
    slots = sizes["gene"]
    quarter = spots // sizes["cell"]
    half = rows // 2
    cell, spot, gene = (lax.axis_index(a) for a in ("cell", "spot", "gene"))
    home = (gene // 2 == spot).astype(jnp.int32)
    side = (gene % 2).astype(jnp.int32)
    chain = Chain(jnp.stack([home, side, cell, gene, spot]).astype(jnp.int32))
    run = chain.run
    offsets = [sum(WIDTHS[:n]) for n in range(len(WIDTHS))]
    chunks = range(len(WIDTHS))
    group_width = [sum(WIDTHS[c] for c in g) for g in GROUPS]

    def over_core(v):
        return lax.ppermute(v, "cell", xor_pairs(4, 1))

    def over_x(v):
        return lax.ppermute(v, "cell", xor_pairs(4, 2))

    def over_gene(v, step):
        return lax.ppermute(v, "gene", xor_pairs(4, step))

    def over_spot(v, step=1):
        return lax.ppermute(v, "spot", xor_pairs(spot_size, step))

    def sum_spot(v):
        step = 1
        while step < spot_size:
            v = v + over_spot(v, step)
            step *= 2
        return v

    ids_row, mask_row = slide_ids.reshape(1, spots), spot_mask.reshape(1, spots)
    dens_row = densities.reshape(1, rows)

    expr = expression.reshape(2, half * 2, genes) if spot_size == 2 else None
    st, sent = {}, {}

    def start_swap(c):
        w = WIDTHS[c]
        if c == 0:
            sent["y0"] = over_spot(expr[:, :, :w])
            return

        def body(fl, i, out, sems):
            copy_all([(None, i[0].at[p, :, pl.ds(offsets[c], w)], out[0].at[p]) for p in range(2)], sems)

        shape = (2, rows, w)
        (v,) = run(
            f"swap{c}", body, [(expr, pl.BlockSpec(memory_space=pltpu.HBM))], [(sds(shape, BF), whole(shape))],
            scratch=[pltpu.SemaphoreType.DMA((2,))],
        )
        sent[f"y{c}"] = over_spot(v)

    def start_along(c):
        w, o = WIDTHS[c], offsets[c] // WIDTHS[c]
        blk, one = (1, half, w), (half, w)

        def body(fl, i, out):
            @pl.when(fl[0] == 1)
            def _():
                out[0][...] = i[0][0]
                out[1][...] = i[1][0]
                out[2][0] = i[2][0]
                out[2][1] = i[3][0]

            @pl.when(fl[0] == 0)
            def _():
                out[0][...] = i[4][0]
                out[1][...] = i[5][0]
                out[2][0] = i[6][0]
                out[2][1] = i[7][0]

        def at(same, part, col):
            return pl.BlockSpec(blk, lambda g, f: (f[1] if same else 1 - f[1], part, col))

        y = sent[f"y{c}"]
        ins = [(y, at(True, 0, 0)), (y, at(False, 0, 0)), (expr, at(False, 0, o)), (expr, at(False, 1, o))]
        ins += [(expr, at(True, 1, o)), (expr, at(False, 1, o)), (y, at(False, 0, 0)), (y, at(False, 1, 0))]
        outs = [(sds(one, BF), whole(one))] * 2 + [(sds((2, half, w), BF), whole((2, half, w)))]
        st["along", c] = run(f"along{c}", body, ins, outs)

    def along_send(c):
        a, b, n = run(f"alongsend{c}", None, through=st["along", c])
        sent[f"f2{c}"], sent[f"f3{c}"], sent[f"n{c}"] = over_gene(a, 2), over_gene(b, 3), over_gene(n, 1)

    def start_back(c):
        w = WIDTHS[c]

        def body(fl, i, out):
            out[0][0] = i[0][...]
            out[0][1] = i[1][...]

        one = whole((half, w))
        (st["f", c],) = run(
            f"back{c}", body, [(sent[f"f2{c}"], one), (sent[f"f3{c}"], one)], [(sds((2, half, w), BF), whole((2, half, w)))],
        )
        sent[f"s{c}"] = over_spot(st["f", c])

    def wait_for(name):
        run("wait" + name.split("+")[0], None, after=[sent[n] for n in name.split("+")])

    def members_of(_):
        def body(fl, i, out):
            ids, valid = column(i[0][...].astype(F32)), column(i[1][...].astype(F32))
            lane = lax.broadcasted_iota(jnp.int32, (quarter, LANES), 1)
            inside = (lane < SLIDES) & (lane.astype(F32) == ids) & (valid == 1.0)
            out[0][...] = jnp.where(inside, 1.0, jnp.where(lane == SLIDES, valid, 0.0))

        row, tall = pl.BlockSpec((1, quarter), lambda g, f: (0, f[2])), whole((quarter, LANES))
        (st["member"],) = run("member", body, [(ids_row, row), (mask_row, row)], [(sds((quarter, LANES), F32), tall)])

    def totals(n):
        sp = whole((8, spots))
        if n == 0:

            def body(fl, i, out):
                out[0][...] = jnp.zeros((8, spots), F32)
                out[0][0:1, :] = jnp.sum(jnp.exp(i[0][...].astype(F32)), axis=0, keepdims=True)
                out[0][1:2, :] = jnp.broadcast_to(jnp.sum(i[1][...]), (1, spots))

            ins = [(logits, whole(logits.shape)), (dens_row, whole(dens_row.shape))]
            (v,) = run("totals", body, ins, [(sds((8, spots), F32), sp)])
            st["tot"] = lax.psum(v, "cell")
            for s in (1, 2, 3):
                sent[f"ez{s}"] = over_gene(st["tot"], s)
        else:
            blk = 2 * LANES

            def body(fl, i, out):
                tot = (i[1][...] + i[2][...]) + (i[3][...] + i[4][...])
                out[3][...] = tot
                inv = 1.0 / tot[0:1, :]
                log_tot = jnp.log(tot[0:1, :])
                vals = i[0][...].astype(F32)
                prob = jnp.exp(vals) * inv
                prob_t = jnp.transpose(prob.astype(BF))
                for q in range(sizes["cell"]):
                    at = pl.multiple_of((fl[2] ^ q) * quarter, quarter)
                    out[0][pl.ds(at, quarter), :] = prob_t[q * quarter : (q + 1) * quarter]
                folded = sum(prob[:, n : n + LANES] for n in range(0, spots, LANES))
                row_sums = jnp.sum(jnp.transpose(folded), axis=0, keepdims=True)
                out[1][...] = jnp.broadcast_to(row_sums, (8, blk))

                @pl.when(pl.program_id(0) == 0)
                def _():
                    out[2][...] = jnp.zeros((8, spots), F32)

                out[2][0:1, :] -= jnp.sum(prob * (vals - log_tot), axis=0, keepdims=True)

            parts = [st["tot"]] + [sent[f"ez{s}"] for s in (1, 2, 3)]
            pt, mass, ent, st["tot"] = run(
                "prob", body,
                [(logits, pl.BlockSpec((blk, spots), lambda g, f: (g, 0)))] + [(a, sp) for a in parts],
                [
                    (sds((spots, rows), BF), pl.BlockSpec((spots, blk), lambda g, f: (0, g))),
                    (sds((8, rows), F32), pl.BlockSpec((8, blk), lambda g, f: (0, g))),
                    (sds((8, spots), F32), sp),
                    (sds((8, spots), F32), sp),
                ],
                grid=(rows // blk,),
            )
            st["pt"], st["ent"] = pt, ent
            st["mass"] = mass if spot_size == 2 else sum_spot(mass)
            if spot_size == 2:
                sent["my"] = over_spot(mass)

    def shares(_):
        masses = [st["mass"]] + ([sent["my"]] if spot_size == 2 else [])

        def body(fl, i, out):
            mass = i[2][0:1, :]
            for extra in i[3:]:
                mass = mass + extra[0:1, :]
            share = i[0][...] / i[1][1:2, 0:1]
            out[0][...] = column(share / mass)
            kl = jnp.sum(share * (jnp.log(share) - jnp.log(mass / spots_all)))
            out[1][...] = jnp.broadcast_to(kl, (8, LANES))

        st["sm"], st["kl"] = run(
            "shares", body,
            [(dens_row, whole(dens_row.shape)), (st["tot"], whole((8, spots)))]
            + [(m, whole((8, rows))) for m in masses],
            [(sds((rows, LANES), F32), whole((rows, LANES))), (sds((8, LANES), F32), whole((8, LANES)))],
        )

    def halves_of(g):
        shape = (quarter, slots * group_width[g])
        return [(sds(shape, F32), whole(shape))] * 2

    def forward(g):
        members, wide_all = GROUPS[g], group_width[g] * slots
        shape = (2, quarter, wide_all)
        outs = [(sds((rows, slots * WIDTHS[c]), BF), whole((rows, slots * WIDTHS[c]))) for c in members]
        outs += [(sds(shape, F32), whole(shape))]
        outs += halves_of(g)

        late = members[-1] if spot_size == 2 and g == len(GROUPS) - 1 else None

        def product(pt, efs, keep, *send, direct=None):
            done = 0
            low, high = send
            for c, ef in zip(members, efs):
                w = WIDTHS[c]
                if c == late:
                    near = jnp.dot(pt[...], ef[:, : 2 * w], preferred_element_type=F32)
                    at = pl.ds(pl.multiple_of(direct, LANES), half)
                    far = jnp.dot(pt[:, at], ef[at, 2 * w :], preferred_element_type=F32)
                    acc = jnp.concatenate([near, far], axis=1)
                else:
                    acc = jnp.dot(pt[...], ef[...], preferred_element_type=F32)
                for q, ref in enumerate((keep.at[0], low, keep.at[1], high)):
                    rows_q = acc[q * quarter : (q + 1) * quarter]
                    for s in range(slots):
                        base = s * group_width[g] + done
                        ref[:, base : base + w] = rows_q[:, s * w : (s + 1) * w]
                done += w

        if spot_size == 2:

            def body(fl, i, out, sems):
                pt, e = i[:2]
                at_home, away = fl[0] == 1, fl[0] == 0
                top, low = pl.ds(0, half), pl.ds(half, half)
                copies = []
                for m, c in enumerate(members):
                    w, ef = WIDTHS[c], out[m]
                    y, n, f = i[2 + 4 * m : 5 + 4 * m]
                    copies += [
                        (at_home, e.at[fl[1], :, pl.ds(offsets[c], w)], ef.at[:, pl.ds(0, w)]),
                        (away, y.at[fl[1]], ef.at[:, pl.ds(0, w)]),
                        (None, n.at[0], ef.at[top, pl.ds(w, w)]),
                        (None, n.at[1], ef.at[low, pl.ds(w, w)]),
                    ]
                    for part in (0, 1):
                        cols = pl.ds((2 + part) * w, w)
                        copies += [(at_home, f.at[part], ef.at[low, cols]), (away, f.at[part], ef.at[top, cols])]
                        if c != late:
                            s = i[5 + 4 * m]
                            copies += [(at_home, s.at[part], ef.at[top, cols]), (away, s.at[part], ef.at[low, cols])]
                copy_all(copies, sems)
                product(pt, out[: len(members)], *out[len(members) :], direct=fl[0] * half)

            ins = [(st["pt"], whole((spots, rows))), (expr, ANY)]
            ins += [
                (a, ANY)
                for c in members
                for a in (sent[f"y{c}"], sent[f"n{c}"], st["f", c], *([] if c == late else [sent[f"s{c}"]]))
            ]
            scratch = [pltpu.SemaphoreType.DMA((12 * len(members),))]
        else:

            def body(fl, i, out):
                for m, c in enumerate(members):
                    w = WIDTHS[c]
                    for s in range(slots):
                        out[m][:, s * w : (s + 1) * w] = i[1 + m * slots + s][...]
                product(i[0], out[: len(members)], *out[len(members) :])

            def at_chunk(c):
                return pl.BlockSpec((rows, WIDTHS[c]), lambda *_: (0, offsets[c] // WIDTHS[c]))

            ins = [(st["pt"], whole((spots, rows)))] + [(a, at_chunk(c)) for c in members for a in st["pieces"]]
            scratch = []
        results = run(f"forward{g}", body, ins, outs, scratch=scratch)
        for c, ef in zip(members, results):
            st["e", c] = ef
        st["r", g], st["send", g] = results[len(members)], results[len(members) + 1 :]

    def forward_late(g):
        c = GROUPS[g][-1]
        w, wide = WIDTHS[c], slots * group_width[g]
        shape = (2, quarter, wide)

        def body(fl, i, out, sems):
            pt, swapped, keep, low, high = i
            at = pl.ds(pl.multiple_of((1 - fl[0]) * half, LANES), half)
            copy_all([(None, swapped.at[n], out[3].at[at, pl.ds((2 + n) * w, w)]) for n in (0, 1)], sems)
            both = jnp.concatenate([swapped[0], swapped[1]], axis=1)
            acc = jnp.dot(pt[:, at], both, preferred_element_type=F32)
            for new, old in zip(out, (keep, low, high)):
                new[...] = old[...]
            for q, ref in enumerate((out[0].at[0], out[1], out[0].at[1], out[2])):
                for n in (0, 1):
                    base = (3 + n) * group_width[g] - w
                    ref[:, base : base + w] += acc[q * quarter : (q + 1) * quarter, n * w : (n + 1) * w]

        one = whole((quarter, wide))
        ins = [(st["pt"], whole((spots, rows))), (sent[f"s{c}"], whole((2, half, w)))]
        ins += [(st["r", g], whole(shape))] + [(a, one) for a in st["send", g]]
        st["r", g], *send, st["e", c] = run(
            f"forwardlate{g}", body, ins, [(sds(shape, F32), whole(shape)), *halves_of(g)], through=[st["e", c]],
            scratch=[pltpu.SemaphoreType.DMA((2,))],
        )
        send_core(g, send)

    def send_core(g, send):
        for n, part in enumerate(send):
            sent[f"rc{n}{g}"] = over_core(part)

    def forward_send(g):
        send_core(g, run(f"send{g}", None, through=st["send", g]))

    def reduce_core(g):
        wide = slots * group_width[g]
        shape, one = (2, quarter, wide), (quarter, wide)

        single = len(GROUPS[g]) == 1

        def body(fl, i, out):
            for n in (0, 1):
                out[n][0:quarter, :] = i[0][n] + i[1 + n][...]
            if single:
                out[1][quarter:, :] = jnp.zeros((PAD, wide), F32)

        ins = [(st["r", g], whole(shape))]
        ins += [(sent[f"rc{n}{g}"], whole(one)) for n in (0, 1)]
        more = (quarter + PAD, wide) if single else one
        st["r", g], b = run(f"core{g}", body, ins, [(sds(one, F32), whole(one)), (sds(more, F32), whole(more))])
        sent[f"rx{g}"] = over_x(b)

    sum_groups = [[g for g in z] for z in SUMS]
    sum_width = [sum(group_width[g] for g in z) for z in SUMS]

    def add_x(g):
        one = whole((quarter, slots * group_width[g]))

        def body(fl, i, out):
            out[0][...] = i[0][...] + i[1][0:quarter, :]

        ins = [(st["r", g], one), (sent[f"rx{g}"], whole(sent[f"rx{g}"].shape))]
        (st["added", g],) = run(f"addx{g}", body, ins, [(sds(one.block_shape, F32), one)])

    def reduce_x(z):
        members, w = sum_groups[z], sum_width[z]
        part = (quarter, w)
        in_halves = z < len(SUMS) - 1

        def body(fl, i, out):
            done, i = 0, list(i)
            for g in members:
                v = group_width[g]
                refs = [i.pop(0) for _ in parts_of[g]]
                for s in range(slots):
                    at = slice(s * v, (s + 1) * v)
                    value = sum(ref[0:quarter, at] for ref in refs)
                    if in_halves and s >= 2:
                        out[2][s - 2, 0:quarter, done : done + v] = value
                    else:
                        out[s][:, done : done + v] = value
                done += v
            if in_halves:
                out[2][:, quarter:, :] = jnp.zeros((2, PAD, w), F32)

        parts_of = {g: [st["added", g]] if ("added", g) in st else [st["r", g], sent[f"rx{g}"]] for g in members}
        ins = [(a, whole(a.shape)) for g in members for a in parts_of[g]]
        outs = [(sds(part, F32), whole(part))] * (2 if in_halves else slots)
        if in_halves:
            padded = (2, quarter + PAD, w)
            outs += [(sds(padded, F32), whole(padded))]
        parts = run(f"x{z}", body, ins, outs)
        if in_halves:
            st["z", z] = parts[:2]
            sent[f"rz2{z}"] = over_gene(parts[2], 2)
        else:
            st["z", z] = parts[:1]
            for s in (1, 2, 3):
                sent[f"rz{s}{z}"] = over_gene(parts[s], s)

    def reduce_half(z):
        part = (quarter, sum_width[z])

        def body(fl, i, out):
            for n in (0, 1):
                out[n][...] = i[n][...] + i[2][n, 0:quarter, :]

        ins = [(a, whole(part)) for a in st["z", z]] + [(sent[f"rz2{z}"], whole((2, quarter + PAD, sum_width[z])))]
        a, b = run(f"half{z}", body, ins, [(sds(part, F32), whole(part))] * 2)
        st["z", z], sent[f"rz1{z}"] = [a], over_gene(b, 1)

    def reduce_gene(z):
        part = (quarter, sum_width[z])
        others = [sent[f"rz{s}{z}"] for s in ((1,) if z < len(SUMS) - 1 else (1, 2, 3))]

        def body(fl, i, out):
            out[0][...] = sum(ref[...] for ref in i)

        ins = [(a, whole(part)) for a in (*st["z", z], *others)]
        (st["sum", z],) = run(f"gene{z}", body, ins, [(sds(part, F32), whole(part))])

    steps = {
        "Y": start_swap, "A": start_along, "a": along_send, "S": start_back,
        "e": totals, "m": shares, "F": forward, "f": forward_send, "G": forward_late, "b": members_of,
        "P": reduce_core, "X": add_x, "Q": reduce_x,
        "U": reduce_half, "R": reduce_gene,
    }
    if spot_size != 2:
        full = lax.all_gather(expression, "spot", axis=0, tiled=True).reshape(slots, rows, genes)
        pieces = [lax.dynamic_index_in_dim(full, gene ^ s, 0, False) for s in range(slots)]
        st["pieces"] = [pieces[0]] + [over_gene(pieces[s], s) for s in (1, 2, 3)]
    for word in " ".join(ORDER).split():
        if word[:2] == "w:":
            if spot_size == 2 or word == "w:ez1+ez2+ez3":
                wait_for(word[2:])
        elif spot_size != 2 and word[0] == "G":
            forward_send(int(word[1]))
        elif spot_size == 2 or word[0] not in "YAaS":
            steps[word[0]](int(word[1]))

    n_ch, n_sum = len(WIDTHS), len(SUMS)
    starts = [offsets[GROUPS[z[0]][0]] for z in SUMS]
    preds = [(st["sum", z], whole((quarter, sum_width[z]))) for z in range(n_sum)]
    mine = (spatial, pl.BlockSpec((quarter, genes), lambda g, f: (f[2], 0)))
    memb = (st["member"], whole((quarter, LANES)))
    gene_spec, spot_spec = whole((16, genes)), whole((8, quarter))

    def stats_body(fl, i, out):
        memb = i[0]
        cols = [jnp.broadcast_to(memb[:, k : k + 1], (quarter, LANES)) for k in range(SLIDES)]
        valid = jnp.sum(memb[:, SLIDES : SLIDES + 1])
        out[0][...] = jnp.broadcast_to(valid, (16, genes))
        totals = [jnp.zeros((quarter, LANES), F32) for _ in range(3)]
        for g in range(n_sum):
            for o in range(0, sum_width[g], LANES):
                at = slice(starts[g] + o, starts[g] + o + LANES)
                pr, ta = i[2 + g][:, o : o + LANES], i[1][:, at].astype(F32)
                for j, v in enumerate((pr * ta, pr * pr, ta * ta)):
                    totals[j] += v
                    for k in range(SLIDES):
                        n = 3 * j + k
                        out[0][n : n + 1, at] = jnp.sum(cols[k] * v, axis=0, keepdims=True)
        out[1][...] = jnp.zeros((8, quarter), F32)
        for j in range(3):
            out[1][j : j + 1, :] = jnp.sum(jnp.transpose(totals[j]), axis=0, keepdims=True)

    gene_sums, spot_sums = run(
        "stats", stats_body, [memb, mine, *preds],
        [(sds((16, genes), F32), gene_spec), (sds((8, quarter), F32), spot_spec)],
    )
    spot_parts = [spot_sums] + [over_gene(spot_sums, s) for s in (1, 2, 3)]
    gene_sums = gene_sums + over_core(gene_sums)
    gene_sums = gene_sums + over_x(gene_sums)
    gene_parts = [gene_sums, over_spot(gene_sums)] if spot_size == 2 else [sum_spot(gene_sums)]

    run("spots", None, after=spot_parts)

    def grads_body(fl, i, out):
        memb, ta_ref, kl, ent = i[:4]
        i = i[4:]
        spot_in, gene_in, preds_in = i[:4], i[4 : 4 + len(gene_parts)], i[4 + len(gene_parts) :]
        scale = -1.0 / (SLIDES * genes_all)
        sums = sum(ref[...] for ref in gene_in)
        num, psq, tsq = sums[0:3], sums[3:6], sums[6:9]
        p_floor, t_floor = jnp.maximum(psq, 1.0), jnp.maximum(tsq, 1.0)
        root = jnp.sqrt(p_floor * t_floor)
        cosine = num / root
        w_t = scale / root
        w_p = jnp.where(psq > 1.0, -scale * cosine / p_floor, 0.0)
        valid_total = jnp.maximum(sums[9, 0], 1.0)
        spot_all = (spot_in[0][...] + spot_in[1][...]) + (spot_in[2][...] + spot_in[3][...])
        s_num, s_p, s_t = [column(spot_all[n : n + 1, :]) for n in range(3)]
        s_p, s_t = s_p + 1e-06, s_t + 1e-06
        root = jnp.sqrt(s_p * s_t)
        cos_spot = s_num / root
        valid = jnp.broadcast_to(memb[:, SLIDES : SLIDES + 1], (quarter, LANES))
        coef = -valid / valid_total
        coef_t, coef_p = coef / root, -coef * cos_spot / s_p
        first = [(fl[n] == 0).astype(F32) for n in (2, 4, 3)]
        terms = [
            jnp.sum(cosine) * first[0] * first[1],
            jnp.sum((valid * cos_spot)[:, 0:1]) * first[2],
            kl[0, 0] * first[1],
            jnp.sum(ent[0:1, :]),
            valid_total * first[0] * first[1] * first[2],
        ]
        lane = lax.broadcasted_iota(jnp.int32, (8, spots), 1)
        value = jnp.zeros((8, spots), F32)
        for n, term in enumerate(terms):
            value = jnp.where(lane == n, term, value)
        out[1][...] = value
        cols = [jnp.broadcast_to(memb[:, k : k + 1], (quarter, LANES)) for k in range(SLIDES)]
        for g in range(n_sum):
            for o in range(0, sum_width[g], LANES):
                at = slice(starts[g] + o, starts[g] + o + LANES)
                f_t, f_p = coef_t, coef_p
                for k in range(SLIDES):
                    f_t = f_t + cols[k] * w_t[k : k + 1, at]
                    f_p = f_p + cols[k] * w_p[k : k + 1, at]
                out[0][:, at] = (f_t * ta_ref[:, at].astype(F32) + f_p * preds_in[g][:, o : o + LANES]).astype(BF)

    row8, flat = whole((8, spots)), whole((8, LANES))
    ins = [memb, mine, (st["kl"], flat), (st["ent"], row8)]
    ins += [(a, spot_spec) for a in spot_parts] + [(a, gene_spec) for a in gene_parts] + preds
    grad, terms = run(
        "grads", grads_body, ins,
        [(sds((quarter, genes), BF), whole((quarter, genes))), (sds((8, spots), F32), row8)],
    )
    terms = [terms, over_spot(terms)] if spot_size == 2 else [sum_spot(terms)]
    grad_x = over_x(grad)
    others = [over_gene(grad, s) for s in (1, 2, 3)]
    one, rest = (quarter, genes), (slots - 1, quarter, genes)

    def gather_body(fl, i, out):
        for n in range(slots - 1):
            out[0][n] = i[n][...]

    (rest_z,) = run(
        "gather", gather_body, [(a, whole(one)) for a in others], [(sds(rest, BF), whole(rest))], after=[grad_x]
    )
    rest_x = over_x(rest_z)
    grads = [grad, over_core(grad), grad_x, over_core(grad_x), rest_z, over_core(rest_z), rest_x, over_core(rest_x)]

    row_blk = rows // 4

    def backward_body(fl, i, out, held, sems):
        lg, tot, sm = i[:3]
        efs, gs, terms = i[3 : 3 + n_ch], i[3 + n_ch : 11 + n_ch], i[11 + n_ch :]

        @pl.when(pl.program_id(0) == 0)
        def _():
            row = lax.broadcasted_iota(jnp.int32, (8, spots), 0)
            out[1][...] = jnp.where(row == 0, 0.0, sum(ref[...] for ref in terms))
            copies = []
            for b in range(sizes["cell"]):
                at = pl.ds(pl.multiple_of((fl[2] ^ b) * quarter, quarter), quarter)
                copies.append((None, gs[b], held.at[0, at, :]))
                copies.append((None, gs[4 + b], held.at[pl.ds(1, slots - 1), at, :]))
            copy_all(copies, sems)

        acc = -jnp.broadcast_to(sm[:, 0:1], (row_blk, spots))
        for s in range(slots):
            left = jnp.concatenate([ef[:, s * w : (s + 1) * w] for w, ef in zip(WIDTHS, efs)], axis=1)
            acc += lax.dot_general(left, held[s], (((1,), (1,)), ((), ())), preferred_element_type=F32)
        out[0][...] = acc
        prob = jnp.exp(lg[...].astype(F32)) * (1.0 / tot[0:1, :])
        out[1][0:1, :] += jnp.sum(prob * acc, axis=0, keepdims=True)

    def by_rows(width, size=row_blk):
        return pl.BlockSpec((size, width), lambda g, f: (g, 0))

    ins = [(logits, by_rows(spots)), (st["tot"], row8), (st["sm"], by_rows(LANES))]
    ins += [(st["e", c], by_rows(slots * WIDTHS[c])) for c in chunks]
    ins += [(a, ANY) for a in grads] + [(a, row8) for a in terms]
    grad_probs, v = run(
        "backward", backward_body, ins,
        [(sds((rows, spots), F32), by_rows(spots)), (sds((8, spots), F32), row8)],
        grid=(rows // row_blk,),
        scratch=[pltpu.VMEM((slots, spots, genes), BF), pltpu.SemaphoreType.DMA((len(grads),))],
    )

    v = v + over_core(v)
    v = v + over_x(v)
    v = (v + over_gene(v, 1)) + (over_gene(v, 2) + over_gene(v, 3))

    def final_body(fl, i, out):
        prob = jnp.exp(i[0][...].astype(F32)) * (1.0 / i[1][0:1, :])
        out[0][...] = prob * (i[2][...] - i[3][0:1, :])

        @pl.when(pl.program_id(0) == 0)
        def _():
            sums = [i[3][1, n] for n in range(5)]
            gene_term, spot_term = sums[0] / (SLIDES * genes_all), sums[1] / sums[4]
            divergence, entropy = sums[2], sums[3] / spots_all
            values = (divergence - gene_term - spot_term, gene_term, spot_term, divergence, entropy)
            for n, value in enumerate(values):
                out[1][n] = value

    last_blk = rows // 2
    blk = by_rows(spots, last_blk)
    grad_logits, loss_terms = run(
        "final", final_body, [(logits, blk), (st["tot"], row8), (grad_probs, blk), (v, row8)],
        [(sds((rows, spots), F32), blk), (sds((5,), F32), pl.BlockSpec(memory_space=pltpu.SMEM))],
        grid=(rows // last_blk,),
    )
    return (loss_terms, grad_logits)


def solution(mesh):
    return jax.shard_map(
        functools.partial(per_device, dict(mesh.shape)),
        mesh=mesh,
        in_specs=(
            P(("cell", "gene"), "spot"),
            P(("cell", "spot"), "gene"),
            P("spot", "gene"),
            P("spot"),
            P("spot"),
            P(("cell", "gene")),
        ),
        out_specs=(P(), P(("cell", "gene"), "spot")),
        check_vma=False,
    )
```

```python
import functools
import jax
import jax.numpy as jnp
from jax import lax
from jax.experimental import pallas as pl
from jax.experimental.pallas import tpu as pltpu
from jax.sharding import PartitionSpec as P

SLIDES = 3
LANES = 128
PAD = 8
ANY = pl.BlockSpec(memory_space=pl.ANY)
BF = jnp.bfloat16
F32 = jnp.float32
VMEM_BYTES = 14 * 1024 * 1024
COSTS = {"spots": 1, "back3": 1, "waits2": 3, "addx1": 9, "half0": 3}
WIDTHS = (128, 128, 128, 128)
GROUPS = ((0, 1), (2,), (3,))
SUMS = ((0,), (1, 2))
ORDER = (
    "Y0 e0 Y1 w:ez1+ez2+ez3",
    "Y2 A0 a0 e3",
    "b0 A1 Y3 w:f20+f30+n0",
    "a1 A2 w:f21+f31+n1 a2",
    "S0 A3 w:f22+f32+n2 a3",
    "S1 w:s0 S2 w:s1",
    "F0 w:f23+f33+n3 S3 f0",
    "P0 w:s2 F1 f1",
    "P1 F2 Q0 G2",
    "P2 X1 Q1 U0",
    "m0 R1 R0",
)


def sds(shape, dtype):
    return jax.ShapeDtypeStruct(shape, dtype)


def whole(shape):
    zeros = (0,) * len(shape)
    return pl.BlockSpec(shape, lambda *_: zeros)


def xor_pairs(size, step):
    return [(n, n ^ step) for n in range(size)]


class Chain:
    def __init__(self, flags):
        self.flags = flags
        self.token = jnp.zeros((8, LANES), F32)

    def run(self, name, body, ins=(), outs=(), after=(), through=(), grid=(1,), scratch=()):
        ins = [*ins, *((a, ANY) for a in after)]
        carried = (*through, self.token)
        n_in, n_out, n_thr = len(ins), len(outs), len(carried)

        def kernel(flags, *refs):
            in_refs = refs[:n_in]
            out_refs = refs[n_in + n_thr : n_in + 2 * n_thr + n_out - 1]
            scratch_refs = refs[n_in + 2 * n_thr + n_out :]
            if body is not None:
                body(flags, in_refs, out_refs, *scratch_refs)

        results = pl.pallas_call(
            kernel,
            out_shape=[s for s, _ in outs] + [sds(a.shape, a.dtype) for a in carried],
            grid_spec=pltpu.PrefetchScalarGridSpec(
                num_scalar_prefetch=1,
                grid=grid,
                in_specs=[s for _, s in ins] + [ANY] * n_thr,
                out_specs=[s for _, s in outs] + [ANY] * n_thr,
                scratch_shapes=list(scratch),
            ),
            input_output_aliases={1 + n_in + j: n_out + j for j in range(n_thr)},
            compiler_params=pltpu.CompilerParams(vmem_limit_bytes=VMEM_BYTES),
            cost_estimate=pl.CostEstimate(flops=COSTS.get(name, 0) * 10**9, bytes_accessed=0, transcendentals=0),
            name=name,
        )(self.flags, *[a for a, _ in ins], *carried)
        self.token = results[-1]
        return results[:-1]


def copy_all(copies, sems):
    made = [(c, pltpu.make_async_copy(s, d, sems.at[n])) for n, (c, s, d) in enumerate(copies)]
    for act in ("start", "wait"):
        for cond, copy in made:
            if cond is None:
                getattr(copy, act)()
            else:
                pl.when(cond)(getattr(copy, act))


def column(row):
    return jnp.transpose(jnp.broadcast_to(row, (LANES, row.shape[1])))


def per_device(sizes, logits, expression, spatial, slide_ids, spot_mask, densities):
    spot_size = sizes["spot"]
    rows, spots = logits.shape
    genes = spatial.shape[1]
    spots_all = spots * spot_size
    genes_all = genes * sizes["gene"]
    slots = sizes["gene"]
    quarter = spots // sizes["cell"]
    half = rows // 2
    cell, spot, gene = (lax.axis_index(a) for a in ("cell", "spot", "gene"))
    home = (gene // 2 == spot).astype(jnp.int32)
    side = (gene % 2).astype(jnp.int32)
    chain = Chain(jnp.stack([home, side, cell, gene, spot]).astype(jnp.int32))
    run = chain.run
    offsets = [sum(WIDTHS[:n]) for n in range(len(WIDTHS))]
    chunks = range(len(WIDTHS))
    group_width = [sum(WIDTHS[c] for c in g) for g in GROUPS]

    def over_core(v):
        return lax.ppermute(v, "cell", xor_pairs(4, 1))

    def over_x(v):
        return lax.ppermute(v, "cell", xor_pairs(4, 2))

    def over_gene(v, step):
        return lax.ppermute(v, "gene", xor_pairs(4, step))

    def over_spot(v, step=1):
        return lax.ppermute(v, "spot", xor_pairs(spot_size, step))

    def sum_spot(v):
        step = 1
        while step < spot_size:
            v = v + over_spot(v, step)
            step *= 2
        return v

    ids_row, mask_row = slide_ids.reshape(1, spots), spot_mask.reshape(1, spots)
    dens_row = densities.reshape(1, rows)

    expr = expression.reshape(2, half * 2, genes) if spot_size == 2 else None
    st, sent = {}, {}

    def start_swap(c):
        w = WIDTHS[c]
        if c == 0:
            sent["y0"] = over_spot(expr[:, :, :w])
            return

        def body(fl, i, out, sems):
            copy_all([(None, i[0].at[p, :, pl.ds(offsets[c], w)], out[0].at[p]) for p in range(2)], sems)

        shape = (2, rows, w)
        (v,) = run(
            f"swap{c}", body, [(expr, pl.BlockSpec(memory_space=pltpu.HBM))], [(sds(shape, BF), whole(shape))],
            scratch=[pltpu.SemaphoreType.DMA((2,))],
        )
        sent[f"y{c}"] = over_spot(v)

    def start_along(c):
        w, o = WIDTHS[c], offsets[c] // WIDTHS[c]
        blk, one = (1, half, w), (half, w)

        def body(fl, i, out):
            @pl.when(fl[0] == 1)
            def _():
                out[0][...] = i[0][0]
                out[1][...] = i[1][0]
                out[2][0] = i[2][0]
                out[2][1] = i[3][0]

            @pl.when(fl[0] == 0)
            def _():
                out[0][...] = i[4][0]
                out[1][...] = i[5][0]
                out[2][0] = i[6][0]
                out[2][1] = i[7][0]

        def at(same, part, col):
            return pl.BlockSpec(blk, lambda g, f: (f[1] if same else 1 - f[1], part, col))

        y = sent[f"y{c}"]
        ins = [(y, at(True, 0, 0)), (y, at(False, 0, 0)), (expr, at(False, 0, o)), (expr, at(False, 1, o))]
        ins += [(expr, at(True, 1, o)), (expr, at(False, 1, o)), (y, at(False, 0, 0)), (y, at(False, 1, 0))]
        outs = [(sds(one, BF), whole(one))] * 2 + [(sds((2, half, w), BF), whole((2, half, w)))]
        st["along", c] = run(f"along{c}", body, ins, outs)

    def along_send(c):
        a, b, n = run(f"alongsend{c}", None, through=st["along", c])
        sent[f"f2{c}"], sent[f"f3{c}"], sent[f"n{c}"] = over_gene(a, 2), over_gene(b, 3), over_gene(n, 1)

    def start_back(c):
        w = WIDTHS[c]

        def body(fl, i, out):
            out[0][0] = i[0][...]
            out[0][1] = i[1][...]

        one = whole((half, w))
        (st["f", c],) = run(
            f"back{c}", body, [(sent[f"f2{c}"], one), (sent[f"f3{c}"], one)], [(sds((2, half, w), BF), whole((2, half, w)))],
        )
        sent[f"s{c}"] = over_spot(st["f", c])

    def wait_for(name):
        run("wait" + name.split("+")[0], None, after=[sent[n] for n in name.split("+")])

    def members_of(_):
        def body(fl, i, out):
            ids, valid = column(i[0][...].astype(F32)), column(i[1][...].astype(F32))
            lane = lax.broadcasted_iota(jnp.int32, (quarter, LANES), 1)
            inside = (lane < SLIDES) & (lane.astype(F32) == ids) & (valid == 1.0)
            out[0][...] = jnp.where(inside, 1.0, jnp.where(lane == SLIDES, valid, 0.0))

        row, tall = pl.BlockSpec((1, quarter), lambda g, f: (0, f[2])), whole((quarter, LANES))
        (st["member"],) = run("member", body, [(ids_row, row), (mask_row, row)], [(sds((quarter, LANES), F32), tall)])

    def totals(n):
        sp = whole((8, spots))
        if n == 0:

            def body(fl, i, out):
                out[0][...] = jnp.zeros((8, spots), F32)
                out[0][0:1, :] = jnp.sum(jnp.exp(i[0][...].astype(F32)), axis=0, keepdims=True)
                out[0][1:2, :] = jnp.broadcast_to(jnp.sum(i[1][...]), (1, spots))

            ins = [(logits, whole(logits.shape)), (dens_row, whole(dens_row.shape))]
            (v,) = run("totals", body, ins, [(sds((8, spots), F32), sp)])
            st["tot"] = lax.psum(v, "cell")
            for s in (1, 2, 3):
                sent[f"ez{s}"] = over_gene(st["tot"], s)
        else:
            blk = 2 * LANES

            def body(fl, i, out):
                tot = (i[1][...] + i[2][...]) + (i[3][...] + i[4][...])
                out[3][...] = tot
                inv = 1.0 / tot[0:1, :]
                log_tot = jnp.log(tot[0:1, :])
                vals = i[0][...].astype(F32)
                prob = jnp.exp(vals) * inv
                prob_t = jnp.transpose(prob.astype(BF))
                for q in range(sizes["cell"]):
                    at = pl.multiple_of((fl[2] ^ q) * quarter, quarter)
                    out[0][pl.ds(at, quarter), :] = prob_t[q * quarter : (q + 1) * quarter]
                folded = sum(prob[:, n : n + LANES] for n in range(0, spots, LANES))
                row_sums = jnp.sum(jnp.transpose(folded), axis=0, keepdims=True)
                out[1][...] = jnp.broadcast_to(row_sums, (8, blk))

                @pl.when(pl.program_id(0) == 0)
                def _():
                    out[2][...] = jnp.zeros((8, spots), F32)

                out[2][0:1, :] -= jnp.sum(prob * (vals - log_tot), axis=0, keepdims=True)

            parts = [st["tot"]] + [sent[f"ez{s}"] for s in (1, 2, 3)]
            pt, mass, ent, st["tot"] = run(
                "prob", body,
                [(logits, pl.BlockSpec((blk, spots), lambda g, f: (g, 0)))] + [(a, sp) for a in parts],
                [
                    (sds((spots, rows), BF), pl.BlockSpec((spots, blk), lambda g, f: (0, g))),
                    (sds((8, rows), F32), pl.BlockSpec((8, blk), lambda g, f: (0, g))),
                    (sds((8, spots), F32), sp),
                    (sds((8, spots), F32), sp),
                ],
                grid=(rows // blk,),
            )
            st["pt"], st["ent"] = pt, ent
            st["mass"] = mass if spot_size == 2 else sum_spot(mass)
            if spot_size == 2:
                sent["my"] = over_spot(mass)

    def shares(_):
        masses = [st["mass"]] + ([sent["my"]] if spot_size == 2 else [])

        def body(fl, i, out):
            mass = i[2][0:1, :]
            for extra in i[3:]:
                mass = mass + extra[0:1, :]
            share = i[0][...] / i[1][1:2, 0:1]
            out[0][...] = column(share / mass)
            kl = jnp.sum(share * (jnp.log(share) - jnp.log(mass / spots_all)))
            out[1][...] = jnp.broadcast_to(kl, (8, LANES))

        st["sm"], st["kl"] = run(
            "shares", body,
            [(dens_row, whole(dens_row.shape)), (st["tot"], whole((8, spots)))]
            + [(m, whole((8, rows))) for m in masses],
            [(sds((rows, LANES), F32), whole((rows, LANES))), (sds((8, LANES), F32), whole((8, LANES)))],
        )

    def halves_of(g):
        shape = (quarter, slots * group_width[g])
        return [(sds(shape, F32), whole(shape))] * 2

    def forward(g):
        members, wide_all = GROUPS[g], group_width[g] * slots
        shape = (2, quarter, wide_all)
        outs = [(sds((rows, slots * WIDTHS[c]), BF), whole((rows, slots * WIDTHS[c]))) for c in members]
        outs += [(sds(shape, F32), whole(shape))]
        outs += halves_of(g)

        late = members[-1] if spot_size == 2 and g == len(GROUPS) - 1 else None

        def product(pt, efs, keep, *send, direct=None):
            done = 0
            low, high = send
            for c, ef in zip(members, efs):
                w = WIDTHS[c]
                if c == late:
                    near = jnp.dot(pt[...], ef[:, : 2 * w], preferred_element_type=F32)
                    at = pl.ds(pl.multiple_of(direct, LANES), half)
                    far = jnp.dot(pt[:, at], ef[at, 2 * w :], preferred_element_type=F32)
                    acc = jnp.concatenate([near, far], axis=1)
                else:
                    acc = jnp.dot(pt[...], ef[...], preferred_element_type=F32)
                for q, ref in enumerate((keep.at[0], low, keep.at[1], high)):
                    rows_q = acc[q * quarter : (q + 1) * quarter]
                    for s in range(slots):
                        base = s * group_width[g] + done
                        ref[:, base : base + w] = rows_q[:, s * w : (s + 1) * w]
                done += w

        if spot_size == 2:

            def body(fl, i, out, sems):
                pt, e = i[:2]
                at_home, away = fl[0] == 1, fl[0] == 0
                top, low = pl.ds(0, half), pl.ds(half, half)
                copies = []
                for m, c in enumerate(members):
                    w, ef = WIDTHS[c], out[m]
                    y, n, f = i[2 + 4 * m : 5 + 4 * m]
                    copies += [
                        (at_home, e.at[fl[1], :, pl.ds(offsets[c], w)], ef.at[:, pl.ds(0, w)]),
                        (away, y.at[fl[1]], ef.at[:, pl.ds(0, w)]),
                        (None, n.at[0], ef.at[top, pl.ds(w, w)]),
                        (None, n.at[1], ef.at[low, pl.ds(w, w)]),
                    ]
                    for part in (0, 1):
                        cols = pl.ds((2 + part) * w, w)
                        copies += [(at_home, f.at[part], ef.at[low, cols]), (away, f.at[part], ef.at[top, cols])]
                        if c != late:
                            s = i[5 + 4 * m]
                            copies += [(at_home, s.at[part], ef.at[top, cols]), (away, s.at[part], ef.at[low, cols])]
                copy_all(copies, sems)
                product(pt, out[: len(members)], *out[len(members) :], direct=fl[0] * half)

            ins = [(st["pt"], whole((spots, rows))), (expr, ANY)]
            ins += [
                (a, ANY)
                for c in members
                for a in (sent[f"y{c}"], sent[f"n{c}"], st["f", c], *([] if c == late else [sent[f"s{c}"]]))
            ]
            scratch = [pltpu.SemaphoreType.DMA((12 * len(members),))]
        else:

            def body(fl, i, out):
                for m, c in enumerate(members):
                    w = WIDTHS[c]
                    for s in range(slots):
                        out[m][:, s * w : (s + 1) * w] = i[1 + m * slots + s][...]
                product(i[0], out[: len(members)], *out[len(members) :])

            def at_chunk(c):
                return pl.BlockSpec((rows, WIDTHS[c]), lambda *_: (0, offsets[c] // WIDTHS[c]))

            ins = [(st["pt"], whole((spots, rows)))] + [(a, at_chunk(c)) for c in members for a in st["pieces"]]
            scratch = []
        results = run(f"forward{g}", body, ins, outs, scratch=scratch)
        for c, ef in zip(members, results):
            st["e", c] = ef
        st["r", g], st["send", g] = results[len(members)], results[len(members) + 1 :]

    def forward_late(g):
        c = GROUPS[g][-1]
        w, wide = WIDTHS[c], slots * group_width[g]
        shape = (2, quarter, wide)

        def body(fl, i, out, sems):
            pt, swapped, keep, low, high = i
            at = pl.ds(pl.multiple_of((1 - fl[0]) * half, LANES), half)
            copy_all([(None, swapped.at[n], out[3].at[at, pl.ds((2 + n) * w, w)]) for n in (0, 1)], sems)
            both = jnp.concatenate([swapped[0], swapped[1]], axis=1)
            acc = jnp.dot(pt[:, at], both, preferred_element_type=F32)
            for new, old in zip(out, (keep, low, high)):
                new[...] = old[...]
            for q, ref in enumerate((out[0].at[0], out[1], out[0].at[1], out[2])):
                for n in (0, 1):
                    base = (3 + n) * group_width[g] - w
                    ref[:, base : base + w] += acc[q * quarter : (q + 1) * quarter, n * w : (n + 1) * w]

        one = whole((quarter, wide))
        ins = [(st["pt"], whole((spots, rows))), (sent[f"s{c}"], whole((2, half, w)))]
        ins += [(st["r", g], whole(shape))] + [(a, one) for a in st["send", g]]
        st["r", g], *send, st["e", c] = run(
            f"forwardlate{g}", body, ins, [(sds(shape, F32), whole(shape)), *halves_of(g)], through=[st["e", c]],
            scratch=[pltpu.SemaphoreType.DMA((2,))],
        )
        send_core(g, send)

    def send_core(g, send):
        for n, part in enumerate(send):
            sent[f"rc{n}{g}"] = over_core(part)

    def forward_send(g):
        send_core(g, run(f"send{g}", None, through=st["send", g]))

    def reduce_core(g):
        wide = slots * group_width[g]
        shape, one = (2, quarter, wide), (quarter, wide)

        single = len(GROUPS[g]) == 1

        def body(fl, i, out):
            for n in (0, 1):
                out[n][0:quarter, :] = i[0][n] + i[1 + n][...]
            if single:
                out[1][quarter:, :] = jnp.zeros((PAD, wide), F32)

        ins = [(st["r", g], whole(shape))]
        ins += [(sent[f"rc{n}{g}"], whole(one)) for n in (0, 1)]
        more = (quarter + PAD, wide) if single else one
        st["r", g], b = run(f"core{g}", body, ins, [(sds(one, F32), whole(one)), (sds(more, F32), whole(more))])
        sent[f"rx{g}"] = over_x(b)

    sum_groups = [[g for g in z] for z in SUMS]
    sum_width = [sum(group_width[g] for g in z) for z in SUMS]

    def add_x(g):
        one = whole((quarter, slots * group_width[g]))

        def body(fl, i, out):
            out[0][...] = i[0][...] + i[1][0:quarter, :]

        ins = [(st["r", g], one), (sent[f"rx{g}"], whole(sent[f"rx{g}"].shape))]
        (st["added", g],) = run(f"addx{g}", body, ins, [(sds(one.block_shape, F32), one)])

    def reduce_x(z):
        members, w = sum_groups[z], sum_width[z]
        part = (quarter, w)
        in_halves = z < len(SUMS) - 1

        def body(fl, i, out):
            done, i = 0, list(i)
            for g in members:
                v = group_width[g]
                refs = [i.pop(0) for _ in parts_of[g]]
                for s in range(slots):
                    at = slice(s * v, (s + 1) * v)
                    value = sum(ref[0:quarter, at] for ref in refs)
                    if in_halves and s >= 2:
                        out[2][s - 2, 0:quarter, done : done + v] = value
                    else:
                        out[s][:, done : done + v] = value
                done += v
            if in_halves:
                out[2][:, quarter:, :] = jnp.zeros((2, PAD, w), F32)

        parts_of = {g: [st["added", g]] if ("added", g) in st else [st["r", g], sent[f"rx{g}"]] for g in members}
        ins = [(a, whole(a.shape)) for g in members for a in parts_of[g]]
        outs = [(sds(part, F32), whole(part))] * (2 if in_halves else slots)
        if in_halves:
            padded = (2, quarter + PAD, w)
            outs += [(sds(padded, F32), whole(padded))]
        parts = run(f"x{z}", body, ins, outs)
        if in_halves:
            st["z", z] = parts[:2]
            sent[f"rz2{z}"] = over_gene(parts[2], 2)
        else:
            st["z", z] = parts[:1]
            for s in (3, 2, 1):
                sent[f"rz{s}{z}"] = over_gene(parts[s], s)

    def reduce_half(z):
        part = (quarter, sum_width[z])

        def body(fl, i, out):
            for n in (0, 1):
                out[n][...] = i[n][...] + i[2][n, 0:quarter, :]

        ins = [(a, whole(part)) for a in st["z", z]] + [(sent[f"rz2{z}"], whole((2, quarter + PAD, sum_width[z])))]
        a, b = run(f"half{z}", body, ins, [(sds(part, F32), whole(part))] * 2)
        st["z", z], sent[f"rz1{z}"] = [a], over_gene(b, 1)

    def reduce_gene(z):
        part = (quarter, sum_width[z])
        others = [sent[f"rz{s}{z}"] for s in ((1,) if z < len(SUMS) - 1 else (1, 2, 3))]

        def body(fl, i, out):
            out[0][...] = sum(ref[...] for ref in i)

        ins = [(a, whole(part)) for a in (*st["z", z], *others)]
        (st["sum", z],) = run(f"gene{z}", body, ins, [(sds(part, F32), whole(part))])

    steps = {
        "Y": start_swap, "A": start_along, "a": along_send, "S": start_back,
        "e": totals, "m": shares, "F": forward, "f": forward_send, "G": forward_late, "b": members_of,
        "P": reduce_core, "X": add_x, "Q": reduce_x,
        "U": reduce_half, "R": reduce_gene,
    }
    if spot_size != 2:
        full = lax.all_gather(expression, "spot", axis=0, tiled=True).reshape(slots, rows, genes)
        pieces = [lax.dynamic_index_in_dim(full, gene ^ s, 0, False) for s in range(slots)]
        st["pieces"] = [pieces[0]] + [over_gene(pieces[s], s) for s in (1, 2, 3)]
    for word in " ".join(ORDER).split():
        if word[:2] == "w:":
            if spot_size == 2 or word == "w:ez1+ez2+ez3":
                wait_for(word[2:])
        elif spot_size != 2 and word[0] == "G":
            forward_send(int(word[1]))
        elif spot_size == 2 or word[0] not in "YAaS":
            steps[word[0]](int(word[1]))

    n_ch, n_sum = len(WIDTHS), len(SUMS)
    starts = [offsets[GROUPS[z[0]][0]] for z in SUMS]
    preds = [(st["sum", z], whole((quarter, sum_width[z]))) for z in range(n_sum)]
    mine = (spatial, pl.BlockSpec((quarter, genes), lambda g, f: (f[2], 0)))
    memb = (st["member"], whole((quarter, LANES)))
    gene_spec, spot_spec = whole((16, genes)), whole((8, quarter))

    def stats_body(fl, i, out):
        memb = i[0]
        cols = [jnp.broadcast_to(memb[:, k : k + 1], (quarter, LANES)) for k in range(SLIDES)]
        valid = jnp.sum(memb[:, SLIDES : SLIDES + 1])
        out[0][...] = jnp.broadcast_to(valid, (16, genes))
        totals = [jnp.zeros((quarter, LANES), F32) for _ in range(3)]
        for g in range(n_sum):
            for o in range(0, sum_width[g], LANES):
                at = slice(starts[g] + o, starts[g] + o + LANES)
                pr, ta = i[2 + g][:, o : o + LANES], i[1][:, at].astype(F32)
                for j, v in enumerate((pr * ta, pr * pr, ta * ta)):
                    totals[j] += v
                    for k in range(SLIDES):
                        n = 3 * j + k
                        out[0][n : n + 1, at] = jnp.sum(cols[k] * v, axis=0, keepdims=True)
        out[1][...] = jnp.zeros((8, quarter), F32)
        for j in range(3):
            out[1][j : j + 1, :] = jnp.sum(jnp.transpose(totals[j]), axis=0, keepdims=True)

    gene_sums, spot_sums = run(
        "stats", stats_body, [memb, mine, *preds],
        [(sds((16, genes), F32), gene_spec), (sds((8, quarter), F32), spot_spec)],
    )
    far = {s: over_gene(spot_sums, s) for s in (3, 2, 1)}
    spot_parts = [spot_sums] + [far[s] for s in (1, 2, 3)]
    gene_sums = gene_sums + over_core(gene_sums)
    gene_sums = gene_sums + over_x(gene_sums)
    gene_parts = [gene_sums, over_spot(gene_sums)] if spot_size == 2 else [sum_spot(gene_sums)]

    run("spots", None, after=spot_parts)

    def grads_body(fl, i, out):
        memb, ta_ref, kl, ent = i[:4]
        i = i[4:]
        spot_in, gene_in, preds_in = i[:4], i[4 : 4 + len(gene_parts)], i[4 + len(gene_parts) :]
        scale = -1.0 / (SLIDES * genes_all)
        sums = sum(ref[...] for ref in gene_in)
        num, psq, tsq = sums[0:3], sums[3:6], sums[6:9]
        p_floor, t_floor = jnp.maximum(psq, 1.0), jnp.maximum(tsq, 1.0)
        root = jnp.sqrt(p_floor * t_floor)
        cosine = num / root
        w_t = scale / root
        w_p = jnp.where(psq > 1.0, -scale * cosine / p_floor, 0.0)
        valid_total = jnp.maximum(sums[9, 0], 1.0)
        spot_all = (spot_in[0][...] + spot_in[1][...]) + (spot_in[2][...] + spot_in[3][...])
        s_num, s_p, s_t = [column(spot_all[n : n + 1, :]) for n in range(3)]
        s_p, s_t = s_p + 1e-06, s_t + 1e-06
        root = jnp.sqrt(s_p * s_t)
        cos_spot = s_num / root
        valid = jnp.broadcast_to(memb[:, SLIDES : SLIDES + 1], (quarter, LANES))
        coef = -valid / valid_total
        coef_t, coef_p = coef / root, -coef * cos_spot / s_p
        first = [(fl[n] == 0).astype(F32) for n in (2, 4, 3)]
        terms = [
            jnp.sum(cosine) * first[0] * first[1],
            jnp.sum((valid * cos_spot)[:, 0:1]) * first[2],
            kl[0, 0] * first[1],
            jnp.sum(ent[0:1, :]),
            valid_total * first[0] * first[1] * first[2],
        ]
        lane = lax.broadcasted_iota(jnp.int32, (8, spots), 1)
        value = jnp.zeros((8, spots), F32)
        for n, term in enumerate(terms):
            value = jnp.where(lane == n, term, value)
        out[1][...] = value
        cols = [jnp.broadcast_to(memb[:, k : k + 1], (quarter, LANES)) for k in range(SLIDES)]
        for g in range(n_sum):
            for o in range(0, sum_width[g], LANES):
                at = slice(starts[g] + o, starts[g] + o + LANES)
                f_t, f_p = coef_t, coef_p
                for k in range(SLIDES):
                    f_t = f_t + cols[k] * w_t[k : k + 1, at]
                    f_p = f_p + cols[k] * w_p[k : k + 1, at]
                out[0][:, at] = (f_t * ta_ref[:, at].astype(F32) + f_p * preds_in[g][:, o : o + LANES]).astype(BF)

    row8, flat = whole((8, spots)), whole((8, LANES))
    ins = [memb, mine, (st["kl"], flat), (st["ent"], row8)]
    ins += [(a, spot_spec) for a in spot_parts] + [(a, gene_spec) for a in gene_parts] + preds
    grad, terms = run(
        "grads", grads_body, ins,
        [(sds((quarter, genes), BF), whole((quarter, genes))), (sds((8, spots), F32), row8)],
    )
    terms = [terms, over_spot(terms)] if spot_size == 2 else [sum_spot(terms)]
    far = {s: over_gene(grad, s) for s in (3, 2, 1)}
    others = [far[s] for s in (1, 2, 3)]
    grad_x = over_x(grad)
    own = [grad, over_core(grad), grad_x, over_core(grad_x)]
    one, rest = (quarter, genes), (slots - 1, quarter, genes)
    row_blk = rows // 4

    def by_rows(width, size=row_blk):
        return pl.BlockSpec((size, width), lambda g, f: (g, 0))

    def place(fl, refs, target, sems):
        copies = []
        for b, ref in enumerate(refs):
            at = pl.ds(pl.multiple_of((fl[2] ^ b) * quarter, quarter), quarter)
            copies.append((None, ref, target(at)))
        copy_all(copies, sems)

    def slot_product(efs, slot, held):
        left = jnp.concatenate([ef[:, slot * w : (slot + 1) * w] for w, ef in zip(WIDTHS, efs)], axis=1)
        return lax.dot_general(left, held, (((1,), (1,)), ((), ())), preferred_element_type=F32)

    def gather_body(fl, i, out):
        for n in range(slots - 1):
            out[0][n] = i[n][...]

    (rest_z,) = run(
        "gather", gather_body, [(a, whole(one)) for a in others], [(sds(rest, BF), whole(rest))], after=[grad_x, *terms[1:]]
    )
    rest_x = over_x(rest_z)

    def own_body(fl, i, out, held, sems):
        sm, efs, gs = i[0], i[1 : 1 + n_ch], i[1 + n_ch :]

        @pl.when(pl.program_id(0) == 0)
        def _():
            place(fl, gs, lambda at: held.at[at, :], sems)

        out[0][...] = slot_product(efs, 0, held[...]) - jnp.broadcast_to(sm[:, 0:1], (row_blk, spots))

    ins = [(st["sm"], by_rows(LANES))] + [(st["e", c], by_rows(WIDTHS[c])) for c in chunks]
    ins += [(a, ANY) for a in own]
    (own_part,) = run(
        "own", own_body, ins, [(sds((rows, spots), F32), by_rows(spots))], grid=(rows // row_blk,),
        scratch=[pltpu.VMEM((spots, genes), BF), pltpu.SemaphoreType.DMA((len(own),))],
    )

    (rest_x,) = run("rest", None, through=[rest_x])
    grads = [rest_z, over_core(rest_z), rest_x, over_core(rest_x)]

    def backward_body(fl, i, out, held, sems):
        lg, tot, before = i[:3]
        efs, gs, terms = i[3 : 3 + n_ch], i[3 + n_ch : 7 + n_ch], i[7 + n_ch :]

        @pl.when(pl.program_id(0) == 0)
        def _():
            row = lax.broadcasted_iota(jnp.int32, (8, spots), 0)
            out[1][...] = jnp.where(row == 0, 0.0, sum(ref[...] for ref in terms))
            place(fl, gs, lambda at: held.at[:, at, :], sems)

        acc = before[...]
        for s in range(1, slots):
            acc += slot_product(efs, s, held[s - 1])
        out[0][...] = acc
        prob = jnp.exp(lg[...].astype(F32)) * (1.0 / tot[0:1, :])
        out[1][0:1, :] += jnp.sum(prob * acc, axis=0, keepdims=True)

    ins = [(logits, by_rows(spots)), (st["tot"], row8), (own_part, by_rows(spots))]
    ins += [(st["e", c], by_rows(slots * WIDTHS[c])) for c in chunks]
    ins += [(a, ANY) for a in grads] + [(a, row8) for a in terms]
    grad_probs, v = run(
        "backward", backward_body, ins,
        [(sds((rows, spots), F32), by_rows(spots)), (sds((8, spots), F32), row8)],
        grid=(rows // row_blk,),
        scratch=[pltpu.VMEM((slots - 1, spots, genes), BF), pltpu.SemaphoreType.DMA((len(grads),))],
    )

    v = v + over_core(v)
    v = v + over_x(v)
    v = (v + over_gene(v, 1)) + (over_gene(v, 2) + over_gene(v, 3))

    def final_body(fl, i, out):
        prob = jnp.exp(i[0][...].astype(F32)) * (1.0 / i[1][0:1, :])
        out[0][...] = prob * (i[2][...] - i[3][0:1, :])

        @pl.when(pl.program_id(0) == 0)
        def _():
            sums = [i[3][1, n] for n in range(5)]
            gene_term, spot_term = sums[0] / (SLIDES * genes_all), sums[1] / sums[4]
            divergence, entropy = sums[2], sums[3] / spots_all
            values = (divergence - gene_term - spot_term, gene_term, spot_term, divergence, entropy)
            for n, value in enumerate(values):
                out[1][n] = value

    last_blk = rows // 2
    blk = by_rows(spots, last_blk)
    grad_logits, loss_terms = run(
        "final", final_body, [(logits, blk), (st["tot"], row8), (grad_probs, blk), (v, row8)],
        [(sds((rows, spots), F32), blk), (sds((5,), F32), pl.BlockSpec(memory_space=pltpu.SMEM))],
        grid=(rows // last_blk,),
    )
    return (loss_terms, grad_logits)


def solution(mesh):
    return jax.shard_map(
        functools.partial(per_device, dict(mesh.shape)),
        mesh=mesh,
        in_specs=(
            P(("cell", "gene"), "spot"),
            P(("cell", "spot"), "gene"),
            P("spot", "gene"),
            P("spot"),
            P("spot"),
            P(("cell", "gene")),
        ),
        out_specs=(P(), P(("cell", "gene"), "spot")),
        check_vma=False,
    )
```

```python
import functools
import jax
import jax.numpy as jnp
from jax import lax
from jax.experimental import pallas as pl
from jax.experimental.pallas import tpu as pltpu
from jax.sharding import PartitionSpec as P

SLIDES = 3
LANES = 128
PAD = 8
ANY = pl.BlockSpec(memory_space=pl.ANY)
BF = jnp.bfloat16
F32 = jnp.float32
SHARED = (0, 0, 0, 256)
VMEM_BYTES = 14 * 1024 * 1024
COSTS = {"spots": 1, "back3": 1, "waits2": 3, "addx1": 9, "half0": 3}
WIDTHS = (128, 128, 128, 128)
GROUPS = ((0, 1), (2,), (3,))
SUMS = ((0,), (1, 2))
ORDER = (
    "Y0 e0 Y1 w:ez1+ez2+ez3",
    "Y2 A0 a0 e3",
    "b0 A1 Y3 w:f20+f30+n0",
    "a1 A2 w:f21+f31+n1 a2",
    "S0 A3 w:f22+f32+n2 a3",
    "S1 w:s0 S2 w:s1",
    "F0 w:f23+f33+n3 S3 f0",
    "P0 w:s2 F1 f1",
    "P1 F2 Q0 G2",
    "P2 X1 Q1 U0",
    "m0 R1 R0",
)


def sds(shape, dtype):
    return jax.ShapeDtypeStruct(shape, dtype)


def whole(shape):
    zeros = (0,) * len(shape)
    return pl.BlockSpec(shape, lambda *_: zeros)


def xor_pairs(size, step):
    return [(n, n ^ step) for n in range(size)]


class Chain:
    def __init__(self, flags):
        self.flags = flags
        self.token = jnp.zeros((8, LANES), F32)

    def run(self, name, body, ins=(), outs=(), after=(), through=(), grid=(1,), scratch=()):
        ins = [*ins, *((a, ANY) for a in after)]
        carried = (*through, self.token)
        n_in, n_out, n_thr = len(ins), len(outs), len(carried)

        def kernel(flags, *refs):
            in_refs = refs[:n_in]
            out_refs = refs[n_in + n_thr : n_in + 2 * n_thr + n_out - 1]
            scratch_refs = refs[n_in + 2 * n_thr + n_out :]
            if body is not None:
                body(flags, in_refs, out_refs, *scratch_refs)

        results = pl.pallas_call(
            kernel,
            out_shape=[s for s, _ in outs] + [sds(a.shape, a.dtype) for a in carried],
            grid_spec=pltpu.PrefetchScalarGridSpec(
                num_scalar_prefetch=1,
                grid=grid,
                in_specs=[s for _, s in ins] + [ANY] * n_thr,
                out_specs=[s for _, s in outs] + [ANY] * n_thr,
                scratch_shapes=list(scratch),
            ),
            input_output_aliases={1 + n_in + j: n_out + j for j in range(n_thr)},
            compiler_params=pltpu.CompilerParams(vmem_limit_bytes=VMEM_BYTES),
            cost_estimate=pl.CostEstimate(flops=COSTS.get(name, 0) * 10**9, bytes_accessed=0, transcendentals=0),
            name=name,
        )(self.flags, *[a for a, _ in ins], *carried)
        self.token = results[-1]
        return results[:-1]


def copy_all(copies, sems):
    made = [(c, pltpu.make_async_copy(s, d, sems.at[n])) for n, (c, s, d) in enumerate(copies)]
    for act in ("start", "wait"):
        for cond, copy in made:
            if cond is None:
                getattr(copy, act)()
            else:
                pl.when(cond)(getattr(copy, act))


def column(row):
    return jnp.transpose(jnp.broadcast_to(row, (LANES, row.shape[1])))


def per_device(sizes, logits, expression, spatial, slide_ids, spot_mask, densities):
    spot_size = sizes["spot"]
    rows, spots = logits.shape
    genes = spatial.shape[1]
    spots_all = spots * spot_size
    genes_all = genes * sizes["gene"]
    slots = sizes["gene"]
    quarter = spots // sizes["cell"]
    cell, spot, gene = (lax.axis_index(a) for a in ("cell", "spot", "gene"))
    home = (gene // 2 == spot).astype(jnp.int32)
    side = (gene % 2).astype(jnp.int32)
    chain = Chain(jnp.stack([home, side, cell, gene, spot]).astype(jnp.int32))
    run = chain.run
    offsets = [sum(WIDTHS[:n]) for n in range(len(WIDTHS))]
    chunks = range(len(WIDTHS))
    group_width = [sum(WIDTHS[c] for c in g) for g in GROUPS]

    def over_core(v):
        return lax.ppermute(v, "cell", xor_pairs(4, 1))

    def over_x(v):
        return lax.ppermute(v, "cell", xor_pairs(4, 2))

    def over_gene(v, step):
        return lax.ppermute(v, "gene", xor_pairs(4, step))

    def over_spot(v, step=1):
        return lax.ppermute(v, "spot", xor_pairs(spot_size, step))

    def sum_spot(v):
        step = 1
        while step < spot_size:
            v = v + over_spot(v, step)
            step *= 2
        return v

    ids_row, mask_row = slide_ids.reshape(1, spots), spot_mask.reshape(1, spots)
    dens_row = densities.reshape(1, rows)

    expr = expression.reshape(2, rows, genes) if spot_size == 2 else None
    st, sent = {}, {}

    def start_swap(c):
        w = WIDTHS[c]
        if c == 0:
            sent["y0"] = over_spot(expr[:, :, :w])
            return

        def body(fl, i, out, sems):
            copy_all([(None, i[0].at[p, :, pl.ds(offsets[c], w)], out[0].at[p]) for p in range(2)], sems)

        shape = (2, rows, w)
        (v,) = run(
            f"swap{c}", body, [(expr, pl.BlockSpec(memory_space=pltpu.HBM))], [(sds(shape, BF), whole(shape))],
            scratch=[pltpu.SemaphoreType.DMA((2,))],
        )
        sent[f"y{c}"] = over_spot(v)

    def parted(c):
        lone = (rows - SHARED[c]) // 2
        return lone, lone + SHARED[c]

    def start_along(c):
        w = WIDTHS[c]
        cols, (_, far) = pl.ds(offsets[c], w), parted(c)

        def body(fl, i, out, sems):
            y, e = i
            at_home, away = fl[0] == 1, fl[0] == 0
            same, other = fl[1], 1 - fl[1]
            first, last = pl.ds(0, far), pl.ds(rows - far, far)
            copies = [
                (at_home, y.at[same, first, :], out[0]),
                (at_home, y.at[other, first, :], out[1]),
                (at_home, e.at[other, :, cols], out[2]),
                (away, e.at[same, last, cols], out[0]),
                (away, e.at[other, last, cols], out[1]),
                (away, y.at[other], out[2]),
            ]
            copy_all(copies, sems)

        shapes = ((far, w), (far, w), (rows, w))
        st["along", c] = run(
            f"along{c}", body, [(sent[f"y{c}"], ANY), (expr, ANY)], [(sds(v, BF), whole(v)) for v in shapes],
            scratch=[pltpu.SemaphoreType.DMA((6,))],
        )

    def along_send(c):
        a, b, n = run(f"alongsend{c}", None, through=st["along", c])
        sent[f"f2{c}"], sent[f"f3{c}"], sent[f"n{c}"] = over_gene(a, 2), over_gene(b, 3), over_gene(n, 1)

    def start_back(c):
        w = WIDTHS[c]
        lone, far = parted(c)

        def body(fl, i, out):
            @pl.when(fl[0] == 1)
            def _():
                for n in (0, 1):
                    out[0][n] = i[n][far - lone :, :]

            @pl.when(fl[0] == 0)
            def _():
                for n in (0, 1):
                    out[0][n] = i[n][:lone, :]

        shape = (2, lone, w)
        ins = [(sent[f"f{n}{c}"], whole((far, w))) for n in (2, 3)]
        (v,) = run(f"back{c}", body, ins, [(sds(shape, BF), whole(shape))])
        sent[f"s{c}"] = over_spot(v)

    def wait_for(name):
        run("wait" + name.split("+")[0], None, after=[sent[n] for n in name.split("+")])

    def members_of(_):
        def body(fl, i, out):
            ids, valid = column(i[0][...].astype(F32)), column(i[1][...].astype(F32))
            lane = lax.broadcasted_iota(jnp.int32, (quarter, LANES), 1)
            inside = (lane < SLIDES) & (lane.astype(F32) == ids) & (valid == 1.0)
            out[0][...] = jnp.where(inside, 1.0, jnp.where(lane == SLIDES, valid, 0.0))

        row, tall = pl.BlockSpec((1, quarter), lambda g, f: (0, f[2])), whole((quarter, LANES))
        (st["member"],) = run("member", body, [(ids_row, row), (mask_row, row)], [(sds((quarter, LANES), F32), tall)])

    def totals(n):
        sp = whole((8, spots))
        if n == 0:

            def body(fl, i, out):
                out[0][...] = jnp.zeros((8, spots), F32)
                out[0][0:1, :] = jnp.sum(jnp.exp(i[0][...].astype(F32)), axis=0, keepdims=True)
                out[0][1:2, :] = jnp.broadcast_to(jnp.sum(i[1][...]), (1, spots))

            ins = [(logits, whole(logits.shape)), (dens_row, whole(dens_row.shape))]
            (v,) = run("totals", body, ins, [(sds((8, spots), F32), sp)])
            st["tot"] = lax.psum(v, "cell")
            for s in (1, 2, 3):
                sent[f"ez{s}"] = over_gene(st["tot"], s)
        else:
            blk = 2 * LANES

            def body(fl, i, out):
                tot = (i[1][...] + i[2][...]) + (i[3][...] + i[4][...])
                out[3][...] = tot
                inv = 1.0 / tot[0:1, :]
                log_tot = jnp.log(tot[0:1, :])
                vals = i[0][...].astype(F32)
                prob = jnp.exp(vals) * inv
                prob_t = jnp.transpose(prob.astype(BF))
                for q in range(sizes["cell"]):
                    at = pl.multiple_of((fl[2] ^ q) * quarter, quarter)
                    out[0][pl.ds(at, quarter), :] = prob_t[q * quarter : (q + 1) * quarter]
                folded = sum(prob[:, n : n + LANES] for n in range(0, spots, LANES))
                row_sums = jnp.sum(jnp.transpose(folded), axis=0, keepdims=True)
                out[1][...] = jnp.broadcast_to(row_sums, (8, blk))

                @pl.when(pl.program_id(0) == 0)
                def _():
                    out[2][...] = jnp.zeros((8, spots), F32)

                out[2][0:1, :] -= jnp.sum(prob * (vals - log_tot), axis=0, keepdims=True)

            parts = [st["tot"]] + [sent[f"ez{s}"] for s in (1, 2, 3)]
            pt, mass, ent, st["tot"] = run(
                "prob", body,
                [(logits, pl.BlockSpec((blk, spots), lambda g, f: (g, 0)))] + [(a, sp) for a in parts],
                [
                    (sds((spots, rows), BF), pl.BlockSpec((spots, blk), lambda g, f: (0, g))),
                    (sds((8, rows), F32), pl.BlockSpec((8, blk), lambda g, f: (0, g))),
                    (sds((8, spots), F32), sp),
                    (sds((8, spots), F32), sp),
                ],
                grid=(rows // blk,),
            )
            st["pt"], st["ent"] = pt, ent
            st["mass"] = mass if spot_size == 2 else sum_spot(mass)
            if spot_size == 2:
                sent["my"] = over_spot(mass)

    def shares(_):
        masses = [st["mass"]] + ([sent["my"]] if spot_size == 2 else [])

        def body(fl, i, out):
            mass = i[2][0:1, :]
            for extra in i[3:]:
                mass = mass + extra[0:1, :]
            share = i[0][...] / i[1][1:2, 0:1]
            out[0][...] = column(share / mass)
            kl = jnp.sum(share * (jnp.log(share) - jnp.log(mass / spots_all)))
            out[1][...] = jnp.broadcast_to(kl, (8, LANES))

        st["sm"], st["kl"] = run(
            "shares", body,
            [(dens_row, whole(dens_row.shape)), (st["tot"], whole((8, spots)))]
            + [(m, whole((8, rows))) for m in masses],
            [(sds((rows, LANES), F32), whole((rows, LANES))), (sds((8, LANES), F32), whole((8, LANES)))],
        )

    def halves_of(g):
        shape = (quarter, slots * group_width[g])
        return [(sds(shape, F32), whole(shape))] * 2

    def forward(g):
        members, wide_all = GROUPS[g], group_width[g] * slots
        shape = (2, quarter, wide_all)
        outs = [(sds((rows, slots * WIDTHS[c]), BF), whole((rows, slots * WIDTHS[c]))) for c in members]
        outs += [(sds(shape, F32), whole(shape))]
        outs += halves_of(g)

        late = members[-1] if spot_size == 2 and g == len(GROUPS) - 1 else None

        def product(pt, efs, keep, *send, direct=None):
            done = 0
            low, high = send
            for c, ef in zip(members, efs):
                w = WIDTHS[c]
                if c == late:
                    near = jnp.dot(pt[...], ef[:, : 2 * w], preferred_element_type=F32)
                    lone, size = parted(c)
                    at = pl.ds(pl.multiple_of(direct * lone, LANES), size)
                    far = jnp.dot(pt[:, at], ef[at, 2 * w :], preferred_element_type=F32)
                    acc = jnp.concatenate([near, far], axis=1)
                else:
                    acc = jnp.dot(pt[...], ef[...], preferred_element_type=F32)
                for q, ref in enumerate((keep.at[0], low, keep.at[1], high)):
                    rows_q = acc[q * quarter : (q + 1) * quarter]
                    for s in range(slots):
                        base = s * group_width[g] + done
                        ref[:, base : base + w] = rows_q[:, s * w : (s + 1) * w]
                done += w

        if spot_size == 2:

            def body(fl, i, out, sems):
                pt, e = i[:2]
                at_home, away = fl[0] == 1, fl[0] == 0
                copies = []
                for m, c in enumerate(members):
                    w, ef = WIDTHS[c], out[m]
                    y, n, f2, f3 = i[2 + 5 * m : 6 + 5 * m]
                    lone, far = parted(c)
                    top, low = pl.ds(0, lone), pl.ds(rows - lone, lone)
                    first, last = pl.ds(0, far), pl.ds(rows - far, far)
                    copies += [
                        (at_home, e.at[fl[1], :, pl.ds(offsets[c], w)], ef.at[:, pl.ds(0, w)]),
                        (away, y.at[fl[1]], ef.at[:, pl.ds(0, w)]),
                        (None, n, ef.at[:, pl.ds(w, w)]),
                    ]
                    for part, f in enumerate((f2, f3)):
                        cols = pl.ds((2 + part) * w, w)
                        copies += [(at_home, f, ef.at[last, cols]), (away, f, ef.at[first, cols])]
                        if c != late:
                            s = i[6 + 5 * m]
                            copies += [(at_home, s.at[part], ef.at[top, cols]), (away, s.at[part], ef.at[low, cols])]
                copy_all(copies, sems)
                product(pt, out[: len(members)], *out[len(members) :], direct=fl[0])

            ins = [(st["pt"], whole((spots, rows))), (expr, ANY)]
            ins += [
                (a, ANY)
                for c in members
                for a in (*(sent[f"{k}{c}"] for k in ("y", "n", "f2", "f3")), *([] if c == late else [sent[f"s{c}"]]))
            ]
            scratch = [pltpu.SemaphoreType.DMA((12 * len(members),))]
        else:

            def body(fl, i, out):
                for m, c in enumerate(members):
                    w = WIDTHS[c]
                    for s in range(slots):
                        out[m][:, s * w : (s + 1) * w] = i[1 + m * slots + s][...]
                product(i[0], out[: len(members)], *out[len(members) :])

            def at_chunk(c):
                return pl.BlockSpec((rows, WIDTHS[c]), lambda *_: (0, offsets[c] // WIDTHS[c]))

            ins = [(st["pt"], whole((spots, rows)))] + [(a, at_chunk(c)) for c in members for a in st["pieces"]]
            scratch = []
        results = run(f"forward{g}", body, ins, outs, scratch=scratch)
        for c, ef in zip(members, results):
            st["e", c] = ef
        st["r", g], st["send", g] = results[len(members)], results[len(members) + 1 :]

    def forward_late(g):
        c = GROUPS[g][-1]
        w, wide = WIDTHS[c], slots * group_width[g]
        shape, lone = (2, quarter, wide), parted(c)[0]

        def body(fl, i, out, sems):
            pt, swapped, keep, low, high = i
            at = pl.ds(pl.multiple_of((1 - fl[0]) * (rows - lone), LANES), lone)
            copy_all([(None, swapped.at[n], out[3].at[at, pl.ds((2 + n) * w, w)]) for n in (0, 1)], sems)
            both = jnp.concatenate([swapped[0], swapped[1]], axis=1)
            acc = jnp.dot(pt[:, at], both, preferred_element_type=F32)
            for new, old in zip(out, (keep, low, high)):
                new[...] = old[...]
            for q, ref in enumerate((out[0].at[0], out[1], out[0].at[1], out[2])):
                for n in (0, 1):
                    base = (3 + n) * group_width[g] - w
                    ref[:, base : base + w] += acc[q * quarter : (q + 1) * quarter, n * w : (n + 1) * w]

        one = whole((quarter, wide))
        ins = [(st["pt"], whole((spots, rows))), (sent[f"s{c}"], whole((2, lone, w)))]
        ins += [(st["r", g], whole(shape))] + [(a, one) for a in st["send", g]]
        st["r", g], *send, st["e", c] = run(
            f"forwardlate{g}", body, ins, [(sds(shape, F32), whole(shape)), *halves_of(g)], through=[st["e", c]],
            scratch=[pltpu.SemaphoreType.DMA((2,))],
        )
        send_core(g, send)

    def send_core(g, send):
        for n, part in enumerate(send):
            sent[f"rc{n}{g}"] = over_core(part)

    def forward_send(g):
        send_core(g, run(f"send{g}", None, through=st["send", g]))

    def reduce_core(g):
        wide = slots * group_width[g]
        shape, one = (2, quarter, wide), (quarter, wide)

        single = 0 < g < len(GROUPS) - 1

        def body(fl, i, out):
            for n in (0, 1):
                out[n][0:quarter, :] = i[0][n] + i[1 + n][...]
            if single:
                out[1][quarter:, :] = jnp.zeros((PAD, wide), F32)

        ins = [(st["r", g], whole(shape))]
        ins += [(sent[f"rc{n}{g}"], whole(one)) for n in (0, 1)]
        more = (quarter + PAD, wide) if single else one
        st["r", g], b = run(f"core{g}", body, ins, [(sds(one, F32), whole(one)), (sds(more, F32), whole(more))])
        sent[f"rx{g}"] = over_x(b)

    sum_groups = [[g for g in z] for z in SUMS]
    sum_width = [sum(group_width[g] for g in z) for z in SUMS]

    def add_x(g):
        one = whole((quarter, slots * group_width[g]))

        def body(fl, i, out):
            out[0][...] = i[0][...] + i[1][0:quarter, :]

        ins = [(st["r", g], one), (sent[f"rx{g}"], whole(sent[f"rx{g}"].shape))]
        (st["added", g],) = run(f"addx{g}", body, ins, [(sds(one.block_shape, F32), one)])

    def reduce_x(z):
        members, w = sum_groups[z], sum_width[z]
        part = (quarter, w)
        in_halves = z < len(SUMS) - 1

        def body(fl, i, out):
            done, i = 0, list(i)
            for g in members:
                v = group_width[g]
                refs = [i.pop(0) for _ in parts_of[g]]
                for s in range(slots):
                    at = slice(s * v, (s + 1) * v)
                    value = sum(ref[0:quarter, at] for ref in refs)
                    if in_halves and s >= 2:
                        out[2][s - 2, :, done : done + v] = value
                    else:
                        out[s][:, done : done + v] = value
                done += v

        parts_of = {g: [st["added", g]] if ("added", g) in st else [st["r", g], sent[f"rx{g}"]] for g in members}
        ins = [(a, whole(a.shape)) for g in members for a in parts_of[g]]
        outs = [(sds(part, F32), whole(part))] * (2 if in_halves else slots)
        if in_halves:
            outs += [(sds((2, *part), F32), whole((2, *part)))]
        parts = run(f"x{z}", body, ins, outs)
        if in_halves:
            st["z", z] = parts[:2]
            sent[f"rz2{z}"] = over_gene(parts[2], 2)
        else:
            st["z", z] = parts[:1]
            for s in (3, 2, 1):
                sent[f"rz{s}{z}"] = over_gene(parts[s], s)

    def reduce_half(z):
        part = (quarter, sum_width[z])

        def body(fl, i, out):
            for n in (0, 1):
                out[n][...] = i[n][...] + i[2][n]

        ins = [(a, whole(part)) for a in st["z", z]] + [(sent[f"rz2{z}"], whole((2, *part)))]
        a, b = run(f"half{z}", body, ins, [(sds(part, F32), whole(part))] * 2)
        st["z", z], sent[f"rz1{z}"] = [a], over_gene(b, 1)

    def reduce_gene(z):
        part = (quarter, sum_width[z])
        others = [sent[f"rz{s}{z}"] for s in ((1,) if z < len(SUMS) - 1 else (1, 2, 3))]

        def body(fl, i, out):
            out[0][...] = sum(ref[...] for ref in i)

        ins = [(a, whole(part)) for a in (*st["z", z], *others)]
        (st["sum", z],) = run(f"gene{z}", body, ins, [(sds(part, F32), whole(part))])

    steps = {
        "Y": start_swap, "A": start_along, "a": along_send, "S": start_back,
        "e": totals, "m": shares, "F": forward, "f": forward_send, "G": forward_late, "b": members_of,
        "P": reduce_core, "X": add_x, "Q": reduce_x,
        "U": reduce_half, "R": reduce_gene,
    }
    if spot_size != 2:
        full = lax.all_gather(expression, "spot", axis=0, tiled=True).reshape(slots, rows, genes)
        pieces = [lax.dynamic_index_in_dim(full, gene ^ s, 0, False) for s in range(slots)]
        st["pieces"] = [pieces[0]] + [over_gene(pieces[s], s) for s in (1, 2, 3)]
    for word in " ".join(ORDER).split():
        if word[:2] == "w:":
            if spot_size == 2 or word == "w:ez1+ez2+ez3":
                wait_for(word[2:])
        elif spot_size != 2 and word[0] == "G":
            forward_send(int(word[1]))
        elif spot_size == 2 or word[0] not in "YAaS":
            steps[word[0]](int(word[1]))

    n_ch, n_sum = len(WIDTHS), len(SUMS)
    starts = [offsets[GROUPS[z[0]][0]] for z in SUMS]
    preds = [(st["sum", z], whole((quarter, sum_width[z]))) for z in range(n_sum)]
    mine = (spatial, pl.BlockSpec((quarter, genes), lambda g, f: (f[2], 0)))
    memb = (st["member"], whole((quarter, LANES)))
    gene_spec, spot_spec = whole((16, genes)), whole((8, quarter))

    def stats_body(fl, i, out):
        memb = i[0]
        cols = [jnp.broadcast_to(memb[:, k : k + 1], (quarter, LANES)) for k in range(SLIDES)]
        valid = jnp.sum(memb[:, SLIDES : SLIDES + 1])
        out[0][...] = jnp.broadcast_to(valid, (16, genes))
        totals = [jnp.zeros((quarter, LANES), F32) for _ in range(3)]
        for g in range(n_sum):
            for o in range(0, sum_width[g], LANES):
                at = slice(starts[g] + o, starts[g] + o + LANES)
                pr, ta = i[2 + g][:, o : o + LANES], i[1][:, at].astype(F32)
                for j, v in enumerate((pr * ta, pr * pr, ta * ta)):
                    totals[j] += v
                    for k in range(SLIDES):
                        n = 3 * j + k
                        out[0][n : n + 1, at] = jnp.sum(cols[k] * v, axis=0, keepdims=True)
        out[1][...] = jnp.zeros((8, quarter), F32)
        for j in range(3):
            out[1][j : j + 1, :] = jnp.sum(jnp.transpose(totals[j]), axis=0, keepdims=True)

    gene_sums, spot_sums = run(
        "stats", stats_body, [memb, mine, *preds],
        [(sds((16, genes), F32), gene_spec), (sds((8, quarter), F32), spot_spec)],
    )
    far = {s: over_gene(spot_sums, s) for s in (3, 2, 1)}
    spot_parts = [spot_sums] + [far[s] for s in (1, 2, 3)]
    gene_sums = gene_sums + over_core(gene_sums)
    gene_sums = gene_sums + over_x(gene_sums)
    gene_parts = [gene_sums, over_spot(gene_sums)] if spot_size == 2 else [sum_spot(gene_sums)]

    run("spots", None, after=spot_parts)

    def grads_body(fl, i, out):
        memb, ta_ref, kl, ent = i[:4]
        i = i[4:]
        spot_in, gene_in, preds_in = i[:4], i[4 : 4 + len(gene_parts)], i[4 + len(gene_parts) :]
        scale = -1.0 / (SLIDES * genes_all)
        sums = sum(ref[...] for ref in gene_in)
        num, psq, tsq = sums[0:3], sums[3:6], sums[6:9]
        p_floor, t_floor = jnp.maximum(psq, 1.0), jnp.maximum(tsq, 1.0)
        root = jnp.sqrt(p_floor * t_floor)
        cosine = num / root
        w_t = scale / root
        w_p = jnp.where(psq > 1.0, -scale * cosine / p_floor, 0.0)
        valid_total = jnp.maximum(sums[9, 0], 1.0)
        spot_all = (spot_in[0][...] + spot_in[1][...]) + (spot_in[2][...] + spot_in[3][...])
        s_num, s_p, s_t = [column(spot_all[n : n + 1, :]) for n in range(3)]
        s_p, s_t = s_p + 1e-06, s_t + 1e-06
        root = jnp.sqrt(s_p * s_t)
        cos_spot = s_num / root
        valid = jnp.broadcast_to(memb[:, SLIDES : SLIDES + 1], (quarter, LANES))
        coef = -valid / valid_total
        coef_t, coef_p = coef / root, -coef * cos_spot / s_p
        first = [(fl[n] == 0).astype(F32) for n in (2, 4, 3)]
        terms = [
            jnp.sum(cosine) * first[0] * first[1],
            jnp.sum((valid * cos_spot)[:, 0:1]) * first[2],
            kl[0, 0] * first[1],
            jnp.sum(ent[0:1, :]),
            valid_total * first[0] * first[1] * first[2],
        ]
        lane = lax.broadcasted_iota(jnp.int32, (8, spots), 1)
        value = jnp.zeros((8, spots), F32)
        for n, term in enumerate(terms):
            value = jnp.where(lane == n, term, value)
        out[1][...] = value
        cols = [jnp.broadcast_to(memb[:, k : k + 1], (quarter, LANES)) for k in range(SLIDES)]
        for g in range(n_sum):
            for o in range(0, sum_width[g], LANES):
                at = slice(starts[g] + o, starts[g] + o + LANES)
                f_t, f_p = coef_t, coef_p
                for k in range(SLIDES):
                    f_t = f_t + cols[k] * w_t[k : k + 1, at]
                    f_p = f_p + cols[k] * w_p[k : k + 1, at]
                out[0][:, at] = (f_t * ta_ref[:, at].astype(F32) + f_p * preds_in[g][:, o : o + LANES]).astype(BF)

    row8, flat = whole((8, spots)), whole((8, LANES))
    ins = [memb, mine, (st["kl"], flat), (st["ent"], row8)]
    ins += [(a, spot_spec) for a in spot_parts] + [(a, gene_spec) for a in gene_parts] + preds
    grad, terms = run(
        "grads", grads_body, ins,
        [(sds((quarter, genes), BF), whole((quarter, genes))), (sds((8, spots), F32), row8)],
    )
    terms = [terms, over_spot(terms)] if spot_size == 2 else [sum_spot(terms)]
    far = {s: over_gene(grad, s) for s in (3, 2, 1)}
    others = [far[s] for s in (1, 2, 3)]
    grad_x = over_x(grad)
    own = [grad, over_core(grad), grad_x, over_core(grad_x)]
    one, rest = (quarter, genes), (slots - 1, quarter, genes)
    row_blk = rows // 4

    def by_rows(width, size=row_blk):
        return pl.BlockSpec((size, width), lambda g, f: (g, 0))

    def place(fl, refs, target, sems):
        copies = []
        for b, ref in enumerate(refs):
            at = pl.ds(pl.multiple_of((fl[2] ^ b) * quarter, quarter), quarter)
            copies.append((None, ref, target(at)))
        copy_all(copies, sems)

    def slot_product(efs, slot, held):
        left = jnp.concatenate([ef[:, slot * w : (slot + 1) * w] for w, ef in zip(WIDTHS, efs)], axis=1)
        return lax.dot_general(left, held, (((1,), (1,)), ((), ())), preferred_element_type=F32)

    def gather_body(fl, i, out):
        for n in range(slots - 1):
            out[0][n] = i[n][...]

    (rest_z,) = run(
        "gather", gather_body, [(a, whole(one)) for a in others], [(sds(rest, BF), whole(rest))], after=[grad_x, *terms[1:]]
    )
    rest_x = over_x(rest_z)

    def own_body(fl, i, out, held, sems):
        sm, efs, gs = i[0], i[1 : 1 + n_ch], i[1 + n_ch :]

        @pl.when(pl.program_id(0) == 0)
        def _():
            place(fl, gs, lambda at: held.at[at, :], sems)

        out[0][...] = slot_product(efs, 0, held[...]) - jnp.broadcast_to(sm[:, 0:1], (row_blk, spots))

    ins = [(st["sm"], by_rows(LANES))] + [(st["e", c], by_rows(WIDTHS[c])) for c in chunks]
    ins += [(a, ANY) for a in own]
    (own_part,) = run(
        "own", own_body, ins, [(sds((rows, spots), F32), by_rows(spots))], grid=(rows // row_blk,),
        scratch=[pltpu.VMEM((spots, genes), BF), pltpu.SemaphoreType.DMA((len(own),))],
    )

    (rest_x,) = run("rest", None, through=[rest_x])
    grads = [rest_z, over_core(rest_z), rest_x, over_core(rest_x)]

    def backward_body(fl, i, out, held, sems):
        lg, tot, before = i[:3]
        efs, gs, terms = i[3 : 3 + n_ch], i[3 + n_ch : 7 + n_ch], i[7 + n_ch :]

        @pl.when(pl.program_id(0) == 0)
        def _():
            row = lax.broadcasted_iota(jnp.int32, (8, spots), 0)
            out[1][...] = jnp.where(row == 0, 0.0, sum(ref[...] for ref in terms))
            place(fl, gs, lambda at: held.at[:, at, :], sems)

        acc = before[...]
        for s in range(1, slots):
            acc += slot_product(efs, s, held[s - 1])
        out[0][...] = acc
        prob = jnp.exp(lg[...].astype(F32)) * (1.0 / tot[0:1, :])
        out[1][0:1, :] += jnp.sum(prob * acc, axis=0, keepdims=True)

    ins = [(logits, by_rows(spots)), (st["tot"], row8), (own_part, by_rows(spots))]
    ins += [(st["e", c], by_rows(slots * WIDTHS[c])) for c in chunks]
    ins += [(a, ANY) for a in grads] + [(a, row8) for a in terms]
    grad_probs, v = run(
        "backward", backward_body, ins,
        [(sds((rows, spots), F32), by_rows(spots)), (sds((8, spots), F32), row8)],
        grid=(rows // row_blk,),
        scratch=[pltpu.VMEM((slots - 1, spots, genes), BF), pltpu.SemaphoreType.DMA((len(grads),))],
    )

    v = v + over_core(v)
    v = v + over_x(v)
    v = (v + over_gene(v, 1)) + (over_gene(v, 2) + over_gene(v, 3))

    def final_body(fl, i, out):
        prob = jnp.exp(i[0][...].astype(F32)) * (1.0 / i[1][0:1, :])
        out[0][...] = prob * (i[2][...] - i[3][0:1, :])

        @pl.when(pl.program_id(0) == 0)
        def _():
            sums = [i[3][1, n] for n in range(5)]
            gene_term, spot_term = sums[0] / (SLIDES * genes_all), sums[1] / sums[4]
            divergence, entropy = sums[2], sums[3] / spots_all
            values = (divergence - gene_term - spot_term, gene_term, spot_term, divergence, entropy)
            for n, value in enumerate(values):
                out[1][n] = value

    last_blk = rows // 2
    blk = by_rows(spots, last_blk)
    grad_logits, loss_terms = run(
        "final", final_body, [(logits, blk), (st["tot"], row8), (grad_probs, blk), (v, row8)],
        [(sds((rows, spots), F32), blk), (sds((5,), F32), pl.BlockSpec(memory_space=pltpu.SMEM))],
        grid=(rows // last_blk,),
    )
    return (loss_terms, grad_logits)


def solution(mesh):
    return jax.shard_map(
        functools.partial(per_device, dict(mesh.shape)),
        mesh=mesh,
        in_specs=(
            P(("cell", "gene"), "spot"),
            P(("cell", "spot"), "gene"),
            P("spot", "gene"),
            P("spot"),
            P("spot"),
            P(("cell", "gene")),
        ),
        out_specs=(P(), P(("cell", "gene"), "spot")),
        check_vma=False,
    )
```

```python
import functools
import jax
import jax.numpy as jnp
from jax import lax
from jax.experimental import pallas as pl
from jax.experimental.pallas import tpu as pltpu
from jax.sharding import PartitionSpec as P

SLIDES = 3
LANES = 128
PAD = 8
ANY = pl.BlockSpec(memory_space=pl.ANY)
BF = jnp.bfloat16
F32 = jnp.float32
SHARED = (0, 0, 0, 256)
VMEM_BYTES = 12 * 1024 * 1024
COSTS = {"spots": 1, "back3": 3, "waits2": 3, "addx1": 9, "half0": 3}
WIDTHS = (128, 128, 128, 128)
GROUPS = ((0, 1), (2,), (3,))
SUMS = ((0,), (1, 2))
ORDER = (
    "Y0 e0 Y1 w:ez1+ez2+ez3",
    "Y2 A0 a0 e3",
    "b0 A1 Y3 w:f20+f30+n0",
    "a1 A2 w:f21+f31+n1 a2",
    "S0 A3 w:f22+f32+n2 a3",
    "S1 w:s0 S2 w:s1",
    "F0 w:f23+f33+n3 S3 f0",
    "P0 w:s2 F1 f1",
    "P1 F2 Q0 G2",
    "P2 X1 Q1 U0",
    "m0 R1 R0",
)


def sds(shape, dtype):
    return jax.ShapeDtypeStruct(shape, dtype)


def whole(shape):
    zeros = (0,) * len(shape)
    return pl.BlockSpec(shape, lambda *_: zeros)


def xor_pairs(size, step):
    return [(n, n ^ step) for n in range(size)]


class Chain:
    def __init__(self, flags):
        self.flags = flags
        self.token = jnp.zeros((8, LANES), F32)

    def run(self, name, body, ins=(), outs=(), after=(), through=(), grid=(1,), scratch=()):
        ins = [*ins, *((a, ANY) for a in after)]
        carried = (*through, self.token)
        n_in, n_out, n_thr = len(ins), len(outs), len(carried)

        def kernel(flags, *refs):
            in_refs = refs[:n_in]
            out_refs = refs[n_in + n_thr : n_in + 2 * n_thr + n_out - 1]
            scratch_refs = refs[n_in + 2 * n_thr + n_out :]
            if body is not None:
                body(flags, in_refs, out_refs, *scratch_refs)

        results = pl.pallas_call(
            kernel,
            out_shape=[s for s, _ in outs] + [sds(a.shape, a.dtype) for a in carried],
            grid_spec=pltpu.PrefetchScalarGridSpec(
                num_scalar_prefetch=1,
                grid=grid,
                in_specs=[s for _, s in ins] + [ANY] * n_thr,
                out_specs=[s for _, s in outs] + [ANY] * n_thr,
                scratch_shapes=list(scratch),
            ),
            input_output_aliases={1 + n_in + j: n_out + j for j in range(n_thr)},
            compiler_params=pltpu.CompilerParams(vmem_limit_bytes=VMEM_BYTES),
            cost_estimate=pl.CostEstimate(flops=COSTS.get(name, 0) * 10**9, bytes_accessed=0, transcendentals=0),
            name=name,
        )(self.flags, *[a for a, _ in ins], *carried)
        self.token = results[-1]
        return results[:-1]


def copy_all(copies, sems):
    made = [(c, pltpu.make_async_copy(s, d, sems.at[n])) for n, (c, s, d) in enumerate(copies)]
    for act in ("start", "wait"):
        for cond, copy in made:
            if cond is None:
                getattr(copy, act)()
            else:
                pl.when(cond)(getattr(copy, act))


def column(row):
    return jnp.transpose(jnp.broadcast_to(row, (LANES, row.shape[1])))


def per_device(sizes, logits, expression, spatial, slide_ids, spot_mask, densities):
    spot_size = sizes["spot"]
    rows, spots = logits.shape
    genes = spatial.shape[1]
    spots_all = spots * spot_size
    genes_all = genes * sizes["gene"]
    slots = sizes["gene"]
    quarter = spots // sizes["cell"]
    cell, spot, gene = (lax.axis_index(a) for a in ("cell", "spot", "gene"))
    home = (gene // 2 == spot).astype(jnp.int32)
    side = (gene % 2).astype(jnp.int32)
    chain = Chain(jnp.stack([home, side, cell, gene, spot]).astype(jnp.int32))
    run = chain.run
    offsets = [sum(WIDTHS[:n]) for n in range(len(WIDTHS))]
    chunks = range(len(WIDTHS))
    group_width = [sum(WIDTHS[c] for c in g) for g in GROUPS]

    def over_core(v):
        return lax.ppermute(v, "cell", xor_pairs(4, 1))

    def over_x(v):
        return lax.ppermute(v, "cell", xor_pairs(4, 2))

    def over_gene(v, step):
        return lax.ppermute(v, "gene", xor_pairs(4, step))

    def over_spot(v, step=1):
        return lax.ppermute(v, "spot", xor_pairs(spot_size, step))

    def sum_spot(v):
        step = 1
        while step < spot_size:
            v = v + over_spot(v, step)
            step *= 2
        return v

    ids_row, mask_row = slide_ids.reshape(1, spots), spot_mask.reshape(1, spots)
    dens_row = densities.reshape(1, rows)

    expr = expression.reshape(2, rows, genes) if spot_size == 2 else None
    st, sent = {}, {}

    def start_swap(c):
        w = WIDTHS[c]
        if c == 0:
            sent["y0"] = over_spot(expr[:, :, :w])
            return

        def body(fl, i, out, sems):
            copy_all([(None, i[0].at[p, :, pl.ds(offsets[c], w)], out[0].at[p]) for p in range(2)], sems)

        shape = (2, rows, w)
        (v,) = run(
            f"swap{c}", body, [(expr, pl.BlockSpec(memory_space=pltpu.HBM))], [(sds(shape, BF), whole(shape))],
            scratch=[pltpu.SemaphoreType.DMA((2,))],
        )
        sent[f"y{c}"] = over_spot(v)

    def parted(c):
        lone = (rows - SHARED[c]) // 2
        return lone, lone + SHARED[c]

    def start_along(c):
        w = WIDTHS[c]
        cols, (_, far) = pl.ds(offsets[c], w), parted(c)

        def body(fl, i, out, sems):
            y, e = i
            at_home, away = fl[0] == 1, fl[0] == 0
            same, other = fl[1], 1 - fl[1]
            first, last = pl.ds(0, far), pl.ds(rows - far, far)
            copies = [
                (at_home, y.at[same, first, :], out[0]),
                (at_home, y.at[other, first, :], out[1]),
                (at_home, e.at[other, :, cols], out[2]),
                (away, e.at[same, last, cols], out[0]),
                (away, e.at[other, last, cols], out[1]),
                (away, y.at[other], out[2]),
            ]
            copy_all(copies, sems)

        shapes = ((far, w), (far, w), (rows, w))
        st["along", c] = run(
            f"along{c}", body, [(sent[f"y{c}"], ANY), (expr, ANY)], [(sds(v, BF), whole(v)) for v in shapes],
            scratch=[pltpu.SemaphoreType.DMA((6,))],
        )

    def along_send(c):
        a, b, n = run(f"alongsend{c}", None, through=st["along", c])
        sent[f"f2{c}"], sent[f"f3{c}"], sent[f"n{c}"] = over_gene(a, 2), over_gene(b, 3), over_gene(n, 1)

    def start_back(c):
        w = WIDTHS[c]
        lone, far = parted(c)

        def body(fl, i, out):
            @pl.when(fl[0] == 1)
            def _():
                for n in (0, 1):
                    out[0][n] = i[n][far - lone :, :]

            @pl.when(fl[0] == 0)
            def _():
                for n in (0, 1):
                    out[0][n] = i[n][:lone, :]

        shape = (2, lone, w)
        ins = [(sent[f"f{n}{c}"], whole((far, w))) for n in (2, 3)]
        (v,) = run(f"back{c}", body, ins, [(sds(shape, BF), whole(shape))])
        sent[f"s{c}"] = over_spot(v)

    def wait_for(name):
        run("wait" + name.split("+")[0], None, after=[sent[n] for n in name.split("+")])

    def members_of(_):
        def body(fl, i, out):
            ids, valid = column(i[0][...].astype(F32)), column(i[1][...].astype(F32))
            lane = lax.broadcasted_iota(jnp.int32, (quarter, LANES), 1)
            inside = (lane < SLIDES) & (lane.astype(F32) == ids) & (valid == 1.0)
            out[0][...] = jnp.where(inside, 1.0, jnp.where(lane == SLIDES, valid, 0.0))

        row, tall = pl.BlockSpec((1, quarter), lambda g, f: (0, f[2])), whole((quarter, LANES))
        (st["member"],) = run("member", body, [(ids_row, row), (mask_row, row)], [(sds((quarter, LANES), F32), tall)])

    def totals(n):
        sp = whole((8, spots))
        if n == 0:

            def body(fl, i, out):
                out[0][...] = jnp.zeros((8, spots), F32)
                out[0][0:1, :] = jnp.sum(jnp.exp(i[0][...].astype(F32)), axis=0, keepdims=True)
                out[0][1:2, :] = jnp.broadcast_to(jnp.sum(i[1][...]), (1, spots))

            ins = [(logits, whole(logits.shape)), (dens_row, whole(dens_row.shape))]
            (v,) = run("totals", body, ins, [(sds((8, spots), F32), sp)])
            st["tot"] = lax.psum(v, "cell")
            for s in (1, 2, 3):
                sent[f"ez{s}"] = over_gene(st["tot"], s)
        else:
            blk = 2 * LANES

            def body(fl, i, out):
                tot = (i[1][...] + i[2][...]) + (i[3][...] + i[4][...])
                out[3][...] = tot
                inv = 1.0 / tot[0:1, :]
                log_tot = jnp.log(tot[0:1, :])
                vals = i[0][...].astype(F32)
                prob = jnp.exp(vals) * inv
                prob_t = jnp.transpose(prob.astype(BF))
                for q in range(sizes["cell"]):
                    at = pl.multiple_of((fl[2] ^ q) * quarter, quarter)
                    out[0][pl.ds(at, quarter), :] = prob_t[q * quarter : (q + 1) * quarter]
                folded = sum(prob[:, n : n + LANES] for n in range(0, spots, LANES))
                row_sums = jnp.sum(jnp.transpose(folded), axis=0, keepdims=True)
                out[1][...] = jnp.broadcast_to(row_sums, (8, blk))

                @pl.when(pl.program_id(0) == 0)
                def _():
                    out[2][...] = jnp.zeros((8, spots), F32)

                out[2][0:1, :] -= jnp.sum(prob * (vals - log_tot), axis=0, keepdims=True)

            parts = [st["tot"]] + [sent[f"ez{s}"] for s in (1, 2, 3)]
            pt, mass, ent, st["tot"] = run(
                "prob", body,
                [(logits, pl.BlockSpec((blk, spots), lambda g, f: (g, 0)))] + [(a, sp) for a in parts],
                [
                    (sds((spots, rows), BF), pl.BlockSpec((spots, blk), lambda g, f: (0, g))),
                    (sds((8, rows), F32), pl.BlockSpec((8, blk), lambda g, f: (0, g))),
                    (sds((8, spots), F32), sp),
                    (sds((8, spots), F32), sp),
                ],
                grid=(rows // blk,),
            )
            st["pt"], st["ent"] = pt, ent
            st["mass"] = mass if spot_size == 2 else sum_spot(mass)
            if spot_size == 2:
                sent["my"] = over_spot(mass)

    def shares(_):
        masses = [st["mass"]] + ([sent["my"]] if spot_size == 2 else [])

        def body(fl, i, out):
            mass = i[2][0:1, :]
            for extra in i[3:]:
                mass = mass + extra[0:1, :]
            share = i[0][...] / i[1][1:2, 0:1]
            out[0][...] = column(share / mass)
            kl = jnp.sum(share * (jnp.log(share) - jnp.log(mass / spots_all)))
            out[1][...] = jnp.broadcast_to(kl, (8, LANES))

        st["sm"], st["kl"] = run(
            "shares", body,
            [(dens_row, whole(dens_row.shape)), (st["tot"], whole((8, spots)))]
            + [(m, whole((8, rows))) for m in masses],
            [(sds((rows, LANES), F32), whole((rows, LANES))), (sds((8, LANES), F32), whole((8, LANES)))],
        )

    def halves_of(g):
        shape = (quarter, slots * group_width[g])
        return [(sds(shape, F32), whole(shape))] * 2

    def forward(g):
        members, wide_all = GROUPS[g], group_width[g] * slots
        shape = (2, quarter, wide_all)
        outs = [(sds((rows, slots * WIDTHS[c]), BF), whole((rows, slots * WIDTHS[c]))) for c in members]
        outs += [(sds(shape, F32), whole(shape))]
        outs += halves_of(g)

        late = members[-1] if spot_size == 2 and g == len(GROUPS) - 1 else None

        def product(pt, efs, keep, *send, direct=None):
            done = 0
            low, high = send
            for c, ef in zip(members, efs):
                w = WIDTHS[c]
                if c == late:
                    near = jnp.dot(pt[...], ef[:, : 2 * w], preferred_element_type=F32)
                    lone, size = parted(c)
                    at = pl.ds(pl.multiple_of(direct * lone, LANES), size)
                    far = jnp.dot(pt[:, at], ef[at, 2 * w :], preferred_element_type=F32)
                    acc = jnp.concatenate([near, far], axis=1)
                else:
                    acc = jnp.dot(pt[...], ef[...], preferred_element_type=F32)
                for q, ref in enumerate((keep.at[0], low, keep.at[1], high)):
                    rows_q = acc[q * quarter : (q + 1) * quarter]
                    for s in range(slots):
                        base = s * group_width[g] + done
                        ref[:, base : base + w] = rows_q[:, s * w : (s + 1) * w]
                done += w

        if spot_size == 2:

            def body(fl, i, out, sems):
                pt, e = i[:2]
                at_home, away = fl[0] == 1, fl[0] == 0
                copies = []
                for m, c in enumerate(members):
                    w, ef = WIDTHS[c], out[m]
                    y, n, f2, f3 = i[2 + 5 * m : 6 + 5 * m]
                    lone, far = parted(c)
                    top, low = pl.ds(0, lone), pl.ds(rows - lone, lone)
                    first, last = pl.ds(0, far), pl.ds(rows - far, far)
                    copies += [
                        (at_home, e.at[fl[1], :, pl.ds(offsets[c], w)], ef.at[:, pl.ds(0, w)]),
                        (away, y.at[fl[1]], ef.at[:, pl.ds(0, w)]),
                        (None, n, ef.at[:, pl.ds(w, w)]),
                    ]
                    for part, f in enumerate((f2, f3)):
                        cols = pl.ds((2 + part) * w, w)
                        copies += [(at_home, f, ef.at[last, cols]), (away, f, ef.at[first, cols])]
                        if c != late:
                            s = i[6 + 5 * m]
                            copies += [(at_home, s.at[part], ef.at[top, cols]), (away, s.at[part], ef.at[low, cols])]
                copy_all(copies, sems)
                product(pt, out[: len(members)], *out[len(members) :], direct=fl[0])

            ins = [(st["pt"], whole((spots, rows))), (expr, ANY)]
            ins += [
                (a, ANY)
                for c in members
                for a in (*(sent[f"{k}{c}"] for k in ("y", "n", "f2", "f3")), *([] if c == late else [sent[f"s{c}"]]))
            ]
            scratch = [pltpu.SemaphoreType.DMA((12 * len(members),))]
        else:

            def body(fl, i, out):
                for m, c in enumerate(members):
                    w = WIDTHS[c]
                    for s in range(slots):
                        out[m][:, s * w : (s + 1) * w] = i[1 + m * slots + s][...]
                product(i[0], out[: len(members)], *out[len(members) :])

            def at_chunk(c):
                return pl.BlockSpec((rows, WIDTHS[c]), lambda *_: (0, offsets[c] // WIDTHS[c]))

            ins = [(st["pt"], whole((spots, rows)))] + [(a, at_chunk(c)) for c in members for a in st["pieces"]]
            scratch = []
        results = run(f"forward{g}", body, ins, outs, scratch=scratch)
        for c, ef in zip(members, results):
            st["e", c] = ef
        st["r", g], st["send", g] = results[len(members)], results[len(members) + 1 :]

    def forward_late(g):
        c = GROUPS[g][-1]
        w, wide = WIDTHS[c], slots * group_width[g]
        shape, lone = (2, quarter, wide), parted(c)[0]

        def body(fl, i, out, sems):
            pt, swapped, keep, low, high = i
            at = pl.ds(pl.multiple_of((1 - fl[0]) * (rows - lone), LANES), lone)
            copy_all([(None, swapped.at[n], out[3].at[at, pl.ds((2 + n) * w, w)]) for n in (0, 1)], sems)
            both = jnp.concatenate([swapped[0], swapped[1]], axis=1)
            acc = jnp.dot(pt[:, at], both, preferred_element_type=F32)
            for new, old in zip(out, (keep, low, high)):
                new[...] = old[...]
            for q, ref in enumerate((out[0].at[0], out[1], out[0].at[1], out[2])):
                for n in (0, 1):
                    base = (3 + n) * group_width[g] - w
                    ref[:, base : base + w] += acc[q * quarter : (q + 1) * quarter, n * w : (n + 1) * w]

        one = whole((quarter, wide))
        ins = [(st["pt"], whole((spots, rows))), (sent[f"s{c}"], whole((2, lone, w)))]
        ins += [(st["r", g], whole(shape))] + [(a, one) for a in st["send", g]]
        st["r", g], *send, st["e", c] = run(
            f"forwardlate{g}", body, ins, [(sds(shape, F32), whole(shape)), *halves_of(g)], through=[st["e", c]],
            scratch=[pltpu.SemaphoreType.DMA((2,))],
        )
        send_core(g, send)

    def send_core(g, send):
        for n, part in enumerate(send):
            sent[f"rc{n}{g}"] = over_core(part)

    def forward_send(g):
        send_core(g, run(f"send{g}", None, through=st["send", g]))

    def reduce_core(g):
        wide = slots * group_width[g]
        shape, one = (2, quarter, wide), (quarter, wide)

        single = 0 < g < len(GROUPS) - 1

        def body(fl, i, out):
            for n in (0, 1):
                out[n][0:quarter, :] = i[0][n] + i[1 + n][...]
            if single:
                out[1][quarter:, :] = jnp.zeros((PAD, wide), F32)

        ins = [(st["r", g], whole(shape))]
        ins += [(sent[f"rc{n}{g}"], whole(one)) for n in (0, 1)]
        more = (quarter + PAD, wide) if single else one
        st["r", g], b = run(f"core{g}", body, ins, [(sds(one, F32), whole(one)), (sds(more, F32), whole(more))])
        sent[f"rx{g}"] = over_x(b)

    sum_groups = [[g for g in z] for z in SUMS]
    sum_width = [sum(group_width[g] for g in z) for z in SUMS]

    def add_x(g):
        one = whole((quarter, slots * group_width[g]))

        def body(fl, i, out):
            out[0][...] = i[0][...] + i[1][0:quarter, :]

        ins = [(st["r", g], one), (sent[f"rx{g}"], whole(sent[f"rx{g}"].shape))]
        (st["added", g],) = run(f"addx{g}", body, ins, [(sds(one.block_shape, F32), one)])

    def reduce_x(z):
        members, w = sum_groups[z], sum_width[z]
        part = (quarter, w)
        in_halves = z < len(SUMS) - 1

        def body(fl, i, out):
            done, i = 0, list(i)
            for g in members:
                v = group_width[g]
                refs = [i.pop(0) for _ in parts_of[g]]
                for s in range(slots):
                    at = slice(s * v, (s + 1) * v)
                    value = sum(ref[0:quarter, at] for ref in refs)
                    if in_halves and s >= 2:
                        out[2][s - 2, :, done : done + v] = value
                    else:
                        out[s][:, done : done + v] = value
                done += v

        parts_of = {g: [st["added", g]] if ("added", g) in st else [st["r", g], sent[f"rx{g}"]] for g in members}
        ins = [(a, whole(a.shape)) for g in members for a in parts_of[g]]
        outs = [(sds(part, F32), whole(part))] * (2 if in_halves else slots)
        if in_halves:
            outs += [(sds((2, *part), F32), whole((2, *part)))]
        parts = run(f"x{z}", body, ins, outs)
        if in_halves:
            st["z", z] = parts[:2]
            sent[f"rz2{z}"] = over_gene(parts[2], 2)
        else:
            st["z", z] = parts[:1]
            for s in (3, 2, 1):
                sent[f"rz{s}{z}"] = over_gene(parts[s], s)

    def reduce_half(z):
        part = (quarter, sum_width[z])

        def body(fl, i, out):
            for n in (0, 1):
                out[n][...] = i[n][...] + i[2][n]

        ins = [(a, whole(part)) for a in st["z", z]] + [(sent[f"rz2{z}"], whole((2, *part)))]
        a, b = run(f"half{z}", body, ins, [(sds(part, F32), whole(part))] * 2)
        st["z", z], sent[f"rz1{z}"] = [a], over_gene(b, 1)

    def reduce_gene(z):
        part = (quarter, sum_width[z])
        others = [sent[f"rz{s}{z}"] for s in ((1,) if z < len(SUMS) - 1 else (1, 2, 3))]

        def body(fl, i, out):
            out[0][...] = sum(ref[...] for ref in i)

        ins = [(a, whole(part)) for a in (*st["z", z], *others)]
        (st["sum", z],) = run(f"gene{z}", body, ins, [(sds(part, F32), whole(part))])

    steps = {
        "Y": start_swap, "A": start_along, "a": along_send, "S": start_back,
        "e": totals, "m": shares, "F": forward, "f": forward_send, "G": forward_late, "b": members_of,
        "P": reduce_core, "X": add_x, "Q": reduce_x,
        "U": reduce_half, "R": reduce_gene,
    }
    if spot_size != 2:
        full = lax.all_gather(expression, "spot", axis=0, tiled=True).reshape(slots, rows, genes)
        pieces = [lax.dynamic_index_in_dim(full, gene ^ s, 0, False) for s in range(slots)]
        st["pieces"] = [pieces[0]] + [over_gene(pieces[s], s) for s in (1, 2, 3)]
    for word in " ".join(ORDER).split():
        if word[:2] == "w:":
            if spot_size == 2 or word == "w:ez1+ez2+ez3":
                wait_for(word[2:])
        elif spot_size != 2 and word[0] == "G":
            forward_send(int(word[1]))
        elif spot_size == 2 or word[0] not in "YAaS":
            steps[word[0]](int(word[1]))

    n_ch, n_sum = len(WIDTHS), len(SUMS)
    starts = [offsets[GROUPS[z[0]][0]] for z in SUMS]
    preds = [(st["sum", z], whole((quarter, sum_width[z]))) for z in range(n_sum)]
    mine = (spatial, pl.BlockSpec((quarter, genes), lambda g, f: (f[2], 0)))
    memb = (st["member"], whole((quarter, LANES)))
    gene_spec, spot_spec = whole((16, genes)), whole((8, quarter))

    def stats_body(fl, i, out):
        memb = i[0]
        cols = [jnp.broadcast_to(memb[:, k : k + 1], (quarter, LANES)) for k in range(SLIDES)]
        valid = jnp.sum(memb[:, SLIDES : SLIDES + 1])
        out[0][...] = jnp.broadcast_to(valid, (16, genes))
        totals = [jnp.zeros((quarter, LANES), F32) for _ in range(3)]
        for g in range(n_sum):
            for o in range(0, sum_width[g], LANES):
                at = slice(starts[g] + o, starts[g] + o + LANES)
                pr, ta = i[2 + g][:, o : o + LANES], i[1][:, at].astype(F32)
                for j, v in enumerate((pr * ta, pr * pr, ta * ta)):
                    totals[j] += v
                    for k in range(SLIDES):
                        n = 3 * j + k
                        out[0][n : n + 1, at] = jnp.sum(cols[k] * v, axis=0, keepdims=True)
        out[1][...] = jnp.zeros((8, quarter), F32)
        for j in range(3):
            out[1][j : j + 1, :] = jnp.sum(jnp.transpose(totals[j]), axis=0, keepdims=True)

    gene_sums, spot_sums = run(
        "stats", stats_body, [memb, mine, *preds],
        [(sds((16, genes), F32), gene_spec), (sds((8, quarter), F32), spot_spec)],
    )
    far = {s: over_gene(spot_sums, s) for s in (3, 2, 1)}
    spot_parts = [spot_sums] + [far[s] for s in (1, 2, 3)]
    gene_sums = gene_sums + over_core(gene_sums)
    gene_sums = gene_sums + over_x(gene_sums)
    gene_parts = [gene_sums, over_spot(gene_sums)] if spot_size == 2 else [sum_spot(gene_sums)]

    run("spots", None, after=spot_parts)

    def grads_body(fl, i, out):
        memb, ta_ref, kl, ent = i[:4]
        i = i[4:]
        spot_in, gene_in, preds_in = i[:4], i[4 : 4 + len(gene_parts)], i[4 + len(gene_parts) :]
        scale = -1.0 / (SLIDES * genes_all)
        sums = sum(ref[...] for ref in gene_in)
        num, psq, tsq = sums[0:3], sums[3:6], sums[6:9]
        p_floor, t_floor = jnp.maximum(psq, 1.0), jnp.maximum(tsq, 1.0)
        root = jnp.sqrt(p_floor * t_floor)
        cosine = num / root
        w_t = scale / root
        w_p = jnp.where(psq > 1.0, -scale * cosine / p_floor, 0.0)
        valid_total = jnp.maximum(sums[9, 0], 1.0)
        spot_all = (spot_in[0][...] + spot_in[1][...]) + (spot_in[2][...] + spot_in[3][...])
        s_num, s_p, s_t = [column(spot_all[n : n + 1, :]) for n in range(3)]
        s_p, s_t = s_p + 1e-06, s_t + 1e-06
        root = jnp.sqrt(s_p * s_t)
        cos_spot = s_num / root
        valid = jnp.broadcast_to(memb[:, SLIDES : SLIDES + 1], (quarter, LANES))
        coef = -valid / valid_total
        coef_t, coef_p = coef / root, -coef * cos_spot / s_p
        first = [(fl[n] == 0).astype(F32) for n in (2, 4, 3)]
        terms = [
            jnp.sum(cosine) * first[0] * first[1],
            jnp.sum((valid * cos_spot)[:, 0:1]) * first[2],
            kl[0, 0] * first[1],
            jnp.sum(ent[0:1, :]),
            valid_total * first[0] * first[1] * first[2],
        ]
        lane = lax.broadcasted_iota(jnp.int32, (8, spots), 1)
        value = jnp.zeros((8, spots), F32)
        for n, term in enumerate(terms):
            value = jnp.where(lane == n, term, value)
        out[1][...] = value
        cols = [jnp.broadcast_to(memb[:, k : k + 1], (quarter, LANES)) for k in range(SLIDES)]
        for g in range(n_sum):
            for o in range(0, sum_width[g], LANES):
                at = slice(starts[g] + o, starts[g] + o + LANES)
                f_t, f_p = coef_t, coef_p
                for k in range(SLIDES):
                    f_t = f_t + cols[k] * w_t[k : k + 1, at]
                    f_p = f_p + cols[k] * w_p[k : k + 1, at]
                out[0][:, at] = (f_t * ta_ref[:, at].astype(F32) + f_p * preds_in[g][:, o : o + LANES]).astype(BF)

    row8, flat = whole((8, spots)), whole((8, LANES))
    ins = [memb, mine, (st["kl"], flat), (st["ent"], row8)]
    ins += [(a, spot_spec) for a in spot_parts] + [(a, gene_spec) for a in gene_parts] + preds
    grad, terms = run(
        "grads", grads_body, ins,
        [(sds((quarter, genes), BF), whole((quarter, genes))), (sds((8, spots), F32), row8)],
    )
    terms = [terms, over_spot(terms)] if spot_size == 2 else [sum_spot(terms)]
    far = {s: over_gene(grad, s) for s in (3, 2, 1)}
    others = [far[s] for s in (1, 2, 3)]
    grad_x = over_x(grad)
    own = [grad, over_core(grad), grad_x, over_core(grad_x)]
    one, rest = (quarter, genes), (slots - 1, quarter, genes)
    row_blk = rows // 4

    def by_rows(width, size=row_blk):
        return pl.BlockSpec((size, width), lambda g, f: (g, 0))

    def place(fl, refs, target, sems):
        copies = []
        for b, ref in enumerate(refs):
            at = pl.ds(pl.multiple_of((fl[2] ^ b) * quarter, quarter), quarter)
            copies.append((None, ref, target(at)))
        copy_all(copies, sems)

    def slot_product(efs, slot, held):
        left = jnp.concatenate([ef[:, slot * w : (slot + 1) * w] for w, ef in zip(WIDTHS, efs)], axis=1)
        return lax.dot_general(left, held, (((1,), (1,)), ((), ())), preferred_element_type=F32)

    def gather_body(fl, i, out):
        for n in range(slots - 1):
            out[0][n] = i[n][...]

    (rest_z,) = run(
        "gather", gather_body, [(a, whole(one)) for a in others], [(sds(rest, BF), whole(rest))], after=[grad_x, *terms[1:]]
    )
    rest_x = over_x(rest_z)

    def own_body(fl, i, out, held, sems):
        sm, efs, gs = i[0], i[1 : 1 + n_ch], i[1 + n_ch :]

        @pl.when(pl.program_id(0) == 0)
        def _():
            place(fl, gs, lambda at: held.at[at, :], sems)

        out[0][...] = slot_product(efs, 0, held[...]) - jnp.broadcast_to(sm[:, 0:1], (row_blk, spots))

    ins = [(st["sm"], by_rows(LANES))] + [(st["e", c], by_rows(WIDTHS[c])) for c in chunks]
    ins += [(a, ANY) for a in own]
    (own_part,) = run(
        "own", own_body, ins, [(sds((rows, spots), F32), by_rows(spots))], grid=(rows // row_blk,),
        scratch=[pltpu.VMEM((spots, genes), BF), pltpu.SemaphoreType.DMA((len(own),))],
    )

    (rest_x,) = run("rest", None, through=[rest_x])
    grads = [rest_z, over_core(rest_z), rest_x, over_core(rest_x)]

    def backward_body(fl, i, out, held, sems):
        lg, tot, before = i[:3]
        efs, gs, terms = i[3 : 3 + n_ch], i[3 + n_ch : 7 + n_ch], i[7 + n_ch :]

        @pl.when(pl.program_id(0) == 0)
        def _():
            row = lax.broadcasted_iota(jnp.int32, (8, spots), 0)
            out[1][...] = jnp.where(row == 0, 0.0, sum(ref[...] for ref in terms))
            place(fl, gs, lambda at: held.at[:, at, :], sems)

        acc = before[...]
        for s in range(1, slots):
            acc += slot_product(efs, s, held[s - 1])
        out[0][...] = acc
        prob = jnp.exp(lg[...].astype(F32)) * (1.0 / tot[0:1, :])
        out[1][0:1, :] += jnp.sum(prob * acc, axis=0, keepdims=True)

    ins = [(logits, by_rows(spots)), (st["tot"], row8), (own_part, by_rows(spots))]
    ins += [(st["e", c], by_rows(slots * WIDTHS[c])) for c in chunks]
    ins += [(a, ANY) for a in grads] + [(a, row8) for a in terms]
    grad_probs, v = run(
        "backward", backward_body, ins,
        [(sds((rows, spots), F32), by_rows(spots)), (sds((8, spots), F32), row8)],
        grid=(rows // row_blk,),
        scratch=[pltpu.VMEM((slots - 1, spots, genes), BF), pltpu.SemaphoreType.DMA((len(grads),))],
    )

    v = (v + over_gene(v, 1)) + (over_gene(v, 2) + over_gene(v, 3))
    v = v + over_x(v)
    v = v + over_core(v)

    def final_body(fl, i, out):
        prob = jnp.exp(i[0][...].astype(F32)) * (1.0 / i[1][0:1, :])
        out[0][...] = prob * (i[2][...] - i[3][0:1, :])

        @pl.when(pl.program_id(0) == 0)
        def _():
            sums = [i[3][1, n] for n in range(5)]
            gene_term, spot_term = sums[0] / (SLIDES * genes_all), sums[1] / sums[4]
            divergence, entropy = sums[2], sums[3] / spots_all
            values = (divergence - gene_term - spot_term, gene_term, spot_term, divergence, entropy)
            for n, value in enumerate(values):
                out[1][n] = value

    last_blk = rows // 2
    blk = by_rows(spots, last_blk)
    grad_logits, loss_terms = run(
        "final", final_body, [(logits, blk), (st["tot"], row8), (grad_probs, blk), (v, row8)],
        [(sds((rows, spots), F32), blk), (sds((5,), F32), pl.BlockSpec(memory_space=pltpu.SMEM))],
        grid=(rows // last_blk,),
    )
    return (loss_terms, grad_logits)


def solution(mesh):
    return jax.shard_map(
        functools.partial(per_device, dict(mesh.shape)),
        mesh=mesh,
        in_specs=(
            P(("cell", "gene"), "spot"),
            P(("cell", "spot"), "gene"),
            P("spot", "gene"),
            P("spot"),
            P("spot"),
            P(("cell", "gene")),
        ),
        out_specs=(P(), P(("cell", "gene"), "spot")),
        check_vma=False,
    )
```

```python
import functools
import jax
import jax.numpy as jnp
from jax import lax
from jax.experimental import pallas as pl
from jax.experimental.pallas import tpu as pltpu
from jax.sharding import PartitionSpec as P

SLIDES = 3
LANES = 128
PAD = 8
ANY = pl.BlockSpec(memory_space=pl.ANY)
BF = jnp.bfloat16
F32 = jnp.float32
SHARED = (0, 0, 0, 256)
VMEM_BYTES = 14 * 1024 * 1024
COSTS = {"spots": 1, "back3": 1, "waits2": 3, "addx1": 9, "half0": 3}
WIDTHS = (128, 128, 128, 128)
GROUPS = ((0, 1), (2,), (3,))
SUMS = ((0,), (1, 2))
ORDER = (
    "Y0 e0 Y1 w:ez1+ez2+ez3",
    "Y2 A0 a0 e3",
    "b0 A1 Y3 w:f20+f30+n0",
    "a1 A2 w:f21+f31+n1 a2",
    "S0 A3 w:f22+f32+n2 a3",
    "S1 w:s0 S2 w:s1",
    "F0 w:f23+f33+n3 S3 f0",
    "P0 w:s2 F1 f1",
    "P1 F2 Q0 G2",
    "P2 X1 Q1 U0",
    "m0 R1 R0",
)


def sds(shape, dtype):
    return jax.ShapeDtypeStruct(shape, dtype)


def whole(shape):
    zeros = (0,) * len(shape)
    return pl.BlockSpec(shape, lambda *_: zeros)


def xor_pairs(size, step):
    return [(n, n ^ step) for n in range(size)]


class Chain:
    def __init__(self, flags):
        self.flags = flags
        self.token = jnp.zeros((8, LANES), F32)

    def run(self, name, body, ins=(), outs=(), after=(), through=(), grid=(1,), scratch=()):
        ins = [*ins, *((a, ANY) for a in after)]
        carried = (*through, self.token)
        n_in, n_out, n_thr = len(ins), len(outs), len(carried)

        def kernel(flags, *refs):
            in_refs = refs[:n_in]
            out_refs = refs[n_in + n_thr : n_in + 2 * n_thr + n_out - 1]
            scratch_refs = refs[n_in + 2 * n_thr + n_out :]
            if body is not None:
                body(flags, in_refs, out_refs, *scratch_refs)

        results = pl.pallas_call(
            kernel,
            out_shape=[s for s, _ in outs] + [sds(a.shape, a.dtype) for a in carried],
            grid_spec=pltpu.PrefetchScalarGridSpec(
                num_scalar_prefetch=1,
                grid=grid,
                in_specs=[s for _, s in ins] + [ANY] * n_thr,
                out_specs=[s for _, s in outs] + [ANY] * n_thr,
                scratch_shapes=list(scratch),
            ),
            input_output_aliases={1 + n_in + j: n_out + j for j in range(n_thr)},
            compiler_params=pltpu.CompilerParams(vmem_limit_bytes=VMEM_BYTES),
            cost_estimate=pl.CostEstimate(flops=COSTS.get(name, 0) * 10**9, bytes_accessed=0, transcendentals=0),
            name=name,
        )(self.flags, *[a for a, _ in ins], *carried)
        self.token = results[-1]
        return results[:-1]


def copy_all(copies, sems):
    made = [(c, pltpu.make_async_copy(s, d, sems.at[n])) for n, (c, s, d) in enumerate(copies)]
    for act in ("start", "wait"):
        for cond, copy in made:
            if cond is None:
                getattr(copy, act)()
            else:
                pl.when(cond)(getattr(copy, act))


def column(row):
    return jnp.transpose(jnp.broadcast_to(row, (LANES, row.shape[1])))


def per_device(sizes, logits, expression, spatial, slide_ids, spot_mask, densities):
    spot_size = sizes["spot"]
    rows, spots = logits.shape
    genes = spatial.shape[1]
    spots_all = spots * spot_size
    genes_all = genes * sizes["gene"]
    slots = sizes["gene"]
    quarter = spots // sizes["cell"]
    cell, spot, gene = (lax.axis_index(a) for a in ("cell", "spot", "gene"))
    home = (gene // 2 == spot).astype(jnp.int32)
    side = (gene % 2).astype(jnp.int32)
    chain = Chain(jnp.stack([home, side, cell, gene, spot]).astype(jnp.int32))
    run = chain.run
    offsets = [sum(WIDTHS[:n]) for n in range(len(WIDTHS))]
    chunks = range(len(WIDTHS))
    group_width = [sum(WIDTHS[c] for c in g) for g in GROUPS]

    def over_core(v):
        return lax.ppermute(v, "cell", xor_pairs(4, 1))

    def over_x(v):
        return lax.ppermute(v, "cell", xor_pairs(4, 2))

    def over_gene(v, step):
        return lax.ppermute(v, "gene", xor_pairs(4, step))

    def over_spot(v, step=1):
        return lax.ppermute(v, "spot", xor_pairs(spot_size, step))

    def sum_spot(v):
        step = 1
        while step < spot_size:
            v = v + over_spot(v, step)
            step *= 2
        return v

    ids_row, mask_row = slide_ids.reshape(1, spots), spot_mask.reshape(1, spots)
    dens_row = densities.reshape(1, rows)

    expr = expression.reshape(2, rows, genes) if spot_size == 2 else None
    st, sent = {}, {}

    def start_swap(c):
        w = WIDTHS[c]
        if c == 0:
            sent["y0"] = over_spot(expr[:, :, :w])
            return

        def body(fl, i, out, sems):
            copy_all([(None, i[0].at[p, :, pl.ds(offsets[c], w)], out[0].at[p]) for p in range(2)], sems)

        shape = (2, rows, w)
        (v,) = run(
            f"swap{c}", body, [(expr, pl.BlockSpec(memory_space=pltpu.HBM))], [(sds(shape, BF), whole(shape))],
            scratch=[pltpu.SemaphoreType.DMA((2,))],
        )
        sent[f"y{c}"] = over_spot(v)

    def parted(c):
        lone = (rows - SHARED[c]) // 2
        return lone, lone + SHARED[c]

    def start_along(c):
        w = WIDTHS[c]
        cols, (_, far) = pl.ds(offsets[c], w), parted(c)

        def body(fl, i, out, sems):
            y, e = i
            at_home, away = fl[0] == 1, fl[0] == 0
            same, other = fl[1], 1 - fl[1]
            first, last = pl.ds(0, far), pl.ds(rows - far, far)
            copies = [
                (at_home, y.at[same, first, :], out[0]),
                (at_home, y.at[other, first, :], out[1]),
                (at_home, e.at[other, :, cols], out[2]),
                (away, e.at[same, last, cols], out[0]),
                (away, e.at[other, last, cols], out[1]),
                (away, y.at[other], out[2]),
            ]
            copy_all(copies, sems)

        shapes = ((far, w), (far, w), (rows, w))
        st["along", c] = run(
            f"along{c}", body, [(sent[f"y{c}"], ANY), (expr, ANY)], [(sds(v, BF), whole(v)) for v in shapes],
            scratch=[pltpu.SemaphoreType.DMA((6,))],
        )

    def along_send(c):
        a, b, n = run(f"alongsend{c}", None, through=st["along", c])
        sent[f"f2{c}"], sent[f"f3{c}"], sent[f"n{c}"] = over_gene(a, 2), over_gene(b, 3), over_gene(n, 1)

    def start_back(c):
        w = WIDTHS[c]
        lone, far = parted(c)

        def body(fl, i, out):
            @pl.when(fl[0] == 1)
            def _():
                for n in (0, 1):
                    out[0][n] = i[n][far - lone :, :]

            @pl.when(fl[0] == 0)
            def _():
                for n in (0, 1):
                    out[0][n] = i[n][:lone, :]

        shape = (2, lone, w)
        ins = [(sent[f"f{n}{c}"], whole((far, w))) for n in (2, 3)]
        (v,) = run(f"back{c}", body, ins, [(sds(shape, BF), whole(shape))])
        sent[f"s{c}"] = over_spot(v)

    def wait_for(name):
        run("wait" + name.split("+")[0], None, after=[sent[n] for n in name.split("+")])

    def members_of(_):
        def body(fl, i, out):
            ids, valid = column(i[0][...].astype(F32)), column(i[1][...].astype(F32))
            lane = lax.broadcasted_iota(jnp.int32, (quarter, LANES), 1)
            inside = (lane < SLIDES) & (lane.astype(F32) == ids) & (valid == 1.0)
            out[0][...] = jnp.where(inside, 1.0, jnp.where(lane == SLIDES, valid, 0.0))

        row, tall = pl.BlockSpec((1, quarter), lambda g, f: (0, f[2])), whole((quarter, LANES))
        (st["member"],) = run("member", body, [(ids_row, row), (mask_row, row)], [(sds((quarter, LANES), F32), tall)])

    def totals(n):
        sp = whole((8, spots))
        if n == 0:

            def body(fl, i, out):
                out[0][...] = jnp.zeros((8, spots), F32)
                out[0][0:1, :] = jnp.sum(jnp.exp(i[0][...].astype(F32)), axis=0, keepdims=True)
                out[0][1:2, :] = jnp.broadcast_to(jnp.sum(i[1][...]), (1, spots))

            ins = [(logits, whole(logits.shape)), (dens_row, whole(dens_row.shape))]
            (v,) = run("totals", body, ins, [(sds((8, spots), F32), sp)])
            st["tot"] = lax.psum(v, "cell")
            for s in (1, 2, 3):
                sent[f"ez{s}"] = over_gene(st["tot"], s)
        else:
            blk = 2 * LANES

            def body(fl, i, out):
                tot = (i[1][...] + i[2][...]) + (i[3][...] + i[4][...])
                out[3][...] = tot
                inv = 1.0 / tot[0:1, :]
                log_tot = jnp.log(tot[0:1, :])
                vals = i[0][...].astype(F32)
                prob = jnp.exp(vals) * inv
                prob_t = jnp.transpose(prob.astype(BF))
                for q in range(sizes["cell"]):
                    at = pl.multiple_of((fl[2] ^ q) * quarter, quarter)
                    out[0][pl.ds(at, quarter), :] = prob_t[q * quarter : (q + 1) * quarter]
                folded = sum(prob[:, n : n + LANES] for n in range(0, spots, LANES))
                row_sums = jnp.sum(jnp.transpose(folded), axis=0, keepdims=True)
                out[1][...] = jnp.broadcast_to(row_sums, (8, blk))

                @pl.when(pl.program_id(0) == 0)
                def _():
                    out[2][...] = jnp.zeros((8, spots), F32)

                out[2][0:1, :] -= jnp.sum(prob * (vals - log_tot), axis=0, keepdims=True)

            parts = [st["tot"]] + [sent[f"ez{s}"] for s in (1, 2, 3)]
            pt, mass, ent, st["tot"] = run(
                "prob", body,
                [(logits, pl.BlockSpec((blk, spots), lambda g, f: (g, 0)))] + [(a, sp) for a in parts],
                [
                    (sds((spots, rows), BF), pl.BlockSpec((spots, blk), lambda g, f: (0, g))),
                    (sds((8, rows), F32), pl.BlockSpec((8, blk), lambda g, f: (0, g))),
                    (sds((8, spots), F32), sp),
                    (sds((8, spots), F32), sp),
                ],
                grid=(rows // blk,),
            )
            st["pt"], st["ent"] = pt, ent
            st["mass"] = mass if spot_size == 2 else sum_spot(mass)
            if spot_size == 2:
                sent["my"] = over_spot(mass)

    def shares(_):
        masses = [st["mass"]] + ([sent["my"]] if spot_size == 2 else [])

        def body(fl, i, out):
            mass = i[2][0:1, :]
            for extra in i[3:]:
                mass = mass + extra[0:1, :]
            share = i[0][...] / i[1][1:2, 0:1]
            out[0][...] = column(share / mass)
            kl = jnp.sum(share * (jnp.log(share) - jnp.log(mass / spots_all)))
            out[1][...] = jnp.broadcast_to(kl, (8, LANES))

        st["sm"], st["kl"] = run(
            "shares", body,
            [(dens_row, whole(dens_row.shape)), (st["tot"], whole((8, spots)))]
            + [(m, whole((8, rows))) for m in masses],
            [(sds((rows, LANES), F32), whole((rows, LANES))), (sds((8, LANES), F32), whole((8, LANES)))],
        )

    def halves_of(g):
        shape = (quarter, slots * group_width[g])
        return [(sds(shape, F32), whole(shape))] * 2

    def forward(g):
        members, wide_all = GROUPS[g], group_width[g] * slots
        shape = (2, quarter, wide_all)
        outs = [(sds((rows, slots * WIDTHS[c]), BF), whole((rows, slots * WIDTHS[c]))) for c in members]
        outs += [(sds(shape, F32), whole(shape))]
        outs += halves_of(g)

        late = members[-1] if spot_size == 2 and g == len(GROUPS) - 1 else None

        def product(pt, efs, keep, *send, direct=None):
            done = 0
            low, high = send
            for c, ef in zip(members, efs):
                w = WIDTHS[c]
                if c == late:
                    near = jnp.dot(pt[...], ef[:, : 2 * w], preferred_element_type=F32)
                    lone, size = parted(c)
                    at = pl.ds(pl.multiple_of(direct * lone, LANES), size)
                    far = jnp.dot(pt[:, at], ef[at, 2 * w :], preferred_element_type=F32)
                    acc = jnp.concatenate([near, far], axis=1)
                else:
                    acc = jnp.dot(pt[...], ef[...], preferred_element_type=F32)
                for q, ref in enumerate((keep.at[0], low, keep.at[1], high)):
                    rows_q = acc[q * quarter : (q + 1) * quarter]
                    for s in range(slots):
                        base = s * group_width[g] + done
                        ref[:, base : base + w] = rows_q[:, s * w : (s + 1) * w]
                done += w

        if spot_size == 2:

            def body(fl, i, out, sems):
                pt, e = i[:2]
                at_home, away = fl[0] == 1, fl[0] == 0
                copies = []
                for m, c in enumerate(members):
                    w, ef = WIDTHS[c], out[m]
                    y, n, f2, f3 = i[2 + 5 * m : 6 + 5 * m]
                    lone, far = parted(c)
                    top, low = pl.ds(0, lone), pl.ds(rows - lone, lone)
                    first, last = pl.ds(0, far), pl.ds(rows - far, far)
                    copies += [
                        (at_home, e.at[fl[1], :, pl.ds(offsets[c], w)], ef.at[:, pl.ds(0, w)]),
                        (away, y.at[fl[1]], ef.at[:, pl.ds(0, w)]),
                        (None, n, ef.at[:, pl.ds(w, w)]),
                    ]
                    for part, f in enumerate((f2, f3)):
                        cols = pl.ds((2 + part) * w, w)
                        copies += [(at_home, f, ef.at[last, cols]), (away, f, ef.at[first, cols])]
                        if c != late:
                            s = i[6 + 5 * m]
                            copies += [(at_home, s.at[part], ef.at[top, cols]), (away, s.at[part], ef.at[low, cols])]
                copy_all(copies, sems)
                product(pt, out[: len(members)], *out[len(members) :], direct=fl[0])

            ins = [(st["pt"], whole((spots, rows))), (expr, ANY)]
            ins += [
                (a, ANY)
                for c in members
                for a in (*(sent[f"{k}{c}"] for k in ("y", "n", "f2", "f3")), *([] if c == late else [sent[f"s{c}"]]))
            ]
            scratch = [pltpu.SemaphoreType.DMA((12 * len(members),))]
        else:

            def body(fl, i, out):
                for m, c in enumerate(members):
                    w = WIDTHS[c]
                    for s in range(slots):
                        out[m][:, s * w : (s + 1) * w] = i[1 + m * slots + s][...]
                product(i[0], out[: len(members)], *out[len(members) :])

            def at_chunk(c):
                return pl.BlockSpec((rows, WIDTHS[c]), lambda *_: (0, offsets[c] // WIDTHS[c]))

            ins = [(st["pt"], whole((spots, rows)))] + [(a, at_chunk(c)) for c in members for a in st["pieces"]]
            scratch = []
        results = run(f"forward{g}", body, ins, outs, scratch=scratch)
        for c, ef in zip(members, results):
            st["e", c] = ef
        st["r", g], st["send", g] = results[len(members)], results[len(members) + 1 :]

    def forward_late(g):
        c = GROUPS[g][-1]
        w, wide = WIDTHS[c], slots * group_width[g]
        shape, lone = (2, quarter, wide), parted(c)[0]

        def body(fl, i, out, sems):
            pt, swapped, keep, low, high = i
            at = pl.ds(pl.multiple_of((1 - fl[0]) * (rows - lone), LANES), lone)
            copy_all([(None, swapped.at[n], out[3].at[at, pl.ds((2 + n) * w, w)]) for n in (0, 1)], sems)
            both = jnp.concatenate([swapped[0], swapped[1]], axis=1)
            acc = jnp.dot(pt[:, at], both, preferred_element_type=F32)
            for new, old in zip(out, (keep, low, high)):
                new[...] = old[...]
            for q, ref in enumerate((out[0].at[0], out[1], out[0].at[1], out[2])):
                for n in (0, 1):
                    base = (3 + n) * group_width[g] - w
                    ref[:, base : base + w] += acc[q * quarter : (q + 1) * quarter, n * w : (n + 1) * w]

        one = whole((quarter, wide))
        ins = [(st["pt"], whole((spots, rows))), (sent[f"s{c}"], whole((2, lone, w)))]
        ins += [(st["r", g], whole(shape))] + [(a, one) for a in st["send", g]]
        st["r", g], *send, st["e", c] = run(
            f"forwardlate{g}", body, ins, [(sds(shape, F32), whole(shape)), *halves_of(g)], through=[st["e", c]],
            scratch=[pltpu.SemaphoreType.DMA((2,))],
        )
        send_core(g, send)

    def send_core(g, send):
        for n, part in enumerate(send):
            sent[f"rc{n}{g}"] = over_core(part)

    def forward_send(g):
        send_core(g, run(f"send{g}", None, through=st["send", g]))

    def reduce_core(g):
        wide = slots * group_width[g]
        shape, one = (2, quarter, wide), (quarter, wide)

        single = 0 < g < len(GROUPS) - 1

        def body(fl, i, out):
            for n in (0, 1):
                out[n][0:quarter, :] = i[0][n] + i[1 + n][...]
            if single:
                out[1][quarter:, :] = jnp.zeros((PAD, wide), F32)

        ins = [(st["r", g], whole(shape))]
        ins += [(sent[f"rc{n}{g}"], whole(one)) for n in (0, 1)]
        more = (quarter + PAD, wide) if single else one
        st["r", g], b = run(f"core{g}", body, ins, [(sds(one, F32), whole(one)), (sds(more, F32), whole(more))])
        sent[f"rx{g}"] = over_x(b)

    sum_groups = [[g for g in z] for z in SUMS]
    sum_width = [sum(group_width[g] for g in z) for z in SUMS]

    def add_x(g):
        one = whole((quarter, slots * group_width[g]))

        def body(fl, i, out):
            out[0][...] = i[0][...] + i[1][0:quarter, :]

        ins = [(st["r", g], one), (sent[f"rx{g}"], whole(sent[f"rx{g}"].shape))]
        (st["added", g],) = run(f"addx{g}", body, ins, [(sds(one.block_shape, F32), one)])

    def reduce_x(z):
        members, w = sum_groups[z], sum_width[z]
        part = (quarter, w)
        in_halves = z < len(SUMS) - 1

        def body(fl, i, out):
            done, i = 0, list(i)
            for g in members:
                v = group_width[g]
                refs = [i.pop(0) for _ in parts_of[g]]
                for s in range(slots):
                    at = slice(s * v, (s + 1) * v)
                    value = sum(ref[0:quarter, at] for ref in refs)
                    if in_halves and s >= 2:
                        out[2][s - 2, :, done : done + v] = value
                    else:
                        out[s][:, done : done + v] = value
                done += v

        parts_of = {g: [st["added", g]] if ("added", g) in st else [st["r", g], sent[f"rx{g}"]] for g in members}
        ins = [(a, whole(a.shape)) for g in members for a in parts_of[g]]
        outs = [(sds(part, F32), whole(part))] * (2 if in_halves else slots)
        if in_halves:
            outs += [(sds((2, *part), F32), whole((2, *part)))]
        parts = run(f"x{z}", body, ins, outs)
        if in_halves:
            st["z", z] = parts[:2]
            sent[f"rz2{z}"] = over_gene(parts[2], 2)
        else:
            st["z", z] = parts[:1]
            for s in (3, 2, 1):
                sent[f"rz{s}{z}"] = over_gene(parts[s], s)

    def reduce_half(z):
        part = (quarter, sum_width[z])

        def body(fl, i, out):
            for n in (0, 1):
                out[n][...] = i[n][...] + i[2][n]

        ins = [(a, whole(part)) for a in st["z", z]] + [(sent[f"rz2{z}"], whole((2, *part)))]
        a, b = run(f"half{z}", body, ins, [(sds(part, F32), whole(part))] * 2)
        st["z", z], sent[f"rz1{z}"] = [a], over_gene(b, 1)

    def reduce_gene(z):
        part = (quarter, sum_width[z])
        others = [sent[f"rz{s}{z}"] for s in ((1,) if z < len(SUMS) - 1 else (1, 2, 3))]

        def body(fl, i, out):
            out[0][...] = sum(ref[...] for ref in i)

        ins = [(a, whole(part)) for a in (*st["z", z], *others)]
        (st["sum", z],) = run(f"gene{z}", body, ins, [(sds(part, F32), whole(part))])

    steps = {
        "Y": start_swap, "A": start_along, "a": along_send, "S": start_back,
        "e": totals, "m": shares, "F": forward, "f": forward_send, "G": forward_late, "b": members_of,
        "P": reduce_core, "X": add_x, "Q": reduce_x,
        "U": reduce_half, "R": reduce_gene,
    }
    if spot_size != 2:
        full = lax.all_gather(expression, "spot", axis=0, tiled=True).reshape(slots, rows, genes)
        pieces = [lax.dynamic_index_in_dim(full, gene ^ s, 0, False) for s in range(slots)]
        st["pieces"] = [pieces[0]] + [over_gene(pieces[s], s) for s in (1, 2, 3)]
    for word in " ".join(ORDER).split():
        if word[:2] == "w:":
            if spot_size == 2 or word == "w:ez1+ez2+ez3":
                wait_for(word[2:])
        elif spot_size != 2 and word[0] == "G":
            forward_send(int(word[1]))
        elif spot_size == 2 or word[0] not in "YAaS":
            steps[word[0]](int(word[1]))

    n_ch, n_sum = len(WIDTHS), len(SUMS)
    starts = [offsets[GROUPS[z[0]][0]] for z in SUMS]
    preds = [(st["sum", z], whole((quarter, sum_width[z]))) for z in range(n_sum)]
    mine = (spatial, pl.BlockSpec((quarter, genes), lambda g, f: (f[2], 0)))
    memb = (st["member"], whole((quarter, LANES)))
    gene_spec, spot_spec = whole((16, genes)), whole((8, quarter))

    def stats_body(fl, i, out):
        memb = i[0]
        cols = [jnp.broadcast_to(memb[:, k : k + 1], (quarter, LANES)) for k in range(SLIDES)]
        valid = jnp.sum(memb[:, SLIDES : SLIDES + 1])
        out[0][...] = jnp.broadcast_to(valid, (16, genes))
        totals = [jnp.zeros((quarter, LANES), F32) for _ in range(3)]
        for g in range(n_sum):
            for o in range(0, sum_width[g], LANES):
                at = slice(starts[g] + o, starts[g] + o + LANES)
                pr, ta = i[2 + g][:, o : o + LANES], i[1][:, at].astype(F32)
                for j, v in enumerate((pr * ta, pr * pr, ta * ta)):
                    totals[j] += v
                    for k in range(SLIDES):
                        n = 3 * j + k
                        out[0][n : n + 1, at] = jnp.sum(cols[k] * v, axis=0, keepdims=True)
        out[1][...] = jnp.zeros((8, quarter), F32)
        for j in range(3):
            out[1][j : j + 1, :] = jnp.sum(jnp.transpose(totals[j]), axis=0, keepdims=True)

    gene_sums, spot_sums = run(
        "stats", stats_body, [memb, mine, *preds],
        [(sds((16, genes), F32), gene_spec), (sds((8, quarter), F32), spot_spec)],
    )
    far = {s: over_gene(spot_sums, s) for s in (3, 2, 1)}
    spot_parts = [spot_sums] + [far[s] for s in (1, 2, 3)]
    gene_sums = gene_sums + over_core(gene_sums)
    gene_sums = gene_sums + over_x(gene_sums)
    gene_parts = [gene_sums, over_spot(gene_sums)] if spot_size == 2 else [sum_spot(gene_sums)]

    run("spots", None, after=spot_parts)

    def grads_body(fl, i, out):
        memb, ta_ref, kl, ent = i[:4]
        i = i[4:]
        spot_in, gene_in, preds_in = i[:4], i[4 : 4 + len(gene_parts)], i[4 + len(gene_parts) :]
        scale = -1.0 / (SLIDES * genes_all)
        sums = sum(ref[...] for ref in gene_in)
        num, psq, tsq = sums[0:3], sums[3:6], sums[6:9]
        p_floor, t_floor = jnp.maximum(psq, 1.0), jnp.maximum(tsq, 1.0)
        root = jnp.sqrt(p_floor * t_floor)
        cosine = num / root
        w_t = scale / root
        w_p = jnp.where(psq > 1.0, -scale * cosine / p_floor, 0.0)
        valid_total = jnp.maximum(sums[9, 0], 1.0)
        spot_all = (spot_in[0][...] + spot_in[1][...]) + (spot_in[2][...] + spot_in[3][...])
        s_num, s_p, s_t = [column(spot_all[n : n + 1, :]) for n in range(3)]
        s_p, s_t = s_p + 1e-06, s_t + 1e-06
        root = jnp.sqrt(s_p * s_t)
        cos_spot = s_num / root
        valid = jnp.broadcast_to(memb[:, SLIDES : SLIDES + 1], (quarter, LANES))
        coef = -valid / valid_total
        coef_t, coef_p = coef / root, -coef * cos_spot / s_p
        first = [(fl[n] == 0).astype(F32) for n in (2, 4, 3)]
        terms = [
            jnp.sum(cosine) * first[0] * first[1],
            jnp.sum((valid * cos_spot)[:, 0:1]) * first[2],
            kl[0, 0] * first[1],
            jnp.sum(ent[0:1, :]),
            valid_total * first[0] * first[1] * first[2],
        ]
        lane = lax.broadcasted_iota(jnp.int32, (8, spots), 1)
        value = jnp.zeros((8, spots), F32)
        for n, term in enumerate(terms):
            value = jnp.where(lane == n, term, value)
        out[1][...] = value
        cols = [jnp.broadcast_to(memb[:, k : k + 1], (quarter, LANES)) for k in range(SLIDES)]
        for g in range(n_sum):
            for o in range(0, sum_width[g], LANES):
                at = slice(starts[g] + o, starts[g] + o + LANES)
                f_t, f_p = coef_t, coef_p
                for k in range(SLIDES):
                    f_t = f_t + cols[k] * w_t[k : k + 1, at]
                    f_p = f_p + cols[k] * w_p[k : k + 1, at]
                out[0][:, at] = (f_t * ta_ref[:, at].astype(F32) + f_p * preds_in[g][:, o : o + LANES]).astype(BF)

    row8, flat = whole((8, spots)), whole((8, LANES))
    ins = [memb, mine, (st["kl"], flat), (st["ent"], row8)]
    ins += [(a, spot_spec) for a in spot_parts] + [(a, gene_spec) for a in gene_parts] + preds
    grad, terms = run(
        "grads", grads_body, ins,
        [(sds((quarter, genes), BF), whole((quarter, genes))), (sds((8, spots), F32), row8)],
    )
    terms = [terms, over_spot(terms)] if spot_size == 2 else [sum_spot(terms)]
    far = {s: over_gene(grad, s) for s in (3, 2, 1)}
    others = [far[s] for s in (1, 2, 3)]
    grad_x = over_x(grad)
    own = [grad, over_core(grad), grad_x, over_core(grad_x)]
    one, rest = (quarter, genes), (slots - 1, quarter, genes)
    row_blk = rows // 4

    def by_rows(width, size=row_blk):
        return pl.BlockSpec((size, width), lambda g, f: (g, 0))

    def place(fl, refs, target, sems):
        copies = []
        for b, ref in enumerate(refs):
            at = pl.ds(pl.multiple_of((fl[2] ^ b) * quarter, quarter), quarter)
            copies.append((None, ref, target(at)))
        copy_all(copies, sems)

    def slot_product(efs, slot, held):
        left = jnp.concatenate([ef[:, slot * w : (slot + 1) * w] for w, ef in zip(WIDTHS, efs)], axis=1)
        return lax.dot_general(left, held, (((1,), (1,)), ((), ())), preferred_element_type=F32)

    def gather_body(fl, i, out):
        for n in range(slots - 1):
            out[0][n] = i[n][...]

    (rest_z,) = run(
        "gather", gather_body, [(a, whole(one)) for a in others], [(sds(rest, BF), whole(rest))], after=[grad_x, *terms[1:]]
    )
    rest_x = over_x(rest_z)

    def own_body(fl, i, out, held, sems):
        sm, efs, gs = i[0], i[1 : 1 + n_ch], i[1 + n_ch :]

        @pl.when(pl.program_id(0) == 0)
        def _():
            place(fl, gs, lambda at: held.at[at, :], sems)

        out[0][...] = slot_product(efs, 0, held[...]) - jnp.broadcast_to(sm[:, 0:1], (row_blk, spots))

    ins = [(st["sm"], by_rows(LANES))] + [(st["e", c], by_rows(WIDTHS[c])) for c in chunks]
    ins += [(a, ANY) for a in own]
    (own_part,) = run(
        "own", own_body, ins, [(sds((rows, spots), F32), by_rows(spots))], grid=(rows // row_blk,),
        scratch=[pltpu.VMEM((spots, genes), BF), pltpu.SemaphoreType.DMA((len(own),))],
    )

    (rest_x,) = run("rest", None, through=[rest_x])
    grads = [rest_z, over_core(rest_z), rest_x, over_core(rest_x)]

    def backward_body(fl, i, out, held, sems):
        lg, tot, before = i[:3]
        efs, gs, terms = i[3 : 3 + n_ch], i[3 + n_ch : 7 + n_ch], i[7 + n_ch :]

        @pl.when(pl.program_id(0) == 0)
        def _():
            row = lax.broadcasted_iota(jnp.int32, (8, spots), 0)
            out[1][...] = jnp.where(row == 0, 0.0, sum(ref[...] for ref in terms))
            place(fl, gs, lambda at: held.at[:, at, :], sems)

        acc = before[...]
        for s in range(1, slots):
            acc += slot_product(efs, s, held[s - 1])
        out[0][...] = acc
        prob = jnp.exp(lg[...].astype(F32)) * (1.0 / tot[0:1, :])
        out[1][0:1, :] += jnp.sum(prob * acc, axis=0, keepdims=True)

    ins = [(logits, by_rows(spots)), (st["tot"], row8), (own_part, by_rows(spots))]
    ins += [(st["e", c], by_rows(slots * WIDTHS[c])) for c in chunks]
    ins += [(a, ANY) for a in grads] + [(a, row8) for a in terms]
    grad_probs, v = run(
        "backward", backward_body, ins,
        [(sds((rows, spots), F32), by_rows(spots)), (sds((8, spots), F32), row8)],
        grid=(rows // row_blk,),
        scratch=[pltpu.VMEM((slots - 1, spots, genes), BF), pltpu.SemaphoreType.DMA((len(grads),))],
    )

    v = v + over_core(v)
    v = v + over_x(v)
    v = (v + over_gene(v, 1)) + (over_gene(v, 2) + over_gene(v, 3))

    def final_body(fl, i, out):
        at = pl.ds(pl.multiple_of(pl.program_id(0) * last_blk, last_blk), last_blk)
        prob = jnp.exp(i[0][at, :].astype(F32)) * (1.0 / i[1][0:1, :])
        out[0][...] = prob * (i[2][at, :] - i[3][0:1, :])

        @pl.when(pl.program_id(0) == 0)
        def _():
            sums = [i[3][1, n] for n in range(5)]
            gene_term, spot_term = sums[0] / (SLIDES * genes_all), sums[1] / sums[4]
            divergence, entropy = sums[2], sums[3] / spots_all
            values = (divergence - gene_term - spot_term, gene_term, spot_term, divergence, entropy)
            for n, value in enumerate(values):
                out[1][n] = value

    last_blk = rows // 4
    held = pl.BlockSpec(memory_space=pltpu.VMEM)
    blk = by_rows(spots, last_blk)
    grad_logits, loss_terms = run(
        "final", final_body, [(logits, held), (st["tot"], row8), (grad_probs, held), (v, row8)],
        [(sds((rows, spots), F32), blk), (sds((5,), F32), pl.BlockSpec(memory_space=pltpu.SMEM))],
        grid=(rows // last_blk,),
    )
    return (loss_terms, grad_logits)


def solution(mesh):
    return jax.shard_map(
        functools.partial(per_device, dict(mesh.shape)),
        mesh=mesh,
        in_specs=(
            P(("cell", "gene"), "spot"),
            P(("cell", "spot"), "gene"),
            P("spot", "gene"),
            P("spot"),
            P("spot"),
            P(("cell", "gene")),
        ),
        out_specs=(P(), P(("cell", "gene"), "spot")),
        check_vma=False,
    )
```
